32 devices in a mesh: doc: 4 (over y, core), seq: 8 (over z, x).
Axes of the slice: x: 2, y: 2, z: 4, core: 2. Of those that a mesh axis runs over, the one named last changes fastest.
Arguments:
- queries: bfloat16 [4096, 512], P(('doc', 'seq')), parts along dimension 0, may hold values from -26 to 26
- key_vectors: bfloat16 [4096, 512], P(('doc', 'seq')), parts along dimension 0, may hold values from -26 to 26
- value_vectors: bfloat16 [4096, 512], P(('doc', 'seq')), parts along dimension 0, may hold values from -6 to 6
- output_grad: bfloat16 [4096, 512], P(('doc', 'seq')), parts along dimension 0, may hold values from -6 to 6
- rand_pick: int32 [64, 3], P('doc'), parts along dimension 0, may hold values from 0 to 1
- global_ids: int32 [8], P('doc'), parts along dimension 0, may hold values from 0 to 15
Outputs:
- grad_queries: bfloat16 [4096, 512], P(('doc', 'seq')), parts along dimension 0
- grad_keys: bfloat16 [4096, 512], P(('doc', 'seq')), parts along dimension 0
- grad_values: bfloat16 [4096, 512], P(('doc', 'seq')), parts along dimension 0
The draws below stay inside these ranges and needn't reach their ends.
There are 4 independent parts, one for each index of `doc`. The reference program is written for one: setup_inputs(seed, part) draws one part's arguments, and reference() takes and returns one part's arrays. A program takes and returns all parts, laid end to end along the dimension named above; each array names one. Nothing has to cross between parts.
All inputs are finite; a program needn't handle non-finite values.
Results may differ from the reference program's by a relative error of at most 0.012.
Values may be sent and summed in bfloat16 or wider, within the bound.
No kernel may reach another device: no remote copies, remote signals or barrier semaphores. Data moves between devices by JAX's collectives and lax.ppermute only.
A program may use at most 64 MiB of HBM per device.

```python
import math
import jax
import jax.numpy as jnp
from jax import lax

D = 512
HEADS = 8
BLOCK = 64
RAND = 3
GLOBAL = 2
RSPAN = 2
TOKENS = 1024
NB = 16


def draw_queries(key, part):
    key = jax.random.fold_in(key, 1)
    drawn = jnp.clip(jax.random.normal(key, (TOKENS, D), jnp.float32), -4.0, 4.0)
    return drawn.astype(jnp.bfloat16)


def draw_key_vectors(key, part):
    key = jax.random.fold_in(key, 2)
    drawn = jnp.clip(jax.random.normal(key, (TOKENS, D), jnp.float32), -4.0, 4.0)
    return drawn.astype(jnp.bfloat16)


def touch_ends(values, rng, low, high):
    place = [jax.random.randint(jax.random.fold_in(rng, axis), (), 0, length) for axis, length in enumerate(values.shape)]
    main_axis = values.shape.index(max(values.shape))
    neighbour = place[:main_axis] + [(place[main_axis] + 1) % values.shape[main_axis]] + place[main_axis + 1:]
    return values.at[tuple(place)].set(low).at[tuple(neighbour)].set(high)


def levels(key, shape, pieces, low, top_value):
    factor_of = 1.0
    for dim, blocks in pieces:
        draws = jax.random.uniform(jax.random.fold_in(jax.random.fold_in(key, 6), dim), (blocks,), jnp.float32, low / len(pieces), top_value / len(pieces))
        factor_of = factor_of * jnp.repeat(jnp.exp(draws), shape[dim] // blocks).reshape((-1,) + (1,) * (len(shape) - 1 - dim))
    return factor_of


def normal_values(own_key, dims, deviation, bound, pieces=(), kind=jnp.bfloat16):
    values = jax.random.normal(own_key, dims, jnp.float32) * deviation
    if len(pieces) > 0:
        values = levels(own_key, dims, pieces, -0.22, 0.18) * values
    return jnp.clip(values, min=-bound, max=bound).astype(kind)


def setup_inputs(seed: int = 0, part: int = 0) -> dict:
    keys = jax.random.split(jax.random.key(seed), 7)
    part_splits = jax.random.split(jax.random.fold_in(keys[6], part), 7)
    queries = draw_queries(jax.random.fold_in(jax.random.fold_in(keys[6], part), 71), part)
    key_vectors = draw_key_vectors(jax.random.fold_in(jax.random.fold_in(keys[6], part), 71), part)
    value_vectors = normal_values(part_splits[2], (TOKENS, D), 1.0, 6.0, ((0, 8),))
    output_grad = normal_values(part_splits[3], (TOKENS, D), 1.0, 6.0, ((0, 8),))
    rand_pick = touch_ends(jax.random.randint(part_splits[4], (NB, RAND), 0, RSPAN), jax.random.fold_in(part_splits[4], 1), 0, RSPAN - 1).astype(jnp.int32)
    global_ids = jax.random.randint(part_splits[5], (GLOBAL,), 0, NB).astype(jnp.int32)
    return dict(queries=queries, key_vectors=key_vectors, value_vectors=value_vectors, output_grad=output_grad, rand_pick=rand_pick, global_ids=global_ids)


def reference(queries, key_vectors, value_vectors, output_grad, rand_pick, global_ids):
    num_blocks = TOKENS // BLOCK
    head_size = D // HEADS
    scale = 1.0 / math.sqrt(head_size)
    entries = 3 + GLOBAL + RAND
    query_blocks = queries.reshape(num_blocks, BLOCK, HEADS, head_size)
    grad_blocks = output_grad.reshape(num_blocks, BLOCK, HEADS, head_size)
    pair_blocks = jnp.concatenate([key_vectors, value_vectors], axis=1).reshape(num_blocks, BLOCK, 2 * D)
    segment = jnp.arange(entries * BLOCK, dtype=jnp.int32) // BLOCK

    def visit(totals, block_idx):
        chosen = [jnp.maximum(block_idx - 1, 0), block_idx, jnp.minimum(block_idx + 1, num_blocks - 1)]
        chosen += [global_ids[slot_idx] for slot_idx in range(GLOBAL)]
        chosen += [(block_idx - (slot_idx + 1) * num_blocks // 4 - rand_pick[block_idx, slot_idx]) % num_blocks for slot_idx in range(RAND)]
        listed = jnp.stack([item.astype(jnp.int32) for item in chosen]).astype(jnp.int32)
        gathered = jnp.take(pair_blocks, listed, axis=0).reshape(entries * BLOCK, 2 * D)
        key_part = gathered[:, :D].reshape(-1, HEADS, head_size).astype(jnp.float32)
        value_part = gathered[:, D:].reshape(-1, HEADS, head_size).astype(jnp.float32)
        query_part = lax.dynamic_index_in_dim(query_blocks, block_idx, 0, keepdims=False).astype(jnp.float32)
        grad_part = lax.dynamic_index_in_dim(grad_blocks, block_idx, 0, keepdims=False).astype(jnp.float32)
        valid = ((segment != 0) | (block_idx > 0)) & ((segment != 2) | (block_idx < num_blocks - 1))
        scores = jnp.einsum('qhe,khe->hqk', query_part, key_part) * scale
        scores = jnp.where(valid[None, None, :], scores, -1e+30)
        row_max = lax.optimization_barrier(jnp.max(scores, axis=-1, keepdims=True))
        expo = jnp.exp(scores - row_max)
        row_total = lax.optimization_barrier(jnp.sum(expo, axis=-1, keepdims=True))
        probs = expo / row_total
        probs_half = lax.optimization_barrier(probs.astype(jnp.bfloat16)).astype(jnp.float32)
        attended = jnp.einsum('hqk,khe->qhe', probs_half, value_part)
        row_dot = lax.optimization_barrier(jnp.sum(grad_part * attended, axis=-1)).T
        grad_probs = jnp.einsum('qhe,khe->hqk', grad_part, value_part)
        grad_scores = probs * (grad_probs - row_dot[:, :, None])
        grad_half = lax.optimization_barrier(grad_scores.astype(jnp.bfloat16)).astype(jnp.float32)
        grad_query = jnp.einsum('hqk,khe->qhe', grad_half, key_part) * scale
        grad_key = jnp.einsum('hqk,qhe->khe', grad_half, query_part) * scale
        grad_value = jnp.einsum('hqk,qhe->khe', probs_half, grad_part)
        update = jnp.concatenate([grad_key.reshape(-1, D), grad_value.reshape(-1, D)], axis=1)
        totals = totals.at[listed].add(update.reshape(entries, BLOCK, 2 * D))
        return (totals, grad_query.reshape(BLOCK, D).astype(jnp.bfloat16))
    start = jnp.zeros((num_blocks, BLOCK, 2 * D), jnp.float32)
    totals, grad_query = lax.scan(visit, start, jnp.arange(num_blocks, dtype=jnp.int32))
    flat = totals.reshape(TOKENS, 2 * D)
    return (grad_query.reshape(TOKENS, D), flat[:, :D].astype(jnp.bfloat16), flat[:, D:].astype(jnp.bfloat16))
```

```python
import functools
import math

import jax
import jax.numpy as jnp
from jax import lax
from jax.experimental import pallas as pl
from jax.experimental.pallas import tpu as pltpu
from jax.sharding import PartitionSpec as P

HEADS = 8
BLOCK = 64
RAND = 3
GLOBAL = 2
HEAD = 64
LANES = 2 * HEAD
WINDOW = 4
ENTRIES = WINDOW + GLOBAL + 2 * RAND
MASKED = -1e30


def low_lanes(shape):
    return lax.broadcasted_iota(jnp.int32, shape, len(shape) - 1) < HEAD


def swap_halves(block):
    return pltpu.roll(block, HEAD, 1)


def pack_kernel(q_ref, k_ref, v_ref, g_ref, out_ref):
    rows = q_ref.shape[0]
    low = low_lanes((rows, LANES))
    for pair in range(HEADS // 2):
        lanes = slice(pair * LANES, (pair + 1) * LANES)
        for place, (first_ref, second_ref) in enumerate(((k_ref, v_ref), (q_ref, g_ref))):
            first = first_ref[:, lanes].astype(jnp.float32)
            second = second_ref[:, lanes].astype(jnp.float32)
            even = jnp.where(low, first, swap_halves(second))
            odd = jnp.where(low, swap_halves(first), second)
            for half, tile in enumerate((even, odd)):
                out_ref[2 * pair + half, place] = tile.astype(jnp.bfloat16)


def unpack_kernel(in_ref, gq_ref, gk_ref, gv_ref):
    rows = gq_ref.shape[0]
    low = low_lanes((rows, LANES))
    low_block = low_lanes((BLOCK, LANES))
    for pair in range(HEADS // 2):
        lanes = slice(pair * LANES, (pair + 1) * LANES)
        even = in_ref[2 * pair].astype(jnp.float32)
        odd = in_ref[2 * pair + 1].astype(jnp.float32)
        gk = jnp.where(low, even[:rows], swap_halves(odd[:rows]))
        gv = jnp.where(low, swap_halves(even[:rows]), odd[:rows])
        gk_ref[:, lanes] = gk.astype(jnp.bfloat16)
        gv_ref[:, lanes] = gv.astype(jnp.bfloat16)
        first = jnp.where(low_block, even[rows:], swap_halves(odd[rows:]))
        second = jnp.where(low_block, swap_halves(even[rows:]), odd[rows:])
        gq_ref[:BLOCK, lanes] = first.astype(jnp.bfloat16)
        gq_ref[BLOCK:, lanes] = second.astype(jnp.bfloat16)


def attend_kernel(alone, scale, picks_ref, globals_ref, range_ref, sent_ref, *rest):
    if alone:
        out_ref, acc_ref = rest
        pool_ref = None
    else:
        pool_ref, gq_ref, acc_ref = rest
    tiles = sent_ref.shape[0]
    blocks = 2 * tiles
    queries = 2 * BLOCK
    low = low_lanes((BLOCK, queries))
    low_rows = low_lanes((queries, LANES))
    acc_ref[...] = jnp.zeros_like(acc_ref)

    def pooled(entry):
        if alone:
            return sent_ref[entry // 2, 0, entry % 2]
        return pool_ref[entry]

    def chosen(tile):
        first = 2 * tile
        if alone:
            window = [max(first - 1, 0), first, first + 1, min(first + 2, blocks - 1)]
            everywhere = [globals_ref[slot] for slot in range(GLOBAL)]
        else:
            window = [first - 1 if tile > 0 else blocks, first, first + 1]
            window += [first + 2 if tile < tiles - 1 else blocks + 1]
            everywhere = [blocks + 2 + slot for slot in range(GLOBAL)]
        picked = []
        for block in (first, first + 1):
            for slot in range(RAND):
                pick = picks_ref[block, slot]
                if alone:
                    behind = block + blocks - (slot + 1) * blocks // 4 - pick
                    picked.append(lax.rem(behind, blocks))
                else:
                    base = blocks + 2 + GLOBAL + slot * (blocks + 1)
                    picked.append(base + block + 1 - pick)
        return window + everywhere + picked

    for tile in range(tiles):
        entries = chosen(tile)
        keys = jnp.concatenate([pooled(entry) for entry in entries], axis=0)
        both = sent_ref[tile, 1].reshape(queries, LANES)
        zero = jnp.zeros_like(both)
        sides = jnp.concatenate(
            [jnp.where(low_rows, both * scale, zero), jnp.where(low_rows, zero, both)], axis=0
        )
        products = lax.dot_general(
            keys, sides, (((1,), (1,)), ((), ())), preferred_element_type=jnp.float32
        )
        grad_probs = products[:, queries:]
        parts = []
        for place in range(ENTRIES):
            part = products[place * BLOCK : (place + 1) * BLOCK, :queries]
            keep = None
            if place == 0:
                keep = low
                if tile == 0:
                    keep = jnp.logical_and(low, False if alone else range_ref[0] > 0)
            elif place == WINDOW - 1:
                keep = jnp.logical_not(low)
                if tile == tiles - 1:
                    inside = False if alone else range_ref[0] < range_ref[1] - 1
                    keep = jnp.logical_and(keep, inside)
            elif place >= WINDOW + GLOBAL + RAND:
                keep = jnp.logical_not(low)
            elif place >= WINDOW + GLOBAL:
                keep = low
            parts.append(part if keep is None else jnp.where(keep, part, MASKED))
        scores = jnp.concatenate(parts, axis=0)
        row_max = jnp.max(scores, axis=0, keepdims=True)
        expo = jnp.exp(scores - row_max)
        row_total = jnp.sum(expo, axis=0, keepdims=True)
        probs = expo * (1.0 / row_total)
        probs_half = probs.astype(jnp.bfloat16)
        row_dot = jnp.sum(probs_half.astype(jnp.float32) * grad_probs, axis=0, keepdims=True)
        grad_half = (probs * (grad_probs - row_dot)).astype(jnp.bfloat16)
        pair = jnp.concatenate([grad_half, probs_half], axis=1)
        key_grads = jnp.dot(pair, sides, preferred_element_type=jnp.float32)
        grad_query = lax.dot_general(
            grad_half, keys, (((0,), (0,)), ((), ())), preferred_element_type=jnp.float32
        )
        grad_query = grad_query * scale
        folded = jnp.where(
            low_lanes((BLOCK, LANES)), grad_query[:BLOCK], swap_halves(grad_query[BLOCK:])
        ).astype(jnp.bfloat16)
        if alone:
            out_ref[tile, queries:] = folded
        else:
            gq_ref[tile] = folded
        for place, entry in enumerate(entries):
            acc_ref[entry] += key_grads[place * BLOCK : (place + 1) * BLOCK]
    if alone:
        for tile in range(tiles):
            for half in range(2):
                grads = acc_ref[2 * tile + half].astype(jnp.bfloat16)
                out_ref[tile, half * BLOCK : (half + 1) * BLOCK] = grads


def exchange(block, ways, groups):
    return lax.all_to_all(block, "seq", 0, 0, axis_index_groups=groups)


def moved(block, ranges, distance, ways, wrap=True):
    route = []
    for source in range(ranges):
        target = source + distance
        if wrap:
            target %= ranges
        if 0 <= target < ranges:
            route += [(source * ways + head, target * ways + head) for head in range(ways)]
    return lax.ppermute(block, "seq", route)


def on_device(queries, key_vectors, value_vectors, output_grad, rand_pick, global_ids):
    group = lax.axis_size("seq")
    rows, width = queries.shape
    ways = HEADS
    ranges = group // ways
    alone = ranges == 1
    blocks = ways * rows // BLOCK
    scale = 1.0 / math.sqrt(width // HEADS)
    vmem = pl.BlockSpec(memory_space=pltpu.VMEM)
    smem = pl.BlockSpec(memory_space=pltpu.SMEM)
    half_type = jnp.bfloat16
    groups = None
    if not alone:
        groups = [[r * ways + head for head in range(ways)] for r in range(ranges)]

    packed = pl.pallas_call(
        pack_kernel,
        out_shape=jax.ShapeDtypeStruct((HEADS, 2, rows, LANES), half_type),
        in_specs=[vmem] * 4,
        out_specs=vmem,
        name="pack",
    )(queries, key_vectors, value_vectors, output_grad)
    sent = exchange(packed, ways, groups).reshape(ways, 2, 2, BLOCK, LANES)

    kernel = functools.partial(attend_kernel, alone, scale)
    back_shape = (ways, rows + BLOCK, LANES)
    if alone:
        back = pl.pallas_call(
            kernel,
            out_shape=jax.ShapeDtypeStruct(back_shape, half_type),
            in_specs=[smem, smem, smem, vmem],
            out_specs=vmem,
            scratch_shapes=[pltpu.VMEM((blocks, BLOCK, LANES), jnp.float32)],
            compiler_params=pltpu.CompilerParams(vmem_limit_bytes=48 * 2**20),
            name="attend",
        )(rand_pick, global_ids, jnp.zeros((2,), jnp.int32), sent)
    else:
        back = spread_out(
            kernel, sent, rand_pick, global_ids, ways, ranges, blocks, back_shape, groups
        )
    received = exchange(back, ways, groups)
    return pl.pallas_call(
        unpack_kernel,
        out_shape=[jax.ShapeDtypeStruct((rows, width), half_type)] * 3,
        in_specs=[vmem],
        out_specs=[vmem] * 3,
        name="unpack",
    )(received)


def spread_out(kernel, sent, rand_pick, global_ids, ways, ranges, blocks, back_shape, groups):
    vmem = pl.BlockSpec(memory_space=pltpu.VMEM)
    smem = pl.BlockSpec(memory_space=pltpu.SMEM)
    mine = lax.axis_index("seq") // ways
    own = sent[:, 0].reshape(blocks, BLOCK, LANES)
    lags = [(slot + 1) * ranges // 4 for slot in range(RAND)]
    heads = [[r * ways + head for r in range(ranges)] for head in range(ways)]
    roots = global_ids // blocks
    offsets = global_ids % blocks
    pool = [own, moved(own[-1:], ranges, 1, ways, False), moved(own[:1], ranges, -1, ways, False)]
    chosen = jnp.where((roots == mine)[:, None, None], jnp.take(own, offsets, axis=0), 0)
    pool.append(lax.psum(chosen.astype(own.dtype), "seq", axis_index_groups=heads))
    for lag in lags:
        pool.append(moved(own[-1:], ranges, lag + 1, ways))
        pool.append(moved(own, ranges, lag, ways))
    pool = jnp.concatenate(pool, axis=0)
    picks = lax.dynamic_slice_in_dim(rand_pick, mine * blocks, blocks, 0)
    where = jnp.stack([mine, jnp.int32(ranges)]).astype(jnp.int32)
    grad_query, totals = pl.pallas_call(
        kernel,
        out_shape=[
            jax.ShapeDtypeStruct((ways, BLOCK, LANES), jnp.bfloat16),
            jax.ShapeDtypeStruct(pool.shape, jnp.float32),
        ],
        in_specs=[smem, smem, smem, vmem, vmem],
        out_specs=[vmem] * 2,
        compiler_params=pltpu.CompilerParams(vmem_limit_bytes=48 * 2**20),
        name="attend",
    )(picks, global_ids, where, sent, pool)
    total = totals[:blocks]
    total = total.at[-1].add(moved(totals[blocks], ranges, -1, ways, False))
    total = total.at[0].add(moved(totals[blocks + 1], ranges, 1, ways, False))
    base = blocks + 2
    summed = lax.psum(totals[base : base + GLOBAL], "seq", axis_index_groups=heads)
    for slot in range(GLOBAL):
        owned = jnp.where(roots[slot] == mine, summed[slot], 0.0)
        total = total.at[offsets[slot]].add(owned)
    base += GLOBAL
    for lag in lags:
        total = total.at[-1].add(moved(totals[base], ranges, -lag - 1, ways))
        total = total + moved(totals[base + 1 : base + 1 + blocks], ranges, -lag, ways)
        base += blocks + 1
    grads = total.astype(jnp.bfloat16).reshape(ways, 2 * BLOCK, LANES)
    return jnp.concatenate([grads, grad_query], axis=1).reshape(back_shape)


def solution(mesh):
    whole = P(("doc", "seq"), None)
    return jax.shard_map(
        on_device,
        mesh=mesh,
        in_specs=(whole, whole, whole, whole, P("doc", None), P("doc")),
        out_specs=(whole, whole, whole),
        check_vma=False,
    )
```

```python
import functools
import math

import jax
import jax.numpy as jnp
from jax import lax
from jax.experimental import pallas as pl
from jax.experimental.pallas import tpu as pltpu
from jax.sharding import PartitionSpec as P

HEADS = 8
BLOCK = 64
RAND = 3
GLOBAL = 2
HEAD = 64
LANES = 2 * HEAD
MASKED = -1e30


def low_lanes(shape):
    return lax.broadcasted_iota(jnp.int32, shape, len(shape) - 1) < HEAD


def swap_halves(block):
    return pltpu.roll(block, HEAD, 1)


def pack_kernel(q_ref, k_ref, v_ref, g_ref, out_ref):
    rows = q_ref.shape[0]
    low = low_lanes((rows, LANES))
    for pair in range(HEADS // 2):
        lanes = slice(pair * LANES, (pair + 1) * LANES)
        for place, (first_ref, second_ref) in enumerate(((k_ref, v_ref), (q_ref, g_ref))):
            first = first_ref[:, lanes].astype(jnp.float32)
            second = second_ref[:, lanes].astype(jnp.float32)
            even = jnp.where(low, first, swap_halves(second))
            odd = jnp.where(low, swap_halves(first), second)
            for half, tile in enumerate((even, odd)):
                out_ref[2 * pair + half, place] = tile.astype(jnp.bfloat16)


def unpack_kernel(in_ref, gq_ref, gk_ref, gv_ref):
    rows = gq_ref.shape[0]
    low = low_lanes((rows, LANES))
    low_block = low_lanes((BLOCK, LANES))
    for pair in range(HEADS // 2):
        lanes = slice(pair * LANES, (pair + 1) * LANES)
        even = in_ref[2 * pair].astype(jnp.float32)
        odd = in_ref[2 * pair + 1].astype(jnp.float32)
        gk = jnp.where(low, even[:rows], swap_halves(odd[:rows]))
        gv = jnp.where(low, swap_halves(even[:rows]), odd[:rows])
        gk_ref[:, lanes] = gk.astype(jnp.bfloat16)
        gv_ref[:, lanes] = gv.astype(jnp.bfloat16)
        first = jnp.where(low_block, even[rows:], swap_halves(odd[rows:]))
        second = jnp.where(low_block, swap_halves(even[rows:]), odd[rows:])
        gq_ref[:BLOCK, lanes] = first.astype(jnp.bfloat16)
        gq_ref[BLOCK:, lanes] = second.astype(jnp.bfloat16)


def attend_kernel(alone, scale, table_ref, sent_ref, *rest):
    if alone:
        out_ref, acc_ref = rest
        pool_ref = None
    else:
        pool_ref, gq_ref, acc_ref = rest
    tiles = sent_ref.shape[0]
    blocks = 2 * tiles
    queries = 2 * BLOCK
    low = low_lanes((BLOCK, queries))
    zero = jnp.zeros((BLOCK, LANES), jnp.bfloat16)
    fixed = blocks * RAND
    acc_ref[...] = jnp.zeros_like(acc_ref)

    def pooled(entry):
        if alone:
            return sent_ref[entry // 2, 0, entry % 2]
        return pool_ref[entry]

    def chosen(tile):
        first = 2 * tile
        pairs = [(first, first), (first + 1, first + 1)]
        for slot in range(GLOBAL):
            entry = table_ref[fixed + slot] if alone else blocks + 2 + slot
            pairs.append((entry, entry))
        before, after = first - 1, first + 2
        if alone:
            before, after = max(before, 0), min(after, blocks - 1)
        else:
            before = before if tile > 0 else blocks
            after = after if tile < tiles - 1 else blocks + 1
        pairs.append((before, after))
        for slot in range(RAND):
            picked = []
            for block in (first, first + 1):
                pick = table_ref[block * RAND + slot]
                if alone:
                    behind = block + blocks - (slot + 1) * blocks // 4 - pick
                    picked.append(lax.rem(behind, blocks))
                else:
                    base = blocks + 2 + GLOBAL + slot * (blocks + 1)
                    picked.append(base + block + 1 - pick)
            pairs.append(tuple(picked))
        return pairs

    def multiply(tile):
        pairs = chosen(tile)
        keys = jnp.concatenate(
            [jnp.concatenate([pooled(a), pooled(b)], axis=1) for a, b in pairs], axis=0
        )
        first, second = sent_ref[tile, 1, 0], sent_ref[tile, 1, 1]
        rows = [
            [jnp.where(low, first * scale, zero), zero],
            [zero, jnp.where(low, second * scale, zero)],
            [jnp.where(low, zero, first), zero],
            [zero, jnp.where(low, zero, second)],
        ]
        sides = jnp.concatenate([jnp.concatenate(row, axis=1) for row in rows], axis=0)
        products = lax.dot_general(
            keys, sides, (((1,), (1,)), ((), ())), preferred_element_type=jnp.float32
        )
        return pairs, keys, sides, products

    def weigh(tile, products):
        scores, grad_probs = products[:, :queries], products[:, queries:]
        edge = (2 + GLOBAL) * BLOCK
        if tile == 0 or tile == tiles - 1:
            if tile == 0:
                keep = jnp.logical_not(low)
                if not alone:
                    keep = jnp.logical_or(keep, table_ref[fixed + GLOBAL] > 0)
            else:
                keep = low
                if not alone:
                    last = table_ref[fixed + GLOBAL + 1] - 1
                    keep = jnp.logical_or(keep, table_ref[fixed + GLOBAL] < last)
            masked = jnp.where(keep, scores[edge : edge + BLOCK], MASKED)
            scores = jnp.concatenate([scores[:edge], masked, scores[edge + BLOCK :]], axis=0)
        row_max = jnp.max(scores, axis=0, keepdims=True)
        expo = jnp.exp(scores - row_max)
        row_total = jnp.sum(expo, axis=0, keepdims=True)
        probs = expo * (1.0 / row_total)
        probs_half = probs.astype(jnp.bfloat16)
        row_dot = jnp.sum(probs_half.astype(jnp.float32) * grad_probs, axis=0, keepdims=True)
        grad_half = (probs * (grad_probs - row_dot)).astype(jnp.bfloat16)
        return grad_half, probs_half

    def gather(tile, pairs, keys, sides, grad_half, probs_half):
        both = jnp.concatenate([grad_half, probs_half], axis=1)
        key_grads = jnp.dot(both, sides, preferred_element_type=jnp.float32)
        grad_query = lax.dot_general(
            grad_half, keys, (((0,), (0,)), ((), ())), preferred_element_type=jnp.float32
        )
        grad_query = grad_query * scale
        folded = jnp.where(
            low, grad_query[:BLOCK, :LANES], swap_halves(grad_query[BLOCK:, LANES:])
        ).astype(jnp.bfloat16)
        if alone:
            out_ref[tile, queries:] = folded
        else:
            gq_ref[tile] = folded
        for place, (a, b) in enumerate(pairs):
            part = key_grads[place * BLOCK : (place + 1) * BLOCK]
            if place < 2 + GLOBAL:
                acc_ref[a] += part[:, :LANES] + part[:, LANES:]
            else:
                acc_ref[a] += part[:, :LANES]
                acc_ref[b] += part[:, LANES:]

    ahead, weighed = {}, {}
    for step in range(tiles + 2):
        if step < tiles:
            ahead[step] = multiply(step)
        if 0 <= step - 1 < tiles:
            weighed[step - 1] = weigh(step - 1, ahead[step - 1][-1])
        if step >= 2:
            pairs, keys, sides, _ = ahead.pop(step - 2)
            gather(step - 2, pairs, keys, sides, *weighed.pop(step - 2))
    if alone:
        for tile in range(tiles):
            for half in range(2):
                grads = acc_ref[2 * tile + half].astype(jnp.bfloat16)
                out_ref[tile, half * BLOCK : (half + 1) * BLOCK] = grads


def exchange(block, ways, groups):
    return lax.all_to_all(block, "seq", 0, 0, axis_index_groups=groups)


def moved(block, ranges, distance, ways, wrap=True):
    route = []
    for source in range(ranges):
        target = source + distance
        if wrap:
            target %= ranges
        if 0 <= target < ranges:
            route += [(source * ways + head, target * ways + head) for head in range(ways)]
    return lax.ppermute(block, "seq", route)


def on_device(queries, key_vectors, value_vectors, output_grad, rand_pick, global_ids):
    group = lax.axis_size("seq")
    rows, width = queries.shape
    ways = HEADS
    ranges = group // ways
    assert group % ways == 0 and (ranges == 1 or ranges % 4 == 0)
    alone = ranges == 1
    blocks = ways * rows // BLOCK
    scale = 1.0 / math.sqrt(width // HEADS)
    vmem = pl.BlockSpec(memory_space=pltpu.VMEM)
    smem = pl.BlockSpec(memory_space=pltpu.SMEM)
    half_type = jnp.bfloat16
    groups = None
    if not alone:
        groups = [[r * ways + head for head in range(ways)] for r in range(ranges)]

    packed = pl.pallas_call(
        pack_kernel,
        out_shape=jax.ShapeDtypeStruct((HEADS, 2, rows, LANES), half_type),
        in_specs=[vmem] * 4,
        out_specs=vmem,
        name="pack",
    )(queries, key_vectors, value_vectors, output_grad)
    sent = exchange(packed, ways, groups).reshape(ways, 2, 2, BLOCK, LANES)

    kernel = functools.partial(attend_kernel, alone, scale)
    back_shape = (ways, rows + BLOCK, LANES)
    if alone:
        back = pl.pallas_call(
            kernel,
            out_shape=jax.ShapeDtypeStruct(back_shape, half_type),
            in_specs=[smem, vmem],
            out_specs=vmem,
            scratch_shapes=[pltpu.VMEM((blocks, BLOCK, LANES), jnp.float32)],
            compiler_params=pltpu.CompilerParams(vmem_limit_bytes=48 * 2**20),
            name="attend",
        )(jnp.concatenate([rand_pick.reshape(-1), global_ids]), sent)
    else:
        back = spread_out(
            kernel, sent, rand_pick, global_ids, ways, ranges, blocks, back_shape, groups
        )
    received = exchange(back, ways, groups)
    return pl.pallas_call(
        unpack_kernel,
        out_shape=[jax.ShapeDtypeStruct((rows, width), half_type)] * 3,
        in_specs=[vmem],
        out_specs=[vmem] * 3,
        name="unpack",
    )(received)


def spread_out(kernel, sent, rand_pick, global_ids, ways, ranges, blocks, back_shape, groups):
    vmem = pl.BlockSpec(memory_space=pltpu.VMEM)
    smem = pl.BlockSpec(memory_space=pltpu.SMEM)
    mine = lax.axis_index("seq") // ways
    own = sent[:, 0].reshape(blocks, BLOCK, LANES)
    lags = [(slot + 1) * ranges // 4 for slot in range(RAND)]
    heads = [[r * ways + head for r in range(ranges)] for head in range(ways)]
    roots = global_ids // blocks
    offsets = global_ids % blocks
    pool = [own, moved(own[-1:], ranges, 1, ways, False), moved(own[:1], ranges, -1, ways, False)]
    chosen = jnp.where((roots == mine)[:, None, None], jnp.take(own, offsets, axis=0), 0)
    pool.append(lax.psum(chosen.astype(own.dtype), "seq", axis_index_groups=heads))
    for lag in lags:
        pool.append(moved(own[-1:], ranges, lag + 1, ways))
        pool.append(moved(own, ranges, lag, ways))
    pool = jnp.concatenate(pool, axis=0)
    picks = lax.dynamic_slice_in_dim(rand_pick, mine * blocks, blocks, 0)
    where = jnp.stack([mine, jnp.int32(ranges)]).astype(jnp.int32)
    table = jnp.concatenate([picks.reshape(-1), global_ids, where])
    grad_query, totals = pl.pallas_call(
        kernel,
        out_shape=[
            jax.ShapeDtypeStruct((ways, BLOCK, LANES), jnp.bfloat16),
            jax.ShapeDtypeStruct(pool.shape, jnp.float32),
        ],
        in_specs=[smem, vmem, vmem],
        out_specs=[vmem] * 2,
        compiler_params=pltpu.CompilerParams(vmem_limit_bytes=48 * 2**20),
        name="attend",
    )(table, sent, pool)
    total = totals[:blocks]
    total = total.at[-1].add(moved(totals[blocks], ranges, -1, ways, False))
    total = total.at[0].add(moved(totals[blocks + 1], ranges, 1, ways, False))
    base = blocks + 2
    summed = lax.psum(totals[base : base + GLOBAL], "seq", axis_index_groups=heads)
    for slot in range(GLOBAL):
        owned = jnp.where(roots[slot] == mine, summed[slot], 0.0)
        total = total.at[offsets[slot]].add(owned)
    base += GLOBAL
    for lag in lags:
        total = total.at[-1].add(moved(totals[base], ranges, -lag - 1, ways))
        total = total + moved(totals[base + 1 : base + 1 + blocks], ranges, -lag, ways)
        base += blocks + 1
    grads = total.astype(jnp.bfloat16).reshape(ways, 2 * BLOCK, LANES)
    return jnp.concatenate([grads, grad_query], axis=1).reshape(back_shape)


def solution(mesh):
    whole = P(("doc", "seq"), None)
    return jax.shard_map(
        on_device,
        mesh=mesh,
        in_specs=(whole, whole, whole, whole, P("doc", None), P("doc")),
        out_specs=(whole, whole, whole),
        check_vma=False,
    )
```

```python
import functools
import math

import jax
import jax.numpy as jnp
from jax import lax
from jax.experimental import pallas as pl
from jax.experimental.pallas import tpu as pltpu
from jax.sharding import PartitionSpec as P

HEADS = 8
BLOCK = 64
RAND = 3
GLOBAL = 2
HEAD = 64
LANES = 2 * HEAD
MASKED = -1e30


def low_lanes(shape):
    return lax.broadcasted_iota(jnp.int32, shape, len(shape) - 1) < HEAD


def swap_halves(block):
    return pltpu.roll(block, HEAD, 1)


def pack_kernel(q_ref, k_ref, v_ref, g_ref, *out_refs):
    rows = q_ref.shape[0]
    low = low_lanes((rows, LANES))
    place = lax.rem(lax.axis_index("seq"), HEADS)
    odd_place = lax.rem(place, 2) == 1
    for near in range(HEADS // 2):
        pair = lax.bitwise_xor(place // 2, near)
        lanes = pl.ds(pl.multiple_of(pair * LANES, LANES), LANES)
        for kind, (first_ref, second_ref) in enumerate(((k_ref, v_ref), (q_ref, g_ref))):
            first = first_ref[:, lanes].astype(jnp.float32)
            second = second_ref[:, lanes].astype(jnp.float32)
            even = jnp.where(low, first, swap_halves(second))
            odd = jnp.where(low, swap_halves(first), second)
            same = jnp.where(odd_place, odd, even).astype(jnp.bfloat16)
            other = jnp.where(odd_place, even, odd).astype(jnp.bfloat16)
            out_refs[2 * near][kind] = same
            out_refs[2 * near + 1][kind] = other


def unpack_kernel(*refs):
    in_refs, (gq_ref, gk_ref, gv_ref) = refs[:HEADS], refs[HEADS:]
    rows = gq_ref.shape[0]
    low = low_lanes((rows, LANES))
    low_block = low_lanes((BLOCK, LANES))
    place = lax.rem(lax.axis_index("seq"), HEADS)
    odd_place = lax.rem(place, 2) == 1
    for near in range(HEADS // 2):
        pair = lax.bitwise_xor(place // 2, near)
        lanes = pl.ds(pl.multiple_of(pair * LANES, LANES), LANES)
        same = in_refs[2 * near][...].astype(jnp.float32)
        other = in_refs[2 * near + 1][...].astype(jnp.float32)
        even = jnp.where(odd_place, other, same)
        odd = jnp.where(odd_place, same, other)
        gk = jnp.where(low, even[:rows], swap_halves(odd[:rows]))
        gv = jnp.where(low, swap_halves(even[:rows]), odd[:rows])
        gk_ref[:, lanes] = gk.astype(jnp.bfloat16)
        gv_ref[:, lanes] = gv.astype(jnp.bfloat16)
        first = jnp.where(low_block, even[rows:], swap_halves(odd[rows:]))
        second = jnp.where(low_block, swap_halves(even[rows:]), odd[rows:])
        gq_ref[:BLOCK, lanes] = first.astype(jnp.bfloat16)
        gq_ref[BLOCK:, lanes] = second.astype(jnp.bfloat16)


def attend_kernel(alone, scale, table_ref, *rest):
    if alone:
        in_refs, out_refs = rest[:HEADS], rest[HEADS : 2 * HEADS]
        sent_ref, gq_ref, acc_ref = rest[2 * HEADS :]
        place = lax.rem(lax.axis_index("seq"), HEADS)
        for m in range(HEADS):
            sent_ref[lax.bitwise_xor(place, m)] = in_refs[m][...]
    else:
        sent_ref, pool_ref, gq_ref, acc_ref = rest
    tiles = sent_ref.shape[0]
    blocks = 2 * tiles
    queries = 2 * BLOCK
    low = low_lanes((BLOCK, queries))
    zero = jnp.zeros((BLOCK, LANES), jnp.bfloat16)
    fixed = blocks * RAND
    acc_ref[...] = jnp.zeros_like(acc_ref)

    def pooled(entry):
        if alone:
            return sent_ref[entry // 2, 0, entry % 2]
        return pool_ref[entry]

    def chosen(tile):
        first = 2 * tile
        pairs = [(first, first), (first + 1, first + 1)]
        for slot in range(GLOBAL):
            entry = table_ref[fixed + slot] if alone else blocks + 2 + slot
            pairs.append((entry, entry))
        before, after = first - 1, first + 2
        if alone:
            before, after = max(before, 0), min(after, blocks - 1)
        else:
            before = before if tile > 0 else blocks
            after = after if tile < tiles - 1 else blocks + 1
        pairs.append((before, after))
        for slot in range(RAND):
            picked = []
            for block in (first, first + 1):
                pick = table_ref[block * RAND + slot]
                if alone:
                    behind = block + blocks - (slot + 1) * blocks // 4 - pick
                    picked.append(lax.rem(behind, blocks))
                else:
                    base = blocks + 2 + GLOBAL + slot * (blocks + 1)
                    picked.append(base + block + 1 - pick)
            pairs.append(tuple(picked))
        return pairs

    def multiply(tile):
        pairs = chosen(tile)
        keys = jnp.concatenate(
            [jnp.concatenate([pooled(a), pooled(b)], axis=1) for a, b in pairs], axis=0
        )
        first, second = sent_ref[tile, 1, 0], sent_ref[tile, 1, 1]
        rows = [
            [jnp.where(low, first * scale, zero), zero],
            [zero, jnp.where(low, second * scale, zero)],
            [jnp.where(low, zero, first), zero],
            [zero, jnp.where(low, zero, second)],
        ]
        sides = jnp.concatenate([jnp.concatenate(row, axis=1) for row in rows], axis=0)
        products = lax.dot_general(
            keys, sides, (((1,), (1,)), ((), ())), preferred_element_type=jnp.float32
        )
        return pairs, keys, sides, products

    def weigh(tile, products):
        scores, grad_probs = products[:, :queries], products[:, queries:]
        edge = (2 + GLOBAL) * BLOCK
        if tile == 0 or tile == tiles - 1:
            if tile == 0:
                keep = jnp.logical_not(low)
                if not alone:
                    keep = jnp.logical_or(keep, table_ref[fixed + GLOBAL] > 0)
            else:
                keep = low
                if not alone:
                    last = table_ref[fixed + GLOBAL + 1] - 1
                    keep = jnp.logical_or(keep, table_ref[fixed + GLOBAL] < last)
            masked = jnp.where(keep, scores[edge : edge + BLOCK], MASKED)
            scores = jnp.concatenate([scores[:edge], masked, scores[edge + BLOCK :]], axis=0)
        row_max = jnp.max(scores, axis=0, keepdims=True)
        expo = jnp.exp(scores - row_max)
        row_total = jnp.sum(expo, axis=0, keepdims=True)
        probs = expo * (1.0 / row_total)
        probs_half = probs.astype(jnp.bfloat16)
        row_dot = jnp.sum(probs_half.astype(jnp.float32) * grad_probs, axis=0, keepdims=True)
        grad_half = (probs * (grad_probs - row_dot)).astype(jnp.bfloat16)
        return grad_half, probs_half

    def gather(tile, pairs, keys, sides, grad_half, probs_half):
        both = jnp.concatenate([grad_half, probs_half], axis=1)
        key_grads = jnp.dot(both, sides, preferred_element_type=jnp.float32)
        grad_query = lax.dot_general(
            grad_half, keys, (((0,), (0,)), ((), ())), preferred_element_type=jnp.float32
        )
        grad_query = grad_query * scale
        folded = jnp.where(
            low, grad_query[:BLOCK, :LANES], swap_halves(grad_query[BLOCK:, LANES:])
        ).astype(jnp.bfloat16)
        gq_ref[tile] = folded
        for place, (a, b) in enumerate(pairs):
            part = key_grads[place * BLOCK : (place + 1) * BLOCK]
            if place < 2 + GLOBAL:
                acc_ref[a] += part[:, :LANES] + part[:, LANES:]
            else:
                acc_ref[a] += part[:, :LANES]
                acc_ref[b] += part[:, LANES:]

    ahead, weighed = {}, {}
    for step in range(tiles + 2):
        if step < tiles:
            ahead[step] = multiply(step)
        if 0 <= step - 1 < tiles:
            weighed[step - 1] = weigh(step - 1, ahead[step - 1][-1])
        if step >= 2:
            pairs, keys, sides, _ = ahead.pop(step - 2)
            gather(step - 2, pairs, keys, sides, *weighed.pop(step - 2))
    if alone:
        for m in range(HEADS):
            tile = lax.bitwise_xor(place, m)
            for half in range(2):
                grads = acc_ref[2 * tile + half].astype(jnp.bfloat16)
                out_refs[m][half * BLOCK : (half + 1) * BLOCK] = grads
            out_refs[m][queries:] = gq_ref[tile]


def exchange(parts):
    group = lax.axis_size("seq")
    arrived = list(parts)
    for m in reversed(range(1, HEADS)):
        route = [(i, i ^ m) for i in range(group)]
        arrived[m] = lax.ppermute(parts[m], "seq", route)
    return arrived


def moved(block, ranges, distance, ways, wrap=True):
    route = []
    for source in range(ranges):
        target = source + distance
        if wrap:
            target %= ranges
        if 0 <= target < ranges:
            route += [(source * ways + head, target * ways + head) for head in range(ways)]
    return lax.ppermute(block, "seq", route)


def on_device(queries, key_vectors, value_vectors, output_grad, rand_pick, global_ids):
    group = lax.axis_size("seq")
    rows, width = queries.shape
    ways = HEADS
    ranges = group // ways
    assert group % ways == 0 and (ranges == 1 or ranges % 4 == 0)
    alone = ranges == 1
    blocks = ways * rows // BLOCK
    scale = 1.0 / math.sqrt(width // HEADS)
    vmem = pl.BlockSpec(memory_space=pltpu.VMEM)
    smem = pl.BlockSpec(memory_space=pltpu.SMEM)
    half_type = jnp.bfloat16

    packed = pl.pallas_call(
        pack_kernel,
        out_shape=[jax.ShapeDtypeStruct((2, rows, LANES), half_type)] * HEADS,
        in_specs=[vmem] * 4,
        out_specs=[vmem] * HEADS,
        name="pack",
    )(queries, key_vectors, value_vectors, output_grad)
    sent = [part.reshape(2, 2, BLOCK, LANES) for part in exchange(packed)]

    kernel = functools.partial(attend_kernel, alone, scale)
    if alone:
        back = pl.pallas_call(
            kernel,
            out_shape=[jax.ShapeDtypeStruct((rows + BLOCK, LANES), half_type)] * HEADS,
            in_specs=[smem] + [vmem] * HEADS,
            out_specs=[vmem] * HEADS,
            scratch_shapes=[
                pltpu.VMEM((ways, 2, 2, BLOCK, LANES), half_type),
                pltpu.VMEM((ways, BLOCK, LANES), half_type),
                pltpu.VMEM((blocks, BLOCK, LANES), jnp.float32),
            ],
            compiler_params=pltpu.CompilerParams(vmem_limit_bytes=48 * 2**20),
            name="attend",
        )(jnp.concatenate([rand_pick.reshape(-1), global_ids]), *sent)
    else:
        back = spread_out(kernel, sent, rand_pick, global_ids, ways, ranges, blocks)
    received = exchange(back)
    return pl.pallas_call(
        unpack_kernel,
        out_shape=[jax.ShapeDtypeStruct((rows, width), half_type)] * 3,
        in_specs=[vmem] * HEADS,
        out_specs=[vmem] * 3,
        name="unpack",
    )(*received)


def spread_out(kernel, sent, rand_pick, global_ids, ways, ranges, blocks):
    vmem = pl.BlockSpec(memory_space=pltpu.VMEM)
    smem = pl.BlockSpec(memory_space=pltpu.SMEM)
    mine = lax.axis_index("seq") // ways
    order = lax.bitwise_xor(lax.axis_index("seq") % ways, jnp.arange(ways, dtype=jnp.int32))
    sent = jnp.take(jnp.stack(sent), order, axis=0)
    own = sent[:, 0].reshape(blocks, BLOCK, LANES)
    lags = [(slot + 1) * ranges // 4 for slot in range(RAND)]
    heads = [[r * ways + head for r in range(ranges)] for head in range(ways)]
    roots = global_ids // blocks
    offsets = global_ids % blocks
    pool = [own, moved(own[-1:], ranges, 1, ways, False), moved(own[:1], ranges, -1, ways, False)]
    chosen = jnp.where((roots == mine)[:, None, None], jnp.take(own, offsets, axis=0), 0)
    pool.append(lax.psum(chosen.astype(own.dtype), "seq", axis_index_groups=heads))
    for lag in lags:
        pool.append(moved(own[-1:], ranges, lag + 1, ways))
        pool.append(moved(own, ranges, lag, ways))
    pool = jnp.concatenate(pool, axis=0)
    picks = lax.dynamic_slice_in_dim(rand_pick, mine * blocks, blocks, 0)
    where = jnp.stack([mine, jnp.int32(ranges)]).astype(jnp.int32)
    table = jnp.concatenate([picks.reshape(-1), global_ids, where])
    grad_query, totals = pl.pallas_call(
        kernel,
        out_shape=[
            jax.ShapeDtypeStruct((ways, BLOCK, LANES), jnp.bfloat16),
            jax.ShapeDtypeStruct(pool.shape, jnp.float32),
        ],
        in_specs=[smem, vmem, vmem],
        out_specs=[vmem] * 2,
        compiler_params=pltpu.CompilerParams(vmem_limit_bytes=48 * 2**20),
        name="attend",
    )(table, sent, pool)
    total = totals[:blocks]
    total = total.at[-1].add(moved(totals[blocks], ranges, -1, ways, False))
    total = total.at[0].add(moved(totals[blocks + 1], ranges, 1, ways, False))
    base = blocks + 2
    summed = lax.psum(totals[base : base + GLOBAL], "seq", axis_index_groups=heads)
    for slot in range(GLOBAL):
        owned = jnp.where(roots[slot] == mine, summed[slot], 0.0)
        total = total.at[offsets[slot]].add(owned)
    base += GLOBAL
    for lag in lags:
        total = total.at[-1].add(moved(totals[base], ranges, -lag - 1, ways))
        total = total + moved(totals[base + 1 : base + 1 + blocks], ranges, -lag, ways)
        base += blocks + 1
    grads = total.astype(jnp.bfloat16).reshape(ways, 2 * BLOCK, LANES)
    back = jnp.take(jnp.concatenate([grads, grad_query], axis=1), order, axis=0)
    return [back[m] for m in range(ways)]


def solution(mesh):
    whole = P(("doc", "seq"), None)
    return jax.shard_map(
        on_device,
        mesh=mesh,
        in_specs=(whole, whole, whole, whole, P("doc", None), P("doc")),
        out_specs=(whole, whole, whole),
        check_vma=False,
    )
```

```python
import functools
import math

import jax
import jax.numpy as jnp
from jax import lax
from jax.experimental import pallas as pl
from jax.experimental.pallas import tpu as pltpu
from jax.sharding import PartitionSpec as P

HEADS = 8
BLOCK = 64
RAND = 3
GLOBAL = 2
HEAD = 64
LANES = 2 * HEAD
PARTNERS = (0, 4, 6, 5, 7, 3, 2, 1)
MASKED = -1e30


def low_lanes(shape):
    return lax.broadcasted_iota(jnp.int32, shape, len(shape) - 1) < HEAD


def swap_halves(block):
    return pltpu.roll(block, HEAD, 1)


def pack_kernel(q_ref, k_ref, v_ref, g_ref, *out_refs):
    rows = q_ref.shape[0]
    low = low_lanes((rows, LANES))
    place = lax.rem(lax.axis_index("seq"), HEADS)
    odd_place = lax.rem(place, 2) == 1
    for near in range(HEADS // 2):
        pair = lax.bitwise_xor(place // 2, near)
        lanes = pl.ds(pl.multiple_of(pair * LANES, LANES), LANES)
        for kind, (first_ref, second_ref) in enumerate(((k_ref, v_ref), (q_ref, g_ref))):
            first = first_ref[:, lanes].astype(jnp.float32)
            second = second_ref[:, lanes].astype(jnp.float32)
            even = jnp.where(low, first, swap_halves(second))
            odd = jnp.where(low, swap_halves(first), second)
            same = jnp.where(odd_place, odd, even).astype(jnp.bfloat16)
            other = jnp.where(odd_place, even, odd).astype(jnp.bfloat16)
            out_refs[2 * near][kind] = same
            out_refs[2 * near + 1][kind] = other


def unpack_kernel(*refs):
    in_refs = dict(zip(PARTNERS, refs[:HEADS]))
    gq_ref, gk_ref, gv_ref = refs[HEADS:]
    rows = gq_ref.shape[0]
    low = low_lanes((rows, LANES))
    low_block = low_lanes((BLOCK, LANES))
    place = lax.rem(lax.axis_index("seq"), HEADS)
    odd_place = lax.rem(place, 2) == 1
    for near in range(HEADS // 2):
        pair = lax.bitwise_xor(place // 2, near)
        lanes = pl.ds(pl.multiple_of(pair * LANES, LANES), LANES)
        same = in_refs[2 * near][...].astype(jnp.float32)
        other = in_refs[2 * near + 1][...].astype(jnp.float32)
        even = jnp.where(odd_place, other, same)
        odd = jnp.where(odd_place, same, other)
        gk = jnp.where(low, even[:rows], swap_halves(odd[:rows]))
        gv = jnp.where(low, swap_halves(even[:rows]), odd[:rows])
        gk_ref[:, lanes] = gk.astype(jnp.bfloat16)
        gv_ref[:, lanes] = gv.astype(jnp.bfloat16)
        first = jnp.where(low_block, even[rows:], swap_halves(odd[rows:]))
        second = jnp.where(low_block, swap_halves(even[rows:]), odd[rows:])
        gq_ref[:BLOCK, lanes] = first.astype(jnp.bfloat16)
        gq_ref[BLOCK:, lanes] = second.astype(jnp.bfloat16)


def attend_kernel(alone, scale, table_ref, *rest):
    if alone:
        in_refs = dict(zip(PARTNERS, rest[:HEADS]))
        out_refs = rest[HEADS : 2 * HEADS]
        sent_ref, gq_ref, acc_ref = rest[2 * HEADS :]
        place = lax.rem(lax.axis_index("seq"), HEADS)
        for m in range(HEADS):
            sent_ref[lax.bitwise_xor(place, m)] = in_refs[m][...]
    else:
        sent_ref, pool_ref, gq_ref, acc_ref = rest
    tiles = sent_ref.shape[0]
    blocks = 2 * tiles
    queries = 2 * BLOCK
    low = low_lanes((BLOCK, queries))
    zero = jnp.zeros((BLOCK, LANES), jnp.bfloat16)
    fixed = blocks * RAND
    acc_ref[...] = jnp.zeros_like(acc_ref)

    def pooled(entry):
        if alone:
            return sent_ref[entry // 2, 0, entry % 2]
        return pool_ref[entry]

    def chosen(tile):
        first = 2 * tile
        pairs = [(first, first), (first + 1, first + 1)]
        for slot in range(GLOBAL):
            entry = table_ref[fixed + slot] if alone else blocks + 2 + slot
            pairs.append((entry, entry))
        before, after = first - 1, first + 2
        if alone:
            before, after = max(before, 0), min(after, blocks - 1)
        else:
            before = before if tile > 0 else blocks
            after = after if tile < tiles - 1 else blocks + 1
        pairs.append((before, after))
        for slot in range(RAND):
            picked = []
            for block in (first, first + 1):
                pick = table_ref[block * RAND + slot]
                if alone:
                    behind = block + blocks - (slot + 1) * blocks // 4 - pick
                    picked.append(lax.rem(behind, blocks))
                else:
                    base = blocks + 2 + GLOBAL + slot * (blocks + 1)
                    picked.append(base + block + 1 - pick)
            pairs.append(tuple(picked))
        return pairs

    def multiply(tile):
        pairs = chosen(tile)
        keys = jnp.concatenate(
            [jnp.concatenate([pooled(a), pooled(b)], axis=1) for a, b in pairs], axis=0
        )
        first, second = sent_ref[tile, 1, 0], sent_ref[tile, 1, 1]
        rows = [
            [jnp.where(low, first * scale, zero), zero],
            [zero, jnp.where(low, second * scale, zero)],
            [jnp.where(low, zero, first), zero],
            [zero, jnp.where(low, zero, second)],
        ]
        sides = jnp.concatenate([jnp.concatenate(row, axis=1) for row in rows], axis=0)
        products = lax.dot_general(
            keys, sides, (((1,), (1,)), ((), ())), preferred_element_type=jnp.float32
        )
        return pairs, keys, sides, products

    def weigh(tile, products):
        scores, grad_probs = products[:, :queries], products[:, queries:]
        edge = (2 + GLOBAL) * BLOCK
        if tile == 0 or tile == tiles - 1:
            if tile == 0:
                keep = jnp.logical_not(low)
                if not alone:
                    keep = jnp.logical_or(keep, table_ref[fixed + GLOBAL] > 0)
            else:
                keep = low
                if not alone:
                    last = table_ref[fixed + GLOBAL + 1] - 1
                    keep = jnp.logical_or(keep, table_ref[fixed + GLOBAL] < last)
            masked = jnp.where(keep, scores[edge : edge + BLOCK], MASKED)
            scores = jnp.concatenate([scores[:edge], masked, scores[edge + BLOCK :]], axis=0)
        row_max = jnp.max(scores, axis=0, keepdims=True)
        expo = jnp.exp(scores - row_max)
        row_total = jnp.sum(expo, axis=0, keepdims=True)
        probs = expo * (1.0 / row_total)
        probs_half = probs.astype(jnp.bfloat16)
        row_dot = jnp.sum(probs_half.astype(jnp.float32) * grad_probs, axis=0, keepdims=True)
        grad_half = (probs * (grad_probs - row_dot)).astype(jnp.bfloat16)
        return grad_half, probs_half

    def gather(tile, pairs, keys, sides, grad_half, probs_half):
        both = jnp.concatenate([grad_half, probs_half], axis=1)
        key_grads = jnp.dot(both, sides, preferred_element_type=jnp.float32)
        grad_query = lax.dot_general(
            grad_half, keys, (((0,), (0,)), ((), ())), preferred_element_type=jnp.float32
        )
        grad_query = grad_query * scale
        folded = jnp.where(
            low, grad_query[:BLOCK, :LANES], swap_halves(grad_query[BLOCK:, LANES:])
        ).astype(jnp.bfloat16)
        gq_ref[tile] = folded
        for place, (a, b) in enumerate(pairs):
            part = key_grads[place * BLOCK : (place + 1) * BLOCK]
            if place < 2 + GLOBAL:
                acc_ref[a] += part[:, :LANES] + part[:, LANES:]
            else:
                acc_ref[a] += part[:, :LANES]
                acc_ref[b] += part[:, LANES:]

    ahead, weighed = {}, {}
    for step in range(tiles + 2):
        if step < tiles:
            ahead[step] = multiply(step)
        if 0 <= step - 1 < tiles:
            weighed[step - 1] = weigh(step - 1, ahead[step - 1][-1])
        if step >= 2:
            pairs, keys, sides, _ = ahead.pop(step - 2)
            gather(step - 2, pairs, keys, sides, *weighed.pop(step - 2))
    if alone:
        for m in range(HEADS):
            tile = lax.bitwise_xor(place, m)
            for half in range(2):
                grads = acc_ref[2 * tile + half].astype(jnp.bfloat16)
                out_refs[m][half * BLOCK : (half + 1) * BLOCK] = grads
            out_refs[m][queries:] = gq_ref[tile]


def exchange(parts):
    group = lax.axis_size("seq")
    arrived = list(parts)
    for m in PARTNERS[1:]:
        route = [(i, i ^ m) for i in range(group)]
        arrived[m] = lax.ppermute(parts[m], "seq", route)
    return arrived


def moved(block, ranges, distance, ways, wrap=True):
    route = []
    for source in range(ranges):
        target = source + distance
        if wrap:
            target %= ranges
        if 0 <= target < ranges:
            route += [(source * ways + head, target * ways + head) for head in range(ways)]
    return lax.ppermute(block, "seq", route)


def on_device(queries, key_vectors, value_vectors, output_grad, rand_pick, global_ids):
    group = lax.axis_size("seq")
    rows, width = queries.shape
    ways = HEADS
    ranges = group // ways
    assert group % ways == 0 and (ranges == 1 or ranges % 4 == 0)
    alone = ranges == 1
    blocks = ways * rows // BLOCK
    scale = 1.0 / math.sqrt(width // HEADS)
    vmem = pl.BlockSpec(memory_space=pltpu.VMEM)
    smem = pl.BlockSpec(memory_space=pltpu.SMEM)
    half_type = jnp.bfloat16

    packed = pl.pallas_call(
        pack_kernel,
        out_shape=[jax.ShapeDtypeStruct((2, rows, LANES), half_type)] * HEADS,
        in_specs=[vmem] * 4,
        out_specs=[vmem] * HEADS,
        compiler_params=pltpu.CompilerParams(vmem_limit_bytes=8 * 2**20),
        name="pack",
    )(queries, key_vectors, value_vectors, output_grad)
    sent = [part.reshape(2, 2, BLOCK, LANES) for part in exchange(packed)]

    kernel = functools.partial(attend_kernel, alone, scale)
    if alone:
        back = pl.pallas_call(
            kernel,
            out_shape=[jax.ShapeDtypeStruct((rows + BLOCK, LANES), half_type)] * HEADS,
            in_specs=[smem] + [vmem] * HEADS,
            out_specs=[vmem] * HEADS,
            scratch_shapes=[
                pltpu.VMEM((ways, 2, 2, BLOCK, LANES), half_type),
                pltpu.VMEM((ways, BLOCK, LANES), half_type),
                pltpu.VMEM((blocks, BLOCK, LANES), jnp.float32),
            ],
            compiler_params=pltpu.CompilerParams(vmem_limit_bytes=24 * 2**20),
            name="attend",
        )(jnp.concatenate([rand_pick.reshape(-1), global_ids]), *[sent[m] for m in PARTNERS])
    else:
        back = spread_out(kernel, sent, rand_pick, global_ids, ways, ranges, blocks)
    received = exchange(back)
    return pl.pallas_call(
        unpack_kernel,
        out_shape=[jax.ShapeDtypeStruct((rows, width), half_type)] * 3,
        in_specs=[vmem] * HEADS,
        out_specs=[vmem] * 3,
        compiler_params=pltpu.CompilerParams(vmem_limit_bytes=8 * 2**20),
        name="unpack",
    )(*[received[m] for m in PARTNERS])


def spread_out(kernel, sent, rand_pick, global_ids, ways, ranges, blocks):
    vmem = pl.BlockSpec(memory_space=pltpu.VMEM)
    smem = pl.BlockSpec(memory_space=pltpu.SMEM)
    mine = lax.axis_index("seq") // ways
    order = lax.bitwise_xor(lax.axis_index("seq") % ways, jnp.arange(ways, dtype=jnp.int32))
    sent = jnp.take(jnp.stack(sent), order, axis=0)
    own = sent[:, 0].reshape(blocks, BLOCK, LANES)
    lags = [(slot + 1) * ranges // 4 for slot in range(RAND)]
    heads = [[r * ways + head for r in range(ranges)] for head in range(ways)]
    roots = global_ids // blocks
    offsets = global_ids % blocks
    pool = [own, moved(own[-1:], ranges, 1, ways, False), moved(own[:1], ranges, -1, ways, False)]
    chosen = jnp.where((roots == mine)[:, None, None], jnp.take(own, offsets, axis=0), 0)
    pool.append(lax.psum(chosen.astype(own.dtype), "seq", axis_index_groups=heads))
    for lag in lags:
        pool.append(moved(own[-1:], ranges, lag + 1, ways))
        pool.append(moved(own, ranges, lag, ways))
    pool = jnp.concatenate(pool, axis=0)
    picks = lax.dynamic_slice_in_dim(rand_pick, mine * blocks, blocks, 0)
    where = jnp.stack([mine, jnp.int32(ranges)]).astype(jnp.int32)
    table = jnp.concatenate([picks.reshape(-1), global_ids, where])
    grad_query, totals = pl.pallas_call(
        kernel,
        out_shape=[
            jax.ShapeDtypeStruct((ways, BLOCK, LANES), jnp.bfloat16),
            jax.ShapeDtypeStruct(pool.shape, jnp.float32),
        ],
        in_specs=[smem, vmem, vmem],
        out_specs=[vmem] * 2,
        compiler_params=pltpu.CompilerParams(vmem_limit_bytes=24 * 2**20),
        name="attend",
    )(table, sent, pool)
    total = totals[:blocks]
    total = total.at[-1].add(moved(totals[blocks], ranges, -1, ways, False))
    total = total.at[0].add(moved(totals[blocks + 1], ranges, 1, ways, False))
    base = blocks + 2
    summed = lax.psum(totals[base : base + GLOBAL], "seq", axis_index_groups=heads)
    for slot in range(GLOBAL):
        owned = jnp.where(roots[slot] == mine, summed[slot], 0.0)
        total = total.at[offsets[slot]].add(owned)
    base += GLOBAL
    for lag in lags:
        total = total.at[-1].add(moved(totals[base], ranges, -lag - 1, ways))
        total = total + moved(totals[base + 1 : base + 1 + blocks], ranges, -lag, ways)
        base += blocks + 1
    grads = total.astype(jnp.bfloat16).reshape(ways, 2 * BLOCK, LANES)
    back = jnp.take(jnp.concatenate([grads, grad_query], axis=1), order, axis=0)
    return [back[m] for m in range(ways)]


def solution(mesh):
    whole = P(("doc", "seq"), None)
    return jax.shard_map(
        on_device,
        mesh=mesh,
        in_specs=(whole, whole, whole, whole, P("doc", None), P("doc")),
        out_specs=(whole, whole, whole),
        check_vma=False,
    )
```

```python
import functools
import math

import jax
import jax.numpy as jnp
from jax import lax
from jax.experimental import pallas as pl
from jax.experimental.pallas import tpu as pltpu
from jax.sharding import PartitionSpec as P

HEADS = 8
BLOCK = 64
RAND = 3
GLOBAL = 2
HEAD = 64
LANES = 2 * HEAD
PARTNERS = (0, 4, 6, 5, 7, 3, 2, 1)
MASKED = -1e30


def low_lanes(shape):
    return lax.broadcasted_iota(jnp.int32, shape, len(shape) - 1) < HEAD


def swap_halves(block):
    return pltpu.roll(block, HEAD, 1)


def pack_kernel(*refs):
    out_refs, held_ref, sems = refs[4 : 4 + HEADS], refs[-2], refs[-1]
    copies = [pltpu.make_async_copy(refs[i], held_ref.at[i], sems.at[i]) for i in range(4)]
    for copy in copies:
        copy.start()
    q_ref, k_ref, v_ref, g_ref = [held_ref.at[i] for i in range(4)]
    rows = held_ref.shape[1]
    low = low_lanes((rows, LANES))
    place = lax.rem(lax.axis_index("seq"), HEADS)
    odd_place = lax.rem(place, 2) == 1
    for copy in copies:
        copy.wait()
    for near in range(HEADS // 2):
        pair = lax.bitwise_xor(place // 2, near)
        lanes = pl.ds(pl.multiple_of(pair * LANES, LANES), LANES)
        for kind, (first_ref, second_ref) in enumerate(((k_ref, v_ref), (q_ref, g_ref))):
            first = first_ref[:, lanes].astype(jnp.float32)
            second = second_ref[:, lanes].astype(jnp.float32)
            even = jnp.where(low, first, swap_halves(second))
            odd = jnp.where(low, swap_halves(first), second)
            same = jnp.where(odd_place, odd, even).astype(jnp.bfloat16)
            other = jnp.where(odd_place, even, odd).astype(jnp.bfloat16)
            out_refs[2 * near][kind] = same
            out_refs[2 * near + 1][kind] = other


def unpack_kernel(*refs):
    in_refs = dict(zip(PARTNERS, refs[:HEADS]))
    gq_ref, gk_ref, gv_ref = refs[HEADS:]
    rows = gq_ref.shape[0]
    low = low_lanes((rows, LANES))
    low_block = low_lanes((BLOCK, LANES))
    place = lax.rem(lax.axis_index("seq"), HEADS)
    odd_place = lax.rem(place, 2) == 1
    for near in range(HEADS // 2):
        pair = lax.bitwise_xor(place // 2, near)
        lanes = pl.ds(pl.multiple_of(pair * LANES, LANES), LANES)
        same = in_refs[2 * near][...].astype(jnp.float32)
        other = in_refs[2 * near + 1][...].astype(jnp.float32)
        even = jnp.where(odd_place, other, same)
        odd = jnp.where(odd_place, same, other)
        gk = jnp.where(low, even[:rows], swap_halves(odd[:rows]))
        gv = jnp.where(low, swap_halves(even[:rows]), odd[:rows])
        gk_ref[:, lanes] = gk.astype(jnp.bfloat16)
        gv_ref[:, lanes] = gv.astype(jnp.bfloat16)
        first = jnp.where(low_block, even[rows:], swap_halves(odd[rows:]))
        second = jnp.where(low_block, swap_halves(even[rows:]), odd[rows:])
        gq_ref[:BLOCK, lanes] = first.astype(jnp.bfloat16)
        gq_ref[BLOCK:, lanes] = second.astype(jnp.bfloat16)


def attend_kernel(alone, scale, table_ref, *rest):
    if alone:
        in_refs = dict(zip(PARTNERS, rest[:HEADS]))
        out_refs = rest[HEADS : 2 * HEADS]
        sent_ref, gq_ref, acc_ref = rest[2 * HEADS :]
        place = lax.rem(lax.axis_index("seq"), HEADS)
        for m in range(HEADS):
            sent_ref[lax.bitwise_xor(place, m)] = in_refs[m][...]
    else:
        sent_ref, pool_ref, gq_ref, acc_ref = rest
    tiles = sent_ref.shape[0]
    blocks = 2 * tiles
    queries = 2 * BLOCK
    low = low_lanes((BLOCK, queries))
    zero = jnp.zeros((BLOCK, LANES), jnp.bfloat16)
    fixed = blocks * RAND
    acc_ref[...] = jnp.zeros_like(acc_ref)

    def pooled(entry):
        if alone:
            return sent_ref[entry // 2, 0, entry % 2]
        return pool_ref[entry]

    def chosen(tile):
        first = 2 * tile
        pairs = [(first, first), (first + 1, first + 1)]
        for slot in range(GLOBAL):
            entry = table_ref[fixed + slot] if alone else blocks + 2 + slot
            pairs.append((entry, entry))
        before, after = first - 1, first + 2
        if alone:
            before, after = max(before, 0), min(after, blocks - 1)
        else:
            before = before if tile > 0 else blocks
            after = after if tile < tiles - 1 else blocks + 1
        pairs.append((before, after))
        for slot in range(RAND):
            picked = []
            for block in (first, first + 1):
                pick = table_ref[block * RAND + slot]
                if alone:
                    behind = block + blocks - (slot + 1) * blocks // 4 - pick
                    picked.append(lax.rem(behind, blocks))
                else:
                    base = blocks + 2 + GLOBAL + slot * (blocks + 1)
                    picked.append(base + block + 1 - pick)
            pairs.append(tuple(picked))
        return pairs

    def multiply(tile):
        pairs = chosen(tile)
        keys = jnp.concatenate(
            [jnp.concatenate([pooled(a), pooled(b)], axis=1) for a, b in pairs], axis=0
        )
        first, second = sent_ref[tile, 1, 0], sent_ref[tile, 1, 1]
        rows = [
            [jnp.where(low, first * scale, zero), zero],
            [zero, jnp.where(low, second * scale, zero)],
            [jnp.where(low, zero, first), zero],
            [zero, jnp.where(low, zero, second)],
        ]
        sides = jnp.concatenate([jnp.concatenate(row, axis=1) for row in rows], axis=0)
        products = lax.dot_general(
            keys, sides, (((1,), (1,)), ((), ())), preferred_element_type=jnp.float32
        )
        return pairs, keys, sides, products

    def weigh(tile, products):
        scores, grad_probs = products[:, :queries], products[:, queries:]
        edge = (2 + GLOBAL) * BLOCK
        if tile == 0 or tile == tiles - 1:
            if tile == 0:
                keep = jnp.logical_not(low)
                if not alone:
                    keep = jnp.logical_or(keep, table_ref[fixed + GLOBAL] > 0)
            else:
                keep = low
                if not alone:
                    last = table_ref[fixed + GLOBAL + 1] - 1
                    keep = jnp.logical_or(keep, table_ref[fixed + GLOBAL] < last)
            masked = jnp.where(keep, scores[edge : edge + BLOCK], MASKED)
            scores = jnp.concatenate([scores[:edge], masked, scores[edge + BLOCK :]], axis=0)
        row_max = jnp.max(scores, axis=0, keepdims=True)
        expo = jnp.exp(scores - row_max)
        row_total = jnp.sum(expo, axis=0, keepdims=True)
        probs = expo * (1.0 / row_total)
        probs_half = probs.astype(jnp.bfloat16)
        row_dot = jnp.sum(probs_half.astype(jnp.float32) * grad_probs, axis=0, keepdims=True)
        grad_half = (probs * (grad_probs - row_dot)).astype(jnp.bfloat16)
        return grad_half, probs_half

    def gather(tile, pairs, keys, sides, grad_half, probs_half):
        both = jnp.concatenate([grad_half, probs_half], axis=1)
        key_grads = jnp.dot(both, sides, preferred_element_type=jnp.float32)
        grad_query = lax.dot_general(
            grad_half, keys, (((0,), (0,)), ((), ())), preferred_element_type=jnp.float32
        )
        grad_query = grad_query * scale
        folded = jnp.where(
            low, grad_query[:BLOCK, :LANES], swap_halves(grad_query[BLOCK:, LANES:])
        ).astype(jnp.bfloat16)
        gq_ref[tile] = folded
        for place, (a, b) in enumerate(pairs):
            part = key_grads[place * BLOCK : (place + 1) * BLOCK]
            if place < 2 + GLOBAL:
                acc_ref[a] += part[:, :LANES] + part[:, LANES:]
            else:
                acc_ref[a] += part[:, :LANES]
                acc_ref[b] += part[:, LANES:]

    ahead, weighed = {}, {}
    for step in range(tiles + 2):
        if step < tiles:
            ahead[step] = multiply(step)
        if 0 <= step - 1 < tiles:
            weighed[step - 1] = weigh(step - 1, ahead[step - 1][-1])
        if step >= 2:
            pairs, keys, sides, _ = ahead.pop(step - 2)
            gather(step - 2, pairs, keys, sides, *weighed.pop(step - 2))
    if alone:
        for m in range(HEADS):
            tile = lax.bitwise_xor(place, m)
            for half in range(2):
                grads = acc_ref[2 * tile + half].astype(jnp.bfloat16)
                out_refs[m][half * BLOCK : (half + 1) * BLOCK] = grads
            out_refs[m][queries:] = gq_ref[tile]


def exchange(parts):
    group = lax.axis_size("seq")
    arrived = list(parts)
    for m in PARTNERS[1:]:
        route = [(i, i ^ m) for i in range(group)]
        arrived[m] = lax.ppermute(parts[m], "seq", route)
    return arrived


def moved(block, ranges, distance, ways, wrap=True):
    route = []
    for source in range(ranges):
        target = source + distance
        if wrap:
            target %= ranges
        if 0 <= target < ranges:
            route += [(source * ways + head, target * ways + head) for head in range(ways)]
    return lax.ppermute(block, "seq", route)


def on_device(queries, key_vectors, value_vectors, output_grad, rand_pick, global_ids):
    group = lax.axis_size("seq")
    rows, width = queries.shape
    ways = HEADS
    ranges = group // ways
    assert group % ways == 0 and (ranges == 1 or ranges % 4 == 0)
    alone = ranges == 1
    blocks = ways * rows // BLOCK
    scale = 1.0 / math.sqrt(width // HEADS)
    vmem = pl.BlockSpec(memory_space=pltpu.VMEM)
    smem = pl.BlockSpec(memory_space=pltpu.SMEM)
    half_type = jnp.bfloat16

    packed = pl.pallas_call(
        pack_kernel,
        out_shape=[jax.ShapeDtypeStruct((2, rows, LANES), half_type)] * HEADS,
        in_specs=[pl.BlockSpec(memory_space=pltpu.HBM)] * 4,
        out_specs=[vmem] * HEADS,
        scratch_shapes=[
            pltpu.VMEM((4, rows, width), half_type),
            pltpu.SemaphoreType.DMA((4,)),
        ],
        compiler_params=pltpu.CompilerParams(vmem_limit_bytes=8 * 2**20),
        name="pack",
    )(queries, key_vectors, value_vectors, output_grad)
    sent = [part.reshape(2, 2, BLOCK, LANES) for part in exchange(packed)]

    kernel = functools.partial(attend_kernel, alone, scale)
    if alone:
        back = pl.pallas_call(
            kernel,
            out_shape=[jax.ShapeDtypeStruct((rows + BLOCK, LANES), half_type)] * HEADS,
            in_specs=[smem] + [vmem] * HEADS,
            out_specs=[vmem] * HEADS,
            scratch_shapes=[
                pltpu.VMEM((ways, 2, 2, BLOCK, LANES), half_type),
                pltpu.VMEM((ways, BLOCK, LANES), half_type),
                pltpu.VMEM((blocks, BLOCK, LANES), jnp.float32),
            ],
            compiler_params=pltpu.CompilerParams(vmem_limit_bytes=24 * 2**20),
            name="attend",
        )(jnp.concatenate([rand_pick.reshape(-1), global_ids]), *[sent[m] for m in PARTNERS])
    else:
        back = spread_out(kernel, sent, rand_pick, global_ids, ways, ranges, blocks)
    received = exchange(back)
    return pl.pallas_call(
        unpack_kernel,
        out_shape=[jax.ShapeDtypeStruct((rows, width), half_type)] * 3,
        in_specs=[vmem] * HEADS,
        out_specs=[vmem] * 3,
        compiler_params=pltpu.CompilerParams(vmem_limit_bytes=8 * 2**20),
        name="unpack",
    )(*[received[m] for m in PARTNERS])


def spread_out(kernel, sent, rand_pick, global_ids, ways, ranges, blocks):
    vmem = pl.BlockSpec(memory_space=pltpu.VMEM)
    smem = pl.BlockSpec(memory_space=pltpu.SMEM)
    mine = lax.axis_index("seq") // ways
    order = lax.bitwise_xor(lax.axis_index("seq") % ways, jnp.arange(ways, dtype=jnp.int32))
    sent = jnp.take(jnp.stack(sent), order, axis=0)
    own = sent[:, 0].reshape(blocks, BLOCK, LANES)
    lags = [(slot + 1) * ranges // 4 for slot in range(RAND)]
    heads = [[r * ways + head for r in range(ranges)] for head in range(ways)]
    roots = global_ids // blocks
    offsets = global_ids % blocks
    pool = [own, moved(own[-1:], ranges, 1, ways, False), moved(own[:1], ranges, -1, ways, False)]
    chosen = jnp.where((roots == mine)[:, None, None], jnp.take(own, offsets, axis=0), 0)
    pool.append(lax.psum(chosen.astype(own.dtype), "seq", axis_index_groups=heads))
    for lag in lags:
        pool.append(moved(own[-1:], ranges, lag + 1, ways))
        pool.append(moved(own, ranges, lag, ways))
    pool = jnp.concatenate(pool, axis=0)
    picks = lax.dynamic_slice_in_dim(rand_pick, mine * blocks, blocks, 0)
    where = jnp.stack([mine, jnp.int32(ranges)]).astype(jnp.int32)
    table = jnp.concatenate([picks.reshape(-1), global_ids, where])
    grad_query, totals = pl.pallas_call(
        kernel,
        out_shape=[
            jax.ShapeDtypeStruct((ways, BLOCK, LANES), jnp.bfloat16),
            jax.ShapeDtypeStruct(pool.shape, jnp.float32),
        ],
        in_specs=[smem, vmem, vmem],
        out_specs=[vmem] * 2,
        compiler_params=pltpu.CompilerParams(vmem_limit_bytes=24 * 2**20),
        name="attend",
    )(table, sent, pool)
    total = totals[:blocks]
    total = total.at[-1].add(moved(totals[blocks], ranges, -1, ways, False))
    total = total.at[0].add(moved(totals[blocks + 1], ranges, 1, ways, False))
    base = blocks + 2
    summed = lax.psum(totals[base : base + GLOBAL], "seq", axis_index_groups=heads)
    for slot in range(GLOBAL):
        owned = jnp.where(roots[slot] == mine, summed[slot], 0.0)
        total = total.at[offsets[slot]].add(owned)
    base += GLOBAL
    for lag in lags:
        total = total.at[-1].add(moved(totals[base], ranges, -lag - 1, ways))
        total = total + moved(totals[base + 1 : base + 1 + blocks], ranges, -lag, ways)
        base += blocks + 1
    grads = total.astype(jnp.bfloat16).reshape(ways, 2 * BLOCK, LANES)
    back = jnp.take(jnp.concatenate([grads, grad_query], axis=1), order, axis=0)
    return [back[m] for m in range(ways)]


def solution(mesh):
    whole = P(("doc", "seq"), None)
    return jax.shard_map(
        on_device,
        mesh=mesh,
        in_specs=(whole, whole, whole, whole, P("doc", None), P("doc")),
        out_specs=(whole, whole, whole),
        check_vma=False,
    )
```

```python
import functools
import math

import jax
import jax.numpy as jnp
from jax import lax
from jax.experimental import pallas as pl
from jax.experimental.pallas import tpu as pltpu
from jax.sharding import PartitionSpec as P

HEADS = 8
BLOCK = 64
RAND = 3
GLOBAL = 2
HEAD = 64
LANES = 2 * HEAD
PARTNERS = (0, 4, 6, 5, 7, 3, 2, 1)
NEAR = (2, 3, 1, 0)
MASKED = -1e30


def low_lanes(shape):
    return lax.broadcasted_iota(jnp.int32, shape, len(shape) - 1) < HEAD


def swap_halves(block):
    return pltpu.roll(block, HEAD, 1)


def pack_kernel(*refs):
    in_refs, out_refs = refs[:4], refs[4 : 4 + HEADS]
    held_ref, packed_ref, in_sems, out_sems = refs[4 + HEADS :]
    rows = held_ref.shape[2]
    low = low_lanes((rows, LANES))
    place = lax.rem(lax.axis_index("seq"), HEADS)
    odd_place = lax.rem(place, 2) == 1
    arriving = {}
    for near in NEAR:
        pair = lax.bitwise_xor(place // 2, near)
        lanes = pl.ds(pl.multiple_of(pair * LANES, LANES), LANES)
        for kind, ref in enumerate(in_refs):
            arriving[near, kind] = pltpu.make_async_copy(
                ref.at[:, lanes], held_ref.at[near, kind], in_sems.at[near, kind]
            )
            arriving[near, kind].start()
    leaving = []
    for near in NEAR:
        for kind in range(4):
            arriving[near, kind].wait()
        q, k, v, g = [held_ref[near, kind].astype(jnp.float32) for kind in range(4)]
        for kind, (first, second) in enumerate(((k, v), (q, g))):
            even = jnp.where(low, first, swap_halves(second))
            odd = jnp.where(low, swap_halves(first), second)
            same = jnp.where(odd_place, odd, even).astype(jnp.bfloat16)
            other = jnp.where(odd_place, even, odd).astype(jnp.bfloat16)
            packed_ref[2 * near, kind] = same
            packed_ref[2 * near + 1, kind] = other
        for m in (2 * near, 2 * near + 1):
            leaving.append(pltpu.make_async_copy(packed_ref.at[m], out_refs[m], out_sems.at[m]))
            leaving[-1].start()
    for copy in leaving:
        copy.wait()


def keep_kernel(in_ref, out_ref):
    out_ref[...] = in_ref[...]


def unpack_kernel(*refs):
    in_refs = dict(zip(PARTNERS, refs[:HEADS]))
    gq_ref, gk_ref, gv_ref = refs[HEADS:]
    rows = gq_ref.shape[0]
    low = low_lanes((rows, LANES))
    low_block = low_lanes((BLOCK, LANES))
    place = lax.rem(lax.axis_index("seq"), HEADS)
    odd_place = lax.rem(place, 2) == 1
    for near in range(HEADS // 2):
        pair = lax.bitwise_xor(place // 2, near)
        lanes = pl.ds(pl.multiple_of(pair * LANES, LANES), LANES)
        same = in_refs[2 * near][...].astype(jnp.float32)
        other = in_refs[2 * near + 1][...].astype(jnp.float32)
        even = jnp.where(odd_place, other, same)
        odd = jnp.where(odd_place, same, other)
        gk = jnp.where(low, even[:rows], swap_halves(odd[:rows]))
        gv = jnp.where(low, swap_halves(even[:rows]), odd[:rows])
        gk_ref[:, lanes] = gk.astype(jnp.bfloat16)
        gv_ref[:, lanes] = gv.astype(jnp.bfloat16)
        first = jnp.where(low_block, even[rows:], swap_halves(odd[rows:]))
        second = jnp.where(low_block, swap_halves(even[rows:]), odd[rows:])
        gq_ref[:BLOCK, lanes] = first.astype(jnp.bfloat16)
        gq_ref[BLOCK:, lanes] = second.astype(jnp.bfloat16)


def attend_kernel(alone, scale, table_ref, *rest):
    if alone:
        in_refs = dict(zip(PARTNERS, rest[:HEADS]))
        out_refs = rest[HEADS : 2 * HEADS]
        sent_ref, gq_ref, acc_ref = rest[2 * HEADS :]
        place = lax.rem(lax.axis_index("seq"), HEADS)
        for m in range(HEADS):
            sent_ref[lax.bitwise_xor(place, m)] = in_refs[m][...]
    else:
        sent_ref, pool_ref, gq_ref, acc_ref = rest
    tiles = sent_ref.shape[0]
    blocks = 2 * tiles
    queries = 2 * BLOCK
    low = low_lanes((BLOCK, queries))
    zero = jnp.zeros((BLOCK, LANES), jnp.bfloat16)
    fixed = blocks * RAND
    acc_ref[...] = jnp.zeros_like(acc_ref)

    def pooled(entry):
        if alone:
            return sent_ref[entry // 2, 0, entry % 2]
        return pool_ref[entry]

    def chosen(tile):
        first = 2 * tile
        pairs = [(first, first), (first + 1, first + 1)]
        for slot in range(GLOBAL):
            entry = table_ref[fixed + slot] if alone else blocks + 2 + slot
            pairs.append((entry, entry))
        before, after = first - 1, first + 2
        if alone:
            before, after = max(before, 0), min(after, blocks - 1)
        else:
            before = before if tile > 0 else blocks
            after = after if tile < tiles - 1 else blocks + 1
        pairs.append((before, after))
        for slot in range(RAND):
            picked = []
            for block in (first, first + 1):
                pick = table_ref[block * RAND + slot]
                if alone:
                    behind = block + blocks - (slot + 1) * blocks // 4 - pick
                    picked.append(lax.rem(behind, blocks))
                else:
                    base = blocks + 2 + GLOBAL + slot * (blocks + 1)
                    picked.append(base + block + 1 - pick)
            pairs.append(tuple(picked))
        return pairs

    def multiply(tile):
        pairs = chosen(tile)
        keys = jnp.concatenate(
            [jnp.concatenate([pooled(a), pooled(b)], axis=1) for a, b in pairs], axis=0
        )
        first, second = sent_ref[tile, 1, 0], sent_ref[tile, 1, 1]
        rows = [
            [jnp.where(low, first * scale, zero), zero],
            [zero, jnp.where(low, second * scale, zero)],
            [jnp.where(low, zero, first), zero],
            [zero, jnp.where(low, zero, second)],
        ]
        sides = jnp.concatenate([jnp.concatenate(row, axis=1) for row in rows], axis=0)
        products = lax.dot_general(
            keys, sides, (((1,), (1,)), ((), ())), preferred_element_type=jnp.float32
        )
        return pairs, keys, sides, products

    def weigh(tile, products):
        scores, grad_probs = products[:, :queries], products[:, queries:]
        edge = (2 + GLOBAL) * BLOCK
        if tile == 0 or tile == tiles - 1:
            if tile == 0:
                keep = jnp.logical_not(low)
                if not alone:
                    keep = jnp.logical_or(keep, table_ref[fixed + GLOBAL] > 0)
            else:
                keep = low
                if not alone:
                    last = table_ref[fixed + GLOBAL + 1] - 1
                    keep = jnp.logical_or(keep, table_ref[fixed + GLOBAL] < last)
            masked = jnp.where(keep, scores[edge : edge + BLOCK], MASKED)
            scores = jnp.concatenate([scores[:edge], masked, scores[edge + BLOCK :]], axis=0)
        row_max = jnp.max(scores, axis=0, keepdims=True)
        expo = jnp.exp(scores - row_max)
        row_total = jnp.sum(expo, axis=0, keepdims=True)
        probs = expo * (1.0 / row_total)
        probs_half = probs.astype(jnp.bfloat16)
        row_dot = jnp.sum(probs_half.astype(jnp.float32) * grad_probs, axis=0, keepdims=True)
        grad_half = (probs * (grad_probs - row_dot)).astype(jnp.bfloat16)
        return grad_half, probs_half

    def gather(tile, pairs, keys, sides, grad_half, probs_half):
        both = jnp.concatenate([grad_half, probs_half], axis=1)
        key_grads = jnp.dot(both, sides, preferred_element_type=jnp.float32)
        grad_query = lax.dot_general(
            grad_half, keys, (((0,), (0,)), ((), ())), preferred_element_type=jnp.float32
        )
        grad_query = grad_query * scale
        folded = jnp.where(
            low, grad_query[:BLOCK, :LANES], swap_halves(grad_query[BLOCK:, LANES:])
        ).astype(jnp.bfloat16)
        gq_ref[tile] = folded
        for place, (a, b) in enumerate(pairs):
            part = key_grads[place * BLOCK : (place + 1) * BLOCK]
            if place < 2 + GLOBAL:
                acc_ref[a] += part[:, :LANES] + part[:, LANES:]
            else:
                acc_ref[a] += part[:, :LANES]
                acc_ref[b] += part[:, LANES:]

    ahead, weighed = {}, {}
    for step in range(tiles + 2):
        if step < tiles:
            ahead[step] = multiply(step)
        if 0 <= step - 1 < tiles:
            weighed[step - 1] = weigh(step - 1, ahead[step - 1][-1])
        if step >= 2:
            pairs, keys, sides, _ = ahead.pop(step - 2)
            gather(step - 2, pairs, keys, sides, *weighed.pop(step - 2))
    if alone:
        for m in range(HEADS):
            tile = lax.bitwise_xor(place, m)
            for half in range(2):
                grads = acc_ref[2 * tile + half].astype(jnp.bfloat16)
                out_refs[m][half * BLOCK : (half + 1) * BLOCK] = grads
            out_refs[m][queries:] = gq_ref[tile]


def exchange(parts):
    group = lax.axis_size("seq")
    arrived = list(parts)
    for m in PARTNERS[1:]:
        route = [(i, i ^ m) for i in range(group)]
        arrived[m] = lax.ppermute(parts[m], "seq", route)
    return arrived


def moved(block, ranges, distance, ways, wrap=True):
    route = []
    for source in range(ranges):
        target = source + distance
        if wrap:
            target %= ranges
        if 0 <= target < ranges:
            route += [(source * ways + head, target * ways + head) for head in range(ways)]
    return lax.ppermute(block, "seq", route)


def on_device(queries, key_vectors, value_vectors, output_grad, rand_pick, global_ids):
    group = lax.axis_size("seq")
    rows, width = queries.shape
    ways = HEADS
    ranges = group // ways
    assert group % ways == 0 and (ranges == 1 or ranges % 4 == 0)
    alone = ranges == 1
    blocks = ways * rows // BLOCK
    scale = 1.0 / math.sqrt(width // HEADS)
    vmem = pl.BlockSpec(memory_space=pltpu.VMEM)
    smem = pl.BlockSpec(memory_space=pltpu.SMEM)
    half_type = jnp.bfloat16

    anywhere = pl.BlockSpec(memory_space=pl.ANY)
    packed = list(pl.pallas_call(
        pack_kernel,
        out_shape=[jax.ShapeDtypeStruct((2, rows, LANES), half_type)] * HEADS,
        in_specs=[anywhere] * 4,
        out_specs=[anywhere] * HEADS,
        scratch_shapes=[
            pltpu.VMEM((HEADS // 2, 4, rows, LANES), half_type),
            pltpu.VMEM((HEADS, 2, rows, LANES), half_type),
            pltpu.SemaphoreType.DMA((HEADS // 2, 4)),
            pltpu.SemaphoreType.DMA((HEADS,)),
        ],
        name="pack",
    )(queries, key_vectors, value_vectors, output_grad))
    packed[0] = pl.pallas_call(
        keep_kernel,
        out_shape=jax.ShapeDtypeStruct((2, rows, LANES), half_type),
        in_specs=[vmem],
        out_specs=vmem,
        compiler_params=pltpu.CompilerParams(vmem_limit_bytes=8 * 2**20),
        name="keep",
    )(packed[0])
    sent = [part.reshape(2, 2, BLOCK, LANES) for part in exchange(packed)]

    kernel = functools.partial(attend_kernel, alone, scale)
    if alone:
        back = pl.pallas_call(
            kernel,
            out_shape=[jax.ShapeDtypeStruct((rows + BLOCK, LANES), half_type)] * HEADS,
            in_specs=[smem] + [vmem] * HEADS,
            out_specs=[vmem] * HEADS,
            scratch_shapes=[
                pltpu.VMEM((ways, 2, 2, BLOCK, LANES), half_type),
                pltpu.VMEM((ways, BLOCK, LANES), half_type),
                pltpu.VMEM((blocks, BLOCK, LANES), jnp.float32),
            ],
            compiler_params=pltpu.CompilerParams(vmem_limit_bytes=24 * 2**20),
            name="attend",
        )(jnp.concatenate([rand_pick.reshape(-1), global_ids]), *[sent[m] for m in PARTNERS])
    else:
        back = spread_out(kernel, sent, rand_pick, global_ids, ways, ranges, blocks)
    received = exchange(back)
    return pl.pallas_call(
        unpack_kernel,
        out_shape=[jax.ShapeDtypeStruct((rows, width), half_type)] * 3,
        in_specs=[vmem] * HEADS,
        out_specs=[vmem] * 3,
        compiler_params=pltpu.CompilerParams(vmem_limit_bytes=8 * 2**20),
        name="unpack",
    )(*[received[m] for m in PARTNERS])


def spread_out(kernel, sent, rand_pick, global_ids, ways, ranges, blocks):
    vmem = pl.BlockSpec(memory_space=pltpu.VMEM)
    smem = pl.BlockSpec(memory_space=pltpu.SMEM)
    mine = lax.axis_index("seq") // ways
    order = lax.bitwise_xor(lax.axis_index("seq") % ways, jnp.arange(ways, dtype=jnp.int32))
    sent = jnp.take(jnp.stack(sent), order, axis=0)
    own = sent[:, 0].reshape(blocks, BLOCK, LANES)
    lags = [(slot + 1) * ranges // 4 for slot in range(RAND)]
    heads = [[r * ways + head for r in range(ranges)] for head in range(ways)]
    roots = global_ids // blocks
    offsets = global_ids % blocks
    pool = [own, moved(own[-1:], ranges, 1, ways, False), moved(own[:1], ranges, -1, ways, False)]
    chosen = jnp.where((roots == mine)[:, None, None], jnp.take(own, offsets, axis=0), 0)
    pool.append(lax.psum(chosen.astype(own.dtype), "seq", axis_index_groups=heads))
    for lag in lags:
        pool.append(moved(own[-1:], ranges, lag + 1, ways))
        pool.append(moved(own, ranges, lag, ways))
    pool = jnp.concatenate(pool, axis=0)
    picks = lax.dynamic_slice_in_dim(rand_pick, mine * blocks, blocks, 0)
    where = jnp.stack([mine, jnp.int32(ranges)]).astype(jnp.int32)
    table = jnp.concatenate([picks.reshape(-1), global_ids, where])
    grad_query, totals = pl.pallas_call(
        kernel,
        out_shape=[
            jax.ShapeDtypeStruct((ways, BLOCK, LANES), jnp.bfloat16),
            jax.ShapeDtypeStruct(pool.shape, jnp.float32),
        ],
        in_specs=[smem, vmem, vmem],
        out_specs=[vmem] * 2,
        compiler_params=pltpu.CompilerParams(vmem_limit_bytes=24 * 2**20),
        name="attend",
    )(table, sent, pool)
    total = totals[:blocks]
    total = total.at[-1].add(moved(totals[blocks], ranges, -1, ways, False))
    total = total.at[0].add(moved(totals[blocks + 1], ranges, 1, ways, False))
    base = blocks + 2
    summed = lax.psum(totals[base : base + GLOBAL], "seq", axis_index_groups=heads)
    for slot in range(GLOBAL):
        owned = jnp.where(roots[slot] == mine, summed[slot], 0.0)
        total = total.at[offsets[slot]].add(owned)
    base += GLOBAL
    for lag in lags:
        total = total.at[-1].add(moved(totals[base], ranges, -lag - 1, ways))
        total = total + moved(totals[base + 1 : base + 1 + blocks], ranges, -lag, ways)
        base += blocks + 1
    grads = total.astype(jnp.bfloat16).reshape(ways, 2 * BLOCK, LANES)
    back = jnp.take(jnp.concatenate([grads, grad_query], axis=1), order, axis=0)
    return [back[m] for m in range(ways)]


def solution(mesh):
    whole = P(("doc", "seq"), None)
    return jax.shard_map(
        on_device,
        mesh=mesh,
        in_specs=(whole, whole, whole, whole, P("doc", None), P("doc")),
        out_specs=(whole, whole, whole),
        check_vma=False,
    )
```

```python
import functools
import math

import jax
import jax.numpy as jnp
from jax import lax
from jax.experimental import pallas as pl
from jax.experimental.pallas import tpu as pltpu
from jax.sharding import PartitionSpec as P

HEADS = 8
BLOCK = 64
RAND = 3
GLOBAL = 2
HEAD = 64
LANES = 2 * HEAD
PARTNERS = (0, 4, 6, 5, 7, 3, 2, 1)
NEAR = (2, 3, 1, 0)
PACK_GRANT = 427 * 2**17
MASKED = -1e30


def low_lanes(shape):
    return lax.broadcasted_iota(jnp.int32, shape, len(shape) - 1) < HEAD


def swap_halves(block):
    return pltpu.roll(block, HEAD, 1)


def pack_kernel(*refs):
    in_refs, out_refs = refs[:4], refs[4 : 4 + HEADS]
    held_ref, in_sems = refs[4 + HEADS :]
    rows = held_ref.shape[2]
    low = low_lanes((rows, LANES))
    place = lax.rem(lax.axis_index("seq"), HEADS)
    odd_place = lax.rem(place, 2) == 1
    arriving = {}
    for near in NEAR:
        pair = lax.bitwise_xor(place // 2, near)
        lanes = pl.ds(pl.multiple_of(pair * LANES, LANES), LANES)
        for kind, ref in enumerate(in_refs):
            arriving[near, kind] = pltpu.make_async_copy(
                ref.at[:, lanes], held_ref.at[near, kind], in_sems.at[near, kind]
            )
            arriving[near, kind].start()
    for near in NEAR:
        for kind in range(4):
            arriving[near, kind].wait()
        q, k, v, g = [held_ref[near, kind].astype(jnp.float32) for kind in range(4)]
        for kind, (first, second) in enumerate(((k, v), (q, g))):
            even = jnp.where(low, first, swap_halves(second))
            odd = jnp.where(low, swap_halves(first), second)
            same = jnp.where(odd_place, odd, even).astype(jnp.bfloat16)
            other = jnp.where(odd_place, even, odd).astype(jnp.bfloat16)
            out_refs[2 * near][kind] = same
            out_refs[2 * near + 1][kind] = other


def unpack_kernel(*refs):
    in_refs = dict(zip(PARTNERS, refs[:HEADS]))
    gq_ref, gk_ref, gv_ref = refs[HEADS:]
    rows = gq_ref.shape[0]
    low = low_lanes((rows, LANES))
    low_block = low_lanes((BLOCK, LANES))
    place = lax.rem(lax.axis_index("seq"), HEADS)
    odd_place = lax.rem(place, 2) == 1
    for near in range(HEADS // 2):
        pair = lax.bitwise_xor(place // 2, near)
        lanes = pl.ds(pl.multiple_of(pair * LANES, LANES), LANES)
        same = in_refs[2 * near][...].astype(jnp.float32)
        other = in_refs[2 * near + 1][...].astype(jnp.float32)
        even = jnp.where(odd_place, other, same)
        odd = jnp.where(odd_place, same, other)
        gk = jnp.where(low, even[:rows], swap_halves(odd[:rows]))
        gv = jnp.where(low, swap_halves(even[:rows]), odd[:rows])
        gk_ref[:, lanes] = gk.astype(jnp.bfloat16)
        gv_ref[:, lanes] = gv.astype(jnp.bfloat16)
        first = jnp.where(low_block, even[rows:], swap_halves(odd[rows:]))
        second = jnp.where(low_block, swap_halves(even[rows:]), odd[rows:])
        gq_ref[:BLOCK, lanes] = first.astype(jnp.bfloat16)
        gq_ref[BLOCK:, lanes] = second.astype(jnp.bfloat16)


def attend_kernel(alone, scale, table_ref, *rest):
    if alone:
        in_refs = dict(zip(PARTNERS, rest[:HEADS]))
        out_refs = rest[HEADS : 2 * HEADS]
        sent_ref, gq_ref, acc_ref = rest[2 * HEADS :]
        place = lax.rem(lax.axis_index("seq"), HEADS)
        for m in range(HEADS):
            sent_ref[lax.bitwise_xor(place, m)] = in_refs[m][...]
    else:
        sent_ref, pool_ref, gq_ref, acc_ref = rest
    tiles = sent_ref.shape[0]
    blocks = 2 * tiles
    queries = 2 * BLOCK
    low = low_lanes((BLOCK, queries))
    zero = jnp.zeros((BLOCK, LANES), jnp.bfloat16)
    fixed = blocks * RAND
    acc_ref[...] = jnp.zeros_like(acc_ref)

    def pooled(entry):
        if alone:
            return sent_ref[entry // 2, 0, entry % 2]
        return pool_ref[entry]

    def chosen(tile):
        first = 2 * tile
        pairs = [(first, first), (first + 1, first + 1)]
        for slot in range(GLOBAL):
            entry = table_ref[fixed + slot] if alone else blocks + 2 + slot
            pairs.append((entry, entry))
        before, after = first - 1, first + 2
        if alone:
            before, after = max(before, 0), min(after, blocks - 1)
        else:
            before = before if tile > 0 else blocks
            after = after if tile < tiles - 1 else blocks + 1
        pairs.append((before, after))
        for slot in range(RAND):
            picked = []
            for block in (first, first + 1):
                pick = table_ref[block * RAND + slot]
                if alone:
                    behind = block + blocks - (slot + 1) * blocks // 4 - pick
                    picked.append(lax.rem(behind, blocks))
                else:
                    base = blocks + 2 + GLOBAL + slot * (blocks + 1)
                    picked.append(base + block + 1 - pick)
            pairs.append(tuple(picked))
        return pairs

    def multiply(tile):
        pairs = chosen(tile)
        keys = jnp.concatenate(
            [jnp.concatenate([pooled(a), pooled(b)], axis=1) for a, b in pairs], axis=0
        )
        first, second = sent_ref[tile, 1, 0], sent_ref[tile, 1, 1]
        rows = [
            [jnp.where(low, first * scale, zero), zero],
            [zero, jnp.where(low, second * scale, zero)],
            [jnp.where(low, zero, first), zero],
            [zero, jnp.where(low, zero, second)],
        ]
        sides = jnp.concatenate([jnp.concatenate(row, axis=1) for row in rows], axis=0)
        products = lax.dot_general(
            keys, sides, (((1,), (1,)), ((), ())), preferred_element_type=jnp.float32
        )
        return pairs, keys, sides, products

    def weigh(tile, products):
        scores, grad_probs = products[:, :queries], products[:, queries:]
        edge = (2 + GLOBAL) * BLOCK
        if tile == 0 or tile == tiles - 1:
            if tile == 0:
                keep = jnp.logical_not(low)
                if not alone:
                    keep = jnp.logical_or(keep, table_ref[fixed + GLOBAL] > 0)
            else:
                keep = low
                if not alone:
                    last = table_ref[fixed + GLOBAL + 1] - 1
                    keep = jnp.logical_or(keep, table_ref[fixed + GLOBAL] < last)
            masked = jnp.where(keep, scores[edge : edge + BLOCK], MASKED)
            scores = jnp.concatenate([scores[:edge], masked, scores[edge + BLOCK :]], axis=0)
        row_max = jnp.max(scores, axis=0, keepdims=True)
        expo = jnp.exp(scores - row_max)
        row_total = jnp.sum(expo, axis=0, keepdims=True)
        probs = expo * (1.0 / row_total)
        probs_half = probs.astype(jnp.bfloat16)
        row_dot = jnp.sum(probs_half.astype(jnp.float32) * grad_probs, axis=0, keepdims=True)
        grad_half = (probs * (grad_probs - row_dot)).astype(jnp.bfloat16)
        return grad_half, probs_half

    def gather(tile, pairs, keys, sides, grad_half, probs_half):
        both = jnp.concatenate([grad_half, probs_half], axis=1)
        key_grads = jnp.dot(both, sides, preferred_element_type=jnp.float32)
        grad_query = lax.dot_general(
            grad_half, keys, (((0,), (0,)), ((), ())), preferred_element_type=jnp.float32
        )
        grad_query = grad_query * scale
        folded = jnp.where(
            low, grad_query[:BLOCK, :LANES], swap_halves(grad_query[BLOCK:, LANES:])
        ).astype(jnp.bfloat16)
        gq_ref[tile] = folded
        for place, (a, b) in enumerate(pairs):
            part = key_grads[place * BLOCK : (place + 1) * BLOCK]
            if place < 2 + GLOBAL:
                acc_ref[a] += part[:, :LANES] + part[:, LANES:]
            else:
                acc_ref[a] += part[:, :LANES]
                acc_ref[b] += part[:, LANES:]

    ahead, weighed = {}, {}
    for step in range(tiles + 2):
        if step < tiles:
            ahead[step] = multiply(step)
        if 0 <= step - 1 < tiles:
            weighed[step - 1] = weigh(step - 1, ahead[step - 1][-1])
        if step >= 2:
            pairs, keys, sides, _ = ahead.pop(step - 2)
            gather(step - 2, pairs, keys, sides, *weighed.pop(step - 2))
    if alone:
        for m in range(HEADS):
            tile = lax.bitwise_xor(place, m)
            for half in range(2):
                grads = acc_ref[2 * tile + half].astype(jnp.bfloat16)
                out_refs[m][half * BLOCK : (half + 1) * BLOCK] = grads
            out_refs[m][queries:] = gq_ref[tile]


def exchange(parts):
    group = lax.axis_size("seq")
    arrived = list(parts)
    for m in PARTNERS[1:]:
        route = [(i, i ^ m) for i in range(group)]
        arrived[m] = lax.ppermute(parts[m], "seq", route)
    return arrived


def moved(block, ranges, distance, ways, wrap=True):
    route = []
    for source in range(ranges):
        target = source + distance
        if wrap:
            target %= ranges
        if 0 <= target < ranges:
            route += [(source * ways + head, target * ways + head) for head in range(ways)]
    return lax.ppermute(block, "seq", route)


def on_device(queries, key_vectors, value_vectors, output_grad, rand_pick, global_ids):
    group = lax.axis_size("seq")
    rows, width = queries.shape
    ways = HEADS
    ranges = group // ways
    assert group % ways == 0 and (ranges == 1 or ranges % 4 == 0)
    alone = ranges == 1
    blocks = ways * rows // BLOCK
    scale = 1.0 / math.sqrt(width // HEADS)
    vmem = pl.BlockSpec(memory_space=pltpu.VMEM)
    smem = pl.BlockSpec(memory_space=pltpu.SMEM)
    half_type = jnp.bfloat16

    anywhere = pl.BlockSpec(memory_space=pl.ANY)
    packed = pl.pallas_call(
        pack_kernel,
        out_shape=[jax.ShapeDtypeStruct((2, rows, LANES), half_type)] * HEADS,
        in_specs=[anywhere] * 4,
        out_specs=[vmem] * HEADS,
        scratch_shapes=[
            pltpu.VMEM((HEADS // 2, 4, rows, LANES), half_type),
            pltpu.SemaphoreType.DMA((HEADS // 2, 4)),
        ],
        compiler_params=pltpu.CompilerParams(vmem_limit_bytes=PACK_GRANT),
        name="pack",
    )(queries, key_vectors, value_vectors, output_grad)
    sent = [part.reshape(2, 2, BLOCK, LANES) for part in exchange(packed)]

    kernel = functools.partial(attend_kernel, alone, scale)
    if alone:
        back = pl.pallas_call(
            kernel,
            out_shape=[jax.ShapeDtypeStruct((rows + BLOCK, LANES), half_type)] * HEADS,
            in_specs=[smem] + [vmem] * HEADS,
            out_specs=[vmem] * HEADS,
            scratch_shapes=[
                pltpu.VMEM((ways, 2, 2, BLOCK, LANES), half_type),
                pltpu.VMEM((ways, BLOCK, LANES), half_type),
                pltpu.VMEM((blocks, BLOCK, LANES), jnp.float32),
            ],
            compiler_params=pltpu.CompilerParams(vmem_limit_bytes=24 * 2**20),
            name="attend",
        )(jnp.concatenate([rand_pick.reshape(-1), global_ids]), *[sent[m] for m in PARTNERS])
    else:
        back = spread_out(kernel, sent, rand_pick, global_ids, ways, ranges, blocks)
    received = exchange(back)
    return pl.pallas_call(
        unpack_kernel,
        out_shape=[jax.ShapeDtypeStruct((rows, width), half_type)] * 3,
        in_specs=[vmem] * HEADS,
        out_specs=[vmem] * 3,
        compiler_params=pltpu.CompilerParams(vmem_limit_bytes=8 * 2**20),
        name="unpack",
    )(*[received[m] for m in PARTNERS])


def spread_out(kernel, sent, rand_pick, global_ids, ways, ranges, blocks):
    vmem = pl.BlockSpec(memory_space=pltpu.VMEM)
    smem = pl.BlockSpec(memory_space=pltpu.SMEM)
    mine = lax.axis_index("seq") // ways
    order = lax.bitwise_xor(lax.axis_index("seq") % ways, jnp.arange(ways, dtype=jnp.int32))
    sent = jnp.take(jnp.stack(sent), order, axis=0)
    own = sent[:, 0].reshape(blocks, BLOCK, LANES)
    lags = [(slot + 1) * ranges // 4 for slot in range(RAND)]
    heads = [[r * ways + head for r in range(ranges)] for head in range(ways)]
    roots = global_ids // blocks
    offsets = global_ids % blocks
    pool = [own, moved(own[-1:], ranges, 1, ways, False), moved(own[:1], ranges, -1, ways, False)]
    chosen = jnp.where((roots == mine)[:, None, None], jnp.take(own, offsets, axis=0), 0)
    pool.append(lax.psum(chosen.astype(own.dtype), "seq", axis_index_groups=heads))
    for lag in lags:
        pool.append(moved(own[-1:], ranges, lag + 1, ways))
        pool.append(moved(own, ranges, lag, ways))
    pool = jnp.concatenate(pool, axis=0)
    picks = lax.dynamic_slice_in_dim(rand_pick, mine * blocks, blocks, 0)
    where = jnp.stack([mine, jnp.int32(ranges)]).astype(jnp.int32)
    table = jnp.concatenate([picks.reshape(-1), global_ids, where])
    grad_query, totals = pl.pallas_call(
        kernel,
        out_shape=[
            jax.ShapeDtypeStruct((ways, BLOCK, LANES), jnp.bfloat16),
            jax.ShapeDtypeStruct(pool.shape, jnp.float32),
        ],
        in_specs=[smem, vmem, vmem],
        out_specs=[vmem] * 2,
        compiler_params=pltpu.CompilerParams(vmem_limit_bytes=24 * 2**20),
        name="attend",
    )(table, sent, pool)
    total = totals[:blocks]
    total = total.at[-1].add(moved(totals[blocks], ranges, -1, ways, False))
    total = total.at[0].add(moved(totals[blocks + 1], ranges, 1, ways, False))
    base = blocks + 2
    summed = lax.psum(totals[base : base + GLOBAL], "seq", axis_index_groups=heads)
    for slot in range(GLOBAL):
        owned = jnp.where(roots[slot] == mine, summed[slot], 0.0)
        total = total.at[offsets[slot]].add(owned)
    base += GLOBAL
    for lag in lags:
        total = total.at[-1].add(moved(totals[base], ranges, -lag - 1, ways))
        total = total + moved(totals[base + 1 : base + 1 + blocks], ranges, -lag, ways)
        base += blocks + 1
    grads = total.astype(jnp.bfloat16).reshape(ways, 2 * BLOCK, LANES)
    back = jnp.take(jnp.concatenate([grads, grad_query], axis=1), order, axis=0)
    return [back[m] for m in range(ways)]


def solution(mesh):
    whole = P(("doc", "seq"), None)
    return jax.shard_map(
        on_device,
        mesh=mesh,
        in_specs=(whole, whole, whole, whole, P("doc", None), P("doc")),
        out_specs=(whole, whole, whole),
        check_vma=False,
    )
```

```python
import functools
import math

import jax
import jax.numpy as jnp
from jax import lax
from jax.experimental import pallas as pl
from jax.experimental.pallas import tpu as pltpu
from jax.sharding import PartitionSpec as P

HEADS = 8
BLOCK = 64
RAND = 3
GLOBAL = 2
HEAD = 64
LANES = 2 * HEAD
PARTNERS_IN = (0, 4, 6, 3, 7, 5, 2, 1)
PARTNERS_BACK = (0, 6, 5, 7, 3, 4, 2, 1)
NEAR = (2, 3, 1, 0)
PACK_GRANT = 427 * 2**17
MASKED = -1e30


def low_lanes(shape):
    return lax.broadcasted_iota(jnp.int32, shape, len(shape) - 1) < HEAD


def swap_halves(block):
    return pltpu.roll(block, HEAD, 1)


def pack_kernel(*refs):
    in_refs, out_refs = refs[:4], refs[4 : 4 + HEADS]
    held_ref, in_sems = refs[4 + HEADS :]
    rows = held_ref.shape[2]
    low = low_lanes((rows, LANES))
    place = lax.rem(lax.axis_index("seq"), HEADS)
    odd_place = lax.rem(place, 2) == 1
    arriving = {}
    for near in NEAR:
        pair = lax.bitwise_xor(place // 2, near)
        lanes = pl.ds(pl.multiple_of(pair * LANES, LANES), LANES)
        for kind, ref in enumerate(in_refs):
            arriving[near, kind] = pltpu.make_async_copy(
                ref.at[:, lanes], held_ref.at[near, kind], in_sems.at[near, kind]
            )
            arriving[near, kind].start()
    for near in NEAR:
        for kind in range(4):
            arriving[near, kind].wait()
        q, k, v, g = [held_ref[near, kind].astype(jnp.float32) for kind in range(4)]
        for kind, (first, second) in enumerate(((k, v), (q, g))):
            even = jnp.where(low, first, swap_halves(second))
            odd = jnp.where(low, swap_halves(first), second)
            same = jnp.where(odd_place, odd, even).astype(jnp.bfloat16)
            other = jnp.where(odd_place, even, odd).astype(jnp.bfloat16)
            out_refs[2 * near][kind] = same
            out_refs[2 * near + 1][kind] = other


def unpack_kernel(*refs):
    in_refs = dict(zip(PARTNERS_BACK, refs[:HEADS]))
    gq_ref, gk_ref, gv_ref = refs[HEADS:]
    rows = gq_ref.shape[0]
    low = low_lanes((rows, LANES))
    low_block = low_lanes((BLOCK, LANES))
    place = lax.rem(lax.axis_index("seq"), HEADS)
    odd_place = lax.rem(place, 2) == 1
    for near in range(HEADS // 2):
        pair = lax.bitwise_xor(place // 2, near)
        lanes = pl.ds(pl.multiple_of(pair * LANES, LANES), LANES)
        same = in_refs[2 * near][...].astype(jnp.float32)
        other = in_refs[2 * near + 1][...].astype(jnp.float32)
        even = jnp.where(odd_place, other, same)
        odd = jnp.where(odd_place, same, other)
        gk = jnp.where(low, even[:rows], swap_halves(odd[:rows]))
        gv = jnp.where(low, swap_halves(even[:rows]), odd[:rows])
        gk_ref[:, lanes] = gk.astype(jnp.bfloat16)
        gv_ref[:, lanes] = gv.astype(jnp.bfloat16)
        first = jnp.where(low_block, even[rows:], swap_halves(odd[rows:]))
        second = jnp.where(low_block, swap_halves(even[rows:]), odd[rows:])
        gq_ref[:BLOCK, lanes] = first.astype(jnp.bfloat16)
        gq_ref[BLOCK:, lanes] = second.astype(jnp.bfloat16)


def attend_kernel(alone, scale, table_ref, *rest):
    if alone:
        in_refs = dict(zip(PARTNERS_IN, rest[:HEADS]))
        out_refs = rest[HEADS : 2 * HEADS]
        sent_ref, gq_ref, acc_ref = rest[2 * HEADS :]
        place = lax.rem(lax.axis_index("seq"), HEADS)
        for m in range(HEADS):
            sent_ref[lax.bitwise_xor(place, m)] = in_refs[m][...]
    else:
        sent_ref, pool_ref, gq_ref, acc_ref = rest
    tiles = sent_ref.shape[0]
    blocks = 2 * tiles
    queries = 2 * BLOCK
    low = low_lanes((BLOCK, queries))
    zero = jnp.zeros((BLOCK, LANES), jnp.bfloat16)
    fixed = blocks * RAND
    acc_ref[...] = jnp.zeros_like(acc_ref)

    def pooled(entry):
        if alone:
            return sent_ref[entry // 2, 0, entry % 2]
        return pool_ref[entry]

    def chosen(tile):
        first = 2 * tile
        pairs = [(first, first), (first + 1, first + 1)]
        for slot in range(GLOBAL):
            entry = table_ref[fixed + slot] if alone else blocks + 2 + slot
            pairs.append((entry, entry))
        before, after = first - 1, first + 2
        if alone:
            before, after = max(before, 0), min(after, blocks - 1)
        else:
            before = before if tile > 0 else blocks
            after = after if tile < tiles - 1 else blocks + 1
        pairs.append((before, after))
        for slot in range(RAND):
            picked = []
            for block in (first, first + 1):
                pick = table_ref[block * RAND + slot]
                if alone:
                    behind = block + blocks - (slot + 1) * blocks // 4 - pick
                    picked.append(lax.rem(behind, blocks))
                else:
                    base = blocks + 2 + GLOBAL + slot * (blocks + 1)
                    picked.append(base + block + 1 - pick)
            pairs.append(tuple(picked))
        return pairs

    def multiply(tile):
        pairs = chosen(tile)
        keys = jnp.concatenate(
            [jnp.concatenate([pooled(a), pooled(b)], axis=1) for a, b in pairs], axis=0
        )
        first, second = sent_ref[tile, 1, 0], sent_ref[tile, 1, 1]
        rows = [
            [jnp.where(low, first * scale, zero), zero],
            [zero, jnp.where(low, second * scale, zero)],
            [jnp.where(low, zero, first), zero],
            [zero, jnp.where(low, zero, second)],
        ]
        sides = jnp.concatenate([jnp.concatenate(row, axis=1) for row in rows], axis=0)
        products = lax.dot_general(
            keys, sides, (((1,), (1,)), ((), ())), preferred_element_type=jnp.float32
        )
        return pairs, keys, sides, products

    def weigh(tile, products):
        scores, grad_probs = products[:, :queries], products[:, queries:]
        edge = (2 + GLOBAL) * BLOCK
        if tile == 0 or tile == tiles - 1:
            if tile == 0:
                keep = jnp.logical_not(low)
                if not alone:
                    keep = jnp.logical_or(keep, table_ref[fixed + GLOBAL] > 0)
            else:
                keep = low
                if not alone:
                    last = table_ref[fixed + GLOBAL + 1] - 1
                    keep = jnp.logical_or(keep, table_ref[fixed + GLOBAL] < last)
            masked = jnp.where(keep, scores[edge : edge + BLOCK], MASKED)
            scores = jnp.concatenate([scores[:edge], masked, scores[edge + BLOCK :]], axis=0)
        row_max = jnp.max(scores, axis=0, keepdims=True)
        expo = jnp.exp(scores - row_max)
        row_total = jnp.sum(expo, axis=0, keepdims=True)
        probs = expo * (1.0 / row_total)
        probs_half = probs.astype(jnp.bfloat16)
        row_dot = jnp.sum(probs_half.astype(jnp.float32) * grad_probs, axis=0, keepdims=True)
        grad_half = (probs * (grad_probs - row_dot)).astype(jnp.bfloat16)
        return grad_half, probs_half

    def gather(tile, pairs, keys, sides, grad_half, probs_half):
        both = jnp.concatenate([grad_half, probs_half], axis=1)
        key_grads = jnp.dot(both, sides, preferred_element_type=jnp.float32)
        grad_query = lax.dot_general(
            grad_half, keys, (((0,), (0,)), ((), ())), preferred_element_type=jnp.float32
        )
        grad_query = grad_query * scale
        folded = jnp.where(
            low, grad_query[:BLOCK, :LANES], swap_halves(grad_query[BLOCK:, LANES:])
        ).astype(jnp.bfloat16)
        gq_ref[tile] = folded
        for place, (a, b) in enumerate(pairs):
            part = key_grads[place * BLOCK : (place + 1) * BLOCK]
            if place < 2 + GLOBAL:
                acc_ref[a] += part[:, :LANES] + part[:, LANES:]
            else:
                acc_ref[a] += part[:, :LANES]
                acc_ref[b] += part[:, LANES:]

    ahead, weighed = {}, {}
    for step in range(tiles + 2):
        if step < tiles:
            ahead[step] = multiply(step)
        if 0 <= step - 1 < tiles:
            weighed[step - 1] = weigh(step - 1, ahead[step - 1][-1])
        if step >= 2:
            pairs, keys, sides, _ = ahead.pop(step - 2)
            gather(step - 2, pairs, keys, sides, *weighed.pop(step - 2))
    if alone:
        for m in range(HEADS):
            tile = lax.bitwise_xor(place, m)
            for half in range(2):
                grads = acc_ref[2 * tile + half].astype(jnp.bfloat16)
                out_refs[m][half * BLOCK : (half + 1) * BLOCK] = grads
            out_refs[m][queries:] = gq_ref[tile]


def exchange(parts, partners):
    group = lax.axis_size("seq")
    arrived = list(parts)
    for m in partners[1:]:
        route = [(i, i ^ m) for i in range(group)]
        arrived[m] = lax.ppermute(parts[m], "seq", route)
    return arrived


def moved(block, ranges, distance, ways, wrap=True):
    route = []
    for source in range(ranges):
        target = source + distance
        if wrap:
            target %= ranges
        if 0 <= target < ranges:
            route += [(source * ways + head, target * ways + head) for head in range(ways)]
    return lax.ppermute(block, "seq", route)


def on_device(queries, key_vectors, value_vectors, output_grad, rand_pick, global_ids):
    group = lax.axis_size("seq")
    rows, width = queries.shape
    ways = HEADS
    ranges = group // ways
    assert group % ways == 0 and (ranges == 1 or ranges % 4 == 0)
    alone = ranges == 1
    blocks = ways * rows // BLOCK
    scale = 1.0 / math.sqrt(width // HEADS)
    vmem = pl.BlockSpec(memory_space=pltpu.VMEM)
    smem = pl.BlockSpec(memory_space=pltpu.SMEM)
    half_type = jnp.bfloat16

    anywhere = pl.BlockSpec(memory_space=pl.ANY)
    packed = pl.pallas_call(
        pack_kernel,
        out_shape=[jax.ShapeDtypeStruct((2, rows, LANES), half_type)] * HEADS,
        in_specs=[anywhere] * 4,
        out_specs=[vmem] * HEADS,
        scratch_shapes=[
            pltpu.VMEM((HEADS // 2, 4, rows, LANES), half_type),
            pltpu.SemaphoreType.DMA((HEADS // 2, 4)),
        ],
        compiler_params=pltpu.CompilerParams(vmem_limit_bytes=PACK_GRANT),
        name="pack",
    )(queries, key_vectors, value_vectors, output_grad)
    sent = [part.reshape(2, 2, BLOCK, LANES) for part in exchange(packed, PARTNERS_IN)]

    kernel = functools.partial(attend_kernel, alone, scale)
    if alone:
        back = pl.pallas_call(
            kernel,
            out_shape=[jax.ShapeDtypeStruct((rows + BLOCK, LANES), half_type)] * HEADS,
            in_specs=[smem] + [vmem] * HEADS,
            out_specs=[vmem] * HEADS,
            scratch_shapes=[
                pltpu.VMEM((ways, 2, 2, BLOCK, LANES), half_type),
                pltpu.VMEM((ways, BLOCK, LANES), half_type),
                pltpu.VMEM((blocks, BLOCK, LANES), jnp.float32),
            ],
            compiler_params=pltpu.CompilerParams(vmem_limit_bytes=24 * 2**20),
            name="attend",
        )(jnp.concatenate([rand_pick.reshape(-1), global_ids]), *[sent[m] for m in PARTNERS_IN])
    else:
        back = spread_out(kernel, sent, rand_pick, global_ids, ways, ranges, blocks)
    received = exchange(back, PARTNERS_BACK)
    return pl.pallas_call(
        unpack_kernel,
        out_shape=[jax.ShapeDtypeStruct((rows, width), half_type)] * 3,
        in_specs=[vmem] * HEADS,
        out_specs=[vmem] * 3,
        compiler_params=pltpu.CompilerParams(vmem_limit_bytes=8 * 2**20),
        name="unpack",
    )(*[received[m] for m in PARTNERS_BACK])


def spread_out(kernel, sent, rand_pick, global_ids, ways, ranges, blocks):
    vmem = pl.BlockSpec(memory_space=pltpu.VMEM)
    smem = pl.BlockSpec(memory_space=pltpu.SMEM)
    mine = lax.axis_index("seq") // ways
    order = lax.bitwise_xor(lax.axis_index("seq") % ways, jnp.arange(ways, dtype=jnp.int32))
    sent = jnp.take(jnp.stack(sent), order, axis=0)
    own = sent[:, 0].reshape(blocks, BLOCK, LANES)
    lags = [(slot + 1) * ranges // 4 for slot in range(RAND)]
    heads = [[r * ways + head for r in range(ranges)] for head in range(ways)]
    roots = global_ids // blocks
    offsets = global_ids % blocks
    pool = [own, moved(own[-1:], ranges, 1, ways, False), moved(own[:1], ranges, -1, ways, False)]
    chosen = jnp.where((roots == mine)[:, None, None], jnp.take(own, offsets, axis=0), 0)
    pool.append(lax.psum(chosen.astype(own.dtype), "seq", axis_index_groups=heads))
    for lag in lags:
        pool.append(moved(own[-1:], ranges, lag + 1, ways))
        pool.append(moved(own, ranges, lag, ways))
    pool = jnp.concatenate(pool, axis=0)
    picks = lax.dynamic_slice_in_dim(rand_pick, mine * blocks, blocks, 0)
    where = jnp.stack([mine, jnp.int32(ranges)]).astype(jnp.int32)
    table = jnp.concatenate([picks.reshape(-1), global_ids, where])
    grad_query, totals = pl.pallas_call(
        kernel,
        out_shape=[
            jax.ShapeDtypeStruct((ways, BLOCK, LANES), jnp.bfloat16),
            jax.ShapeDtypeStruct(pool.shape, jnp.float32),
        ],
        in_specs=[smem, vmem, vmem],
        out_specs=[vmem] * 2,
        compiler_params=pltpu.CompilerParams(vmem_limit_bytes=24 * 2**20),
        name="attend",
    )(table, sent, pool)
    total = totals[:blocks]
    total = total.at[-1].add(moved(totals[blocks], ranges, -1, ways, False))
    total = total.at[0].add(moved(totals[blocks + 1], ranges, 1, ways, False))
    base = blocks + 2
    summed = lax.psum(totals[base : base + GLOBAL], "seq", axis_index_groups=heads)
    for slot in range(GLOBAL):
        owned = jnp.where(roots[slot] == mine, summed[slot], 0.0)
        total = total.at[offsets[slot]].add(owned)
    base += GLOBAL
    for lag in lags:
        total = total.at[-1].add(moved(totals[base], ranges, -lag - 1, ways))
        total = total + moved(totals[base + 1 : base + 1 + blocks], ranges, -lag, ways)
        base += blocks + 1
    grads = total.astype(jnp.bfloat16).reshape(ways, 2 * BLOCK, LANES)
    back = jnp.take(jnp.concatenate([grads, grad_query], axis=1), order, axis=0)
    return [back[m] for m in range(ways)]


def solution(mesh):
    whole = P(("doc", "seq"), None)
    return jax.shard_map(
        on_device,
        mesh=mesh,
        in_specs=(whole, whole, whole, whole, P("doc", None), P("doc")),
        out_specs=(whole, whole, whole),
        check_vma=False,
    )
```

```python
import functools
import math

import jax
import jax.numpy as jnp
from jax import lax
from jax.experimental import pallas as pl
from jax.experimental.pallas import tpu as pltpu
from jax.sharding import PartitionSpec as P

HEADS = 8
BLOCK = 64
RAND = 3
GLOBAL = 2
HEAD = 64
LANES = 2 * HEAD
PARTNERS_IN = (0, 6, 5, 7, 3, 4, 2, 1)
PARTNERS_BACK = (0, 2, 6, 3, 5, 4, 1)
NEAR = (2, 3, 1, 0)
PACK_GRANT = 427 * 2**17
MASKED = -1e30


def low_lanes(shape):
    return lax.broadcasted_iota(jnp.int32, shape, len(shape) - 1) < HEAD


def swap_halves(block):
    return pltpu.roll(block, HEAD, 1)


def pack_kernel(*refs):
    in_refs, out_refs = refs[:4], refs[4 : 4 + HEADS]
    held_ref, in_sems = refs[4 + HEADS :]
    rows = held_ref.shape[2]
    low = low_lanes((rows, LANES))
    place = lax.rem(lax.axis_index("seq"), HEADS)
    odd_place = lax.rem(place, 2) == 1
    arriving = {}
    for near in NEAR:
        pair = lax.bitwise_xor(place // 2, near)
        lanes = pl.ds(pl.multiple_of(pair * LANES, LANES), LANES)
        for kind, ref in enumerate(in_refs):
            arriving[near, kind] = pltpu.make_async_copy(
                ref.at[:, lanes], held_ref.at[near, kind], in_sems.at[near, kind]
            )
            arriving[near, kind].start()
    for near in NEAR:
        for kind in range(4):
            arriving[near, kind].wait()
        q, k, v, g = [held_ref[near, kind].astype(jnp.float32) for kind in range(4)]
        for kind, (first, second) in enumerate(((k, v), (q, g))):
            even = jnp.where(low, first, swap_halves(second))
            odd = jnp.where(low, swap_halves(first), second)
            same = jnp.where(odd_place, odd, even).astype(jnp.bfloat16)
            other = jnp.where(odd_place, even, odd).astype(jnp.bfloat16)
            out_refs[2 * near][kind] = same
            out_refs[2 * near + 1][kind] = other


def unpack_kernel(*refs):
    in_refs = dict(zip(PARTNERS_BACK + (7,), refs))
    in_refs[6] = in_refs[6].at[0]
    gq_ref, gk_ref, gv_ref = refs[HEADS:]
    rows = gq_ref.shape[0]
    low = low_lanes((rows, LANES))
    low_block = low_lanes((BLOCK, LANES))
    place = lax.rem(lax.axis_index("seq"), HEADS)
    odd_place = lax.rem(place, 2) == 1
    for near in range(HEADS // 2):
        pair = lax.bitwise_xor(place // 2, near)
        lanes = pl.ds(pl.multiple_of(pair * LANES, LANES), LANES)
        same = in_refs[2 * near][...].astype(jnp.float32)
        other = in_refs[2 * near + 1][...].astype(jnp.float32)
        even = jnp.where(odd_place, other, same)
        odd = jnp.where(odd_place, same, other)
        gk = jnp.where(low, even[:rows], swap_halves(odd[:rows]))
        gv = jnp.where(low, swap_halves(even[:rows]), odd[:rows])
        gk_ref[:, lanes] = gk.astype(jnp.bfloat16)
        gv_ref[:, lanes] = gv.astype(jnp.bfloat16)
        first = jnp.where(low_block, even[rows:], swap_halves(odd[rows:]))
        second = jnp.where(low_block, swap_halves(even[rows:]), odd[rows:])
        gq_ref[:BLOCK, lanes] = first.astype(jnp.bfloat16)
        gq_ref[BLOCK:, lanes] = second.astype(jnp.bfloat16)


def attend_kernel(alone, scale, table_ref, *rest):
    if alone:
        in_refs = dict(zip(PARTNERS_IN, rest[:HEADS]))
        out_refs = dict(zip(PARTNERS_BACK, rest[HEADS:]))
        out_refs[6], out_refs[7] = out_refs[6].at[0], out_refs[6].at[1]
        sent_ref, gq_ref, acc_ref = rest[HEADS + len(PARTNERS_BACK) :]
        place = lax.rem(lax.axis_index("seq"), HEADS)
        for m in range(HEADS):
            sent_ref[lax.bitwise_xor(place, m)] = in_refs[m][...]
    else:
        sent_ref, pool_ref, gq_ref, acc_ref = rest
    tiles = sent_ref.shape[0]
    blocks = 2 * tiles
    queries = 2 * BLOCK
    low = low_lanes((BLOCK, queries))
    zero = jnp.zeros((BLOCK, LANES), jnp.bfloat16)
    fixed = blocks * RAND
    acc_ref[...] = jnp.zeros_like(acc_ref)

    def pooled(entry):
        if alone:
            return sent_ref[entry // 2, 0, entry % 2]
        return pool_ref[entry]

    def chosen(tile):
        first = 2 * tile
        pairs = [(first, first), (first + 1, first + 1)]
        for slot in range(GLOBAL):
            entry = table_ref[fixed + slot] if alone else blocks + 2 + slot
            pairs.append((entry, entry))
        before, after = first - 1, first + 2
        if alone:
            before, after = max(before, 0), min(after, blocks - 1)
        else:
            before = before if tile > 0 else blocks
            after = after if tile < tiles - 1 else blocks + 1
        pairs.append((before, after))
        for slot in range(RAND):
            picked = []
            for block in (first, first + 1):
                pick = table_ref[block * RAND + slot]
                if alone:
                    behind = block + blocks - (slot + 1) * blocks // 4 - pick
                    picked.append(lax.rem(behind, blocks))
                else:
                    base = blocks + 2 + GLOBAL + slot * (blocks + 1)
                    picked.append(base + block + 1 - pick)
            pairs.append(tuple(picked))
        return pairs

    def multiply(tile):
        pairs = chosen(tile)
        keys = jnp.concatenate(
            [jnp.concatenate([pooled(a), pooled(b)], axis=1) for a, b in pairs], axis=0
        )
        first, second = sent_ref[tile, 1, 0], sent_ref[tile, 1, 1]
        rows = [
            [jnp.where(low, first * scale, zero), zero],
            [zero, jnp.where(low, second * scale, zero)],
            [jnp.where(low, zero, first), zero],
            [zero, jnp.where(low, zero, second)],
        ]
        sides = jnp.concatenate([jnp.concatenate(row, axis=1) for row in rows], axis=0)
        products = lax.dot_general(
            keys, sides, (((1,), (1,)), ((), ())), preferred_element_type=jnp.float32
        )
        return pairs, keys, sides, products

    def weigh(tile, products):
        scores, grad_probs = products[:, :queries], products[:, queries:]
        edge = (2 + GLOBAL) * BLOCK
        if tile == 0 or tile == tiles - 1:
            if tile == 0:
                keep = jnp.logical_not(low)
                if not alone:
                    keep = jnp.logical_or(keep, table_ref[fixed + GLOBAL] > 0)
            else:
                keep = low
                if not alone:
                    last = table_ref[fixed + GLOBAL + 1] - 1
                    keep = jnp.logical_or(keep, table_ref[fixed + GLOBAL] < last)
            masked = jnp.where(keep, scores[edge : edge + BLOCK], MASKED)
            scores = jnp.concatenate([scores[:edge], masked, scores[edge + BLOCK :]], axis=0)
        row_max = jnp.max(scores, axis=0, keepdims=True)
        expo = jnp.exp(scores - row_max)
        row_total = jnp.sum(expo, axis=0, keepdims=True)
        probs = expo * (1.0 / row_total)
        probs_half = probs.astype(jnp.bfloat16)
        row_dot = jnp.sum(probs_half.astype(jnp.float32) * grad_probs, axis=0, keepdims=True)
        grad_half = (probs * (grad_probs - row_dot)).astype(jnp.bfloat16)
        return grad_half, probs_half

    def gather(tile, pairs, keys, sides, grad_half, probs_half):
        both = jnp.concatenate([grad_half, probs_half], axis=1)
        key_grads = jnp.dot(both, sides, preferred_element_type=jnp.float32)
        grad_query = lax.dot_general(
            grad_half, keys, (((0,), (0,)), ((), ())), preferred_element_type=jnp.float32
        )
        grad_query = grad_query * scale
        folded = jnp.where(
            low, grad_query[:BLOCK, :LANES], swap_halves(grad_query[BLOCK:, LANES:])
        ).astype(jnp.bfloat16)
        gq_ref[tile] = folded
        for place, (a, b) in enumerate(pairs):
            part = key_grads[place * BLOCK : (place + 1) * BLOCK]
            if place < 2 + GLOBAL:
                acc_ref[a] += part[:, :LANES] + part[:, LANES:]
            else:
                acc_ref[a] += part[:, :LANES]
                acc_ref[b] += part[:, LANES:]

    ahead, weighed = {}, {}
    for step in range(tiles + 2):
        if step < tiles:
            ahead[step] = multiply(step)
        if 0 <= step - 1 < tiles:
            weighed[step - 1] = weigh(step - 1, ahead[step - 1][-1])
        if step >= 2:
            pairs, keys, sides, _ = ahead.pop(step - 2)
            gather(step - 2, pairs, keys, sides, *weighed.pop(step - 2))
    if alone:
        for m in range(HEADS):
            tile = lax.bitwise_xor(place, m)
            for half in range(2):
                grads = acc_ref[2 * tile + half].astype(jnp.bfloat16)
                out_refs[m][half * BLOCK : (half + 1) * BLOCK] = grads
            out_refs[m][queries:] = gq_ref[tile]


def send(part, m):
    return lax.ppermute(part, "seq", [(i, i ^ m) for i in range(lax.axis_size("seq"))])


def second_kernel(got_ref, out_ref):
    out_ref[...] = got_ref[1]


def send_back(back):
    got = [back[0]] + [send(part, m) for part, m in zip(back[1:], PARTNERS_BACK[1:])]
    vmem = pl.BlockSpec(memory_space=pltpu.VMEM)
    relayed = pl.pallas_call(
        second_kernel,
        out_shape=jax.ShapeDtypeStruct(back[0].shape, back[0].dtype),
        in_specs=[vmem],
        out_specs=vmem,
        compiler_params=pltpu.CompilerParams(vmem_limit_bytes=8 * 2**20),
        name="second",
    )(got[PARTNERS_BACK.index(6)])
    return got + [send(relayed, 1)]


def moved(block, ranges, distance, ways, wrap=True):
    route = []
    for source in range(ranges):
        target = source + distance
        if wrap:
            target %= ranges
        if 0 <= target < ranges:
            route += [(source * ways + head, target * ways + head) for head in range(ways)]
    return lax.ppermute(block, "seq", route)


def on_device(queries, key_vectors, value_vectors, output_grad, rand_pick, global_ids):
    group = lax.axis_size("seq")
    rows, width = queries.shape
    ways = HEADS
    ranges = group // ways
    assert group % ways == 0 and (ranges == 1 or ranges % 4 == 0)
    alone = ranges == 1
    blocks = ways * rows // BLOCK
    scale = 1.0 / math.sqrt(width // HEADS)
    vmem = pl.BlockSpec(memory_space=pltpu.VMEM)
    smem = pl.BlockSpec(memory_space=pltpu.SMEM)
    half_type = jnp.bfloat16

    anywhere = pl.BlockSpec(memory_space=pl.ANY)
    packed = pl.pallas_call(
        pack_kernel,
        out_shape=[jax.ShapeDtypeStruct((2, rows, LANES), half_type)] * HEADS,
        in_specs=[anywhere] * 4,
        out_specs=[vmem] * HEADS,
        scratch_shapes=[
            pltpu.VMEM((HEADS // 2, 4, rows, LANES), half_type),
            pltpu.SemaphoreType.DMA((HEADS // 2, 4)),
        ],
        compiler_params=pltpu.CompilerParams(vmem_limit_bytes=PACK_GRANT),
        name="pack",
    )(queries, key_vectors, value_vectors, output_grad)
    sent = list(packed)
    for m in PARTNERS_IN[1:]:
        sent[m] = send(packed[m], m)
    sent = [part.reshape(2, 2, BLOCK, LANES) for part in sent]

    kernel = functools.partial(attend_kernel, alone, scale)
    back_shape = (rows + BLOCK, LANES)
    if alone:
        back_shapes = [(2, *back_shape) if m == 6 else back_shape for m in PARTNERS_BACK]
        back = pl.pallas_call(
            kernel,
            out_shape=[jax.ShapeDtypeStruct(shape, half_type) for shape in back_shapes],
            in_specs=[smem] + [vmem] * HEADS,
            out_specs=[vmem] * len(back_shapes),
            scratch_shapes=[
                pltpu.VMEM((ways, 2, 2, BLOCK, LANES), half_type),
                pltpu.VMEM((ways, BLOCK, LANES), half_type),
                pltpu.VMEM((blocks, BLOCK, LANES), jnp.float32),
            ],
            compiler_params=pltpu.CompilerParams(vmem_limit_bytes=24 * 2**20),
            name="attend",
        )(jnp.concatenate([rand_pick.reshape(-1), global_ids]), *[sent[m] for m in PARTNERS_IN])
    else:
        back = spread_out(kernel, sent, rand_pick, global_ids, ways, ranges, blocks)
    received = send_back(back)
    return pl.pallas_call(
        unpack_kernel,
        out_shape=[jax.ShapeDtypeStruct((rows, width), half_type)] * 3,
        in_specs=[vmem] * len(received),
        out_specs=[vmem] * 3,
        compiler_params=pltpu.CompilerParams(vmem_limit_bytes=8 * 2**20),
        name="unpack",
    )(*received)


def spread_out(kernel, sent, rand_pick, global_ids, ways, ranges, blocks):
    vmem = pl.BlockSpec(memory_space=pltpu.VMEM)
    smem = pl.BlockSpec(memory_space=pltpu.SMEM)
    mine = lax.axis_index("seq") // ways
    order = lax.bitwise_xor(lax.axis_index("seq") % ways, jnp.arange(ways, dtype=jnp.int32))
    sent = jnp.take(jnp.stack(sent), order, axis=0)
    own = sent[:, 0].reshape(blocks, BLOCK, LANES)
    lags = [(slot + 1) * ranges // 4 for slot in range(RAND)]
    heads = [[r * ways + head for r in range(ranges)] for head in range(ways)]
    roots = global_ids // blocks
    offsets = global_ids % blocks
    pool = [own, moved(own[-1:], ranges, 1, ways, False), moved(own[:1], ranges, -1, ways, False)]
    chosen = jnp.where((roots == mine)[:, None, None], jnp.take(own, offsets, axis=0), 0)
    pool.append(lax.psum(chosen.astype(own.dtype), "seq", axis_index_groups=heads))
    for lag in lags:
        pool.append(moved(own[-1:], ranges, lag + 1, ways))
        pool.append(moved(own, ranges, lag, ways))
    pool = jnp.concatenate(pool, axis=0)
    picks = lax.dynamic_slice_in_dim(rand_pick, mine * blocks, blocks, 0)
    where = jnp.stack([mine, jnp.int32(ranges)]).astype(jnp.int32)
    table = jnp.concatenate([picks.reshape(-1), global_ids, where])
    grad_query, totals = pl.pallas_call(
        kernel,
        out_shape=[
            jax.ShapeDtypeStruct((ways, BLOCK, LANES), jnp.bfloat16),
            jax.ShapeDtypeStruct(pool.shape, jnp.float32),
        ],
        in_specs=[smem, vmem, vmem],
        out_specs=[vmem] * 2,
        compiler_params=pltpu.CompilerParams(vmem_limit_bytes=24 * 2**20),
        name="attend",
    )(table, sent, pool)
    total = totals[:blocks]
    total = total.at[-1].add(moved(totals[blocks], ranges, -1, ways, False))
    total = total.at[0].add(moved(totals[blocks + 1], ranges, 1, ways, False))
    base = blocks + 2
    summed = lax.psum(totals[base : base + GLOBAL], "seq", axis_index_groups=heads)
    for slot in range(GLOBAL):
        owned = jnp.where(roots[slot] == mine, summed[slot], 0.0)
        total = total.at[offsets[slot]].add(owned)
    base += GLOBAL
    for lag in lags:
        total = total.at[-1].add(moved(totals[base], ranges, -lag - 1, ways))
        total = total + moved(totals[base + 1 : base + 1 + blocks], ranges, -lag, ways)
        base += blocks + 1
    grads = total.astype(jnp.bfloat16).reshape(ways, 2 * BLOCK, LANES)
    back = jnp.take(jnp.concatenate([grads, grad_query], axis=1), order, axis=0)
    return [back[6:] if m == 6 else back[m] for m in PARTNERS_BACK]


def solution(mesh):
    whole = P(("doc", "seq"), None)
    return jax.shard_map(
        on_device,
        mesh=mesh,
        in_specs=(whole, whole, whole, whole, P("doc", None), P("doc")),
        out_specs=(whole, whole, whole),
        check_vma=False,
    )
```

```python
import functools
import math

import jax
import jax.numpy as jnp
from jax import lax
from jax.experimental import pallas as pl
from jax.experimental.pallas import tpu as pltpu
from jax.sharding import PartitionSpec as P

HEADS = 8
BLOCK = 64
RAND = 3
GLOBAL = 2
HEAD = 64
LANES = 2 * HEAD
PARTNERS_IN = (0, 4, 6, 3, 7, 5, 2, 1)
PARTNERS_BACK = (0, 6, 5, 7, 3, 4, 2, 1)
NEAR = (2, 3, 1, 0)
PACK_GRANT = 427 * 2**17
MASKED = -1e30


def low_lanes(shape):
    return lax.broadcasted_iota(jnp.int32, shape, len(shape) - 1) < HEAD


def swap_halves(block):
    return pltpu.roll(block, HEAD, 1)


def pack_kernel(*refs):
    in_refs, out_refs = refs[:4], refs[4 : 4 + HEADS]
    held_ref, in_sems = refs[4 + HEADS :]
    rows = held_ref.shape[2]
    low = low_lanes((rows, LANES))
    place = lax.rem(lax.axis_index("seq"), HEADS)
    odd_place = lax.rem(place, 2) == 1
    arriving = {}
    for near in NEAR:
        pair = lax.bitwise_xor(place // 2, near)
        lanes = pl.ds(pl.multiple_of(pair * LANES, LANES), LANES)
        for kind, ref in enumerate(in_refs):
            arriving[near, kind] = pltpu.make_async_copy(
                ref.at[:, lanes], held_ref.at[near, kind], in_sems.at[near, kind]
            )
            arriving[near, kind].start()
    for near in NEAR:
        for kind in range(4):
            arriving[near, kind].wait()
        q, k, v, g = [held_ref[near, kind].astype(jnp.float32) for kind in range(4)]
        for kind, (first, second) in enumerate(((k, v), (q, g))):
            even = jnp.where(low, first, swap_halves(second))
            odd = jnp.where(low, swap_halves(first), second)
            same = jnp.where(odd_place, odd, even).astype(jnp.bfloat16)
            other = jnp.where(odd_place, even, odd).astype(jnp.bfloat16)
            out_refs[2 * near][kind] = same
            out_refs[2 * near + 1][kind] = other


def unpack_kernel(*refs):
    in_refs = dict(zip(PARTNERS_BACK, refs[:HEADS]))
    gq_ref, gk_ref, gv_ref = refs[HEADS:]
    rows = gq_ref.shape[0]
    low = low_lanes((rows, LANES))
    low_block = low_lanes((BLOCK, LANES))
    place = lax.rem(lax.axis_index("seq"), HEADS)
    odd_place = lax.rem(place, 2) == 1
    for near in range(HEADS // 2):
        pair = lax.bitwise_xor(place // 2, near)
        lanes = pl.ds(pl.multiple_of(pair * LANES, LANES), LANES)
        same = in_refs[2 * near][...].astype(jnp.float32)
        other = in_refs[2 * near + 1][...].astype(jnp.float32)
        even = jnp.where(odd_place, other, same)
        odd = jnp.where(odd_place, same, other)
        gk = jnp.where(low, even[:rows], swap_halves(odd[:rows]))
        gv = jnp.where(low, swap_halves(even[:rows]), odd[:rows])
        gk_ref[:, lanes] = gk.astype(jnp.bfloat16)
        gv_ref[:, lanes] = gv.astype(jnp.bfloat16)
        first = jnp.where(low_block, even[rows:], swap_halves(odd[rows:]))
        second = jnp.where(low_block, swap_halves(even[rows:]), odd[rows:])
        gq_ref[:BLOCK, lanes] = first.astype(jnp.bfloat16)
        gq_ref[BLOCK:, lanes] = second.astype(jnp.bfloat16)


def attend_kernel(alone, scale, ints_ref, *rest):
    if alone:
        in_refs = dict(zip(PARTNERS_IN, rest[:HEADS]))
        out_refs = rest[HEADS : 2 * HEADS]
        sent_ref, pool_ref, gq_ref, acc_ref, swapped_ref, table_ref, sem = rest[2 * HEADS :]
    else:
        sent_ref, pool_ref, gq_ref, acc_ref, swapped_ref, table_ref, sem = rest
    fetch = pltpu.make_async_copy(ints_ref, table_ref, sem)
    fetch.start()
    if alone:
        place = lax.rem(lax.axis_index("seq"), HEADS)
        for m in range(HEADS):
            tile = lax.bitwise_xor(place, m)
            sent_ref[tile] = in_refs[m][1]
            for half in range(2):
                pool_ref[2 * tile + half] = in_refs[m][0, half]
    for entry in range(pool_ref.shape[0]):
        swapped = swap_halves(pool_ref[entry].astype(jnp.float32))
        swapped_ref[entry] = swapped.astype(jnp.bfloat16)
    tiles = sent_ref.shape[0]
    blocks = 2 * tiles
    queries = 2 * BLOCK
    low = low_lanes((BLOCK, queries))
    zero = jnp.zeros((BLOCK, LANES), jnp.bfloat16)
    fixed = blocks * RAND
    acc_ref[...] = jnp.zeros_like(acc_ref)
    fetch.wait()

    def chosen(tile):
        first = 2 * tile
        pairs = [(first, first), (first + 1, first + 1)]
        for slot in range(GLOBAL):
            entry = table_ref[fixed + slot] if alone else blocks + 2 + slot
            pairs.append((entry, entry))
        before, after = first - 1, first + 2
        if alone:
            before, after = max(before, 0), min(after, blocks - 1)
        else:
            before = before if tile > 0 else blocks
            after = after if tile < tiles - 1 else blocks + 1
        pairs.append((before, after))
        for slot in range(RAND):
            picked = []
            for block in (first, first + 1):
                pick = table_ref[block * RAND + slot]
                if alone:
                    behind = block + blocks - (slot + 1) * blocks // 4 - pick
                    picked.append(lax.rem(behind, blocks))
                else:
                    base = blocks + 2 + GLOBAL + slot * (blocks + 1)
                    picked.append(base + block + 1 - pick)
            pairs.append(tuple(picked))
        return pairs

    def multiply(tile):
        pairs = chosen(tile)
        keys = jnp.concatenate(
            [jnp.concatenate([pool_ref[a], pool_ref[b]], axis=1) for a, b in pairs], axis=0
        )
        first, second = sent_ref[tile, 0], sent_ref[tile, 1]
        rows = [
            [jnp.where(low, first * scale, zero), zero],
            [zero, jnp.where(low, second * scale, zero)],
            [jnp.where(low, zero, first), zero],
            [zero, jnp.where(low, zero, second)],
        ]
        sides = jnp.concatenate([jnp.concatenate(row, axis=1) for row in rows], axis=0)
        products = lax.dot_general(
            keys, sides, (((1,), (1,)), ((), ())), preferred_element_type=jnp.float32
        )
        return pairs, sides, products

    def weigh(tile, products):
        scores, grad_probs = products[:, :queries], products[:, queries:]
        edge = (2 + GLOBAL) * BLOCK
        if tile == 0 or tile == tiles - 1:
            if tile == 0:
                keep = jnp.logical_not(low)
                if not alone:
                    keep = jnp.logical_or(keep, table_ref[fixed + GLOBAL] > 0)
            else:
                keep = low
                if not alone:
                    last = table_ref[fixed + GLOBAL + 1] - 1
                    keep = jnp.logical_or(keep, table_ref[fixed + GLOBAL] < last)
            masked = jnp.where(keep, scores[edge : edge + BLOCK], MASKED)
            scores = jnp.concatenate([scores[:edge], masked, scores[edge + BLOCK :]], axis=0)
        row_max = jnp.max(scores, axis=0, keepdims=True)
        expo = jnp.exp(scores - row_max)
        row_total = jnp.sum(expo, axis=0, keepdims=True)
        probs = expo * (1.0 / row_total)
        probs_half = probs.astype(jnp.bfloat16)
        row_dot = jnp.sum(probs_half.astype(jnp.float32) * grad_probs, axis=0, keepdims=True)
        grad_half = (probs * (grad_probs - row_dot)).astype(jnp.bfloat16)
        return grad_half, probs_half

    def gather(tile, pairs, sides, grad_half, probs_half):
        both = jnp.concatenate([grad_half, probs_half], axis=1)
        key_grads = jnp.dot(both, sides, preferred_element_type=jnp.float32)
        keys = jnp.concatenate(
            [jnp.where(low, pool_ref[a], swapped_ref[b]) for a, b in pairs], axis=0
        )
        grad_query = lax.dot_general(
            grad_half, keys, (((0,), (0,)), ((), ())), preferred_element_type=jnp.float32
        )
        grad_query = grad_query * scale
        folded = jnp.where(low, grad_query[:BLOCK], grad_query[BLOCK:])
        gq_ref[tile] = folded.astype(jnp.bfloat16)
        for place, (a, b) in enumerate(pairs):
            part = key_grads[place * BLOCK : (place + 1) * BLOCK]
            if place < 2 + GLOBAL:
                acc_ref[a] += part[:, :LANES] + part[:, LANES:]
            else:
                acc_ref[a] += part[:, :LANES]
                acc_ref[b] += part[:, LANES:]

    ahead, weighed = {}, {}
    for step in range(tiles + 2):
        if step < tiles:
            ahead[step] = multiply(step)
        if 0 <= step - 1 < tiles:
            weighed[step - 1] = weigh(step - 1, ahead[step - 1][-1])
        if step >= 2:
            pairs, sides, _ = ahead.pop(step - 2)
            gather(step - 2, pairs, sides, *weighed.pop(step - 2))
    if alone:
        for m in range(HEADS):
            tile = lax.bitwise_xor(place, m)
            for half in range(2):
                grads = acc_ref[2 * tile + half].astype(jnp.bfloat16)
                out_refs[m][half * BLOCK : (half + 1) * BLOCK] = grads
            out_refs[m][queries:] = gq_ref[tile]


def exchange(parts, partners):
    group = lax.axis_size("seq")
    arrived = list(parts)
    for m in partners[1:]:
        route = [(i, i ^ m) for i in range(group)]
        arrived[m] = lax.ppermute(parts[m], "seq", route)
    return arrived


def moved(block, ranges, distance, ways, wrap=True):
    route = []
    for source in range(ranges):
        target = source + distance
        if wrap:
            target %= ranges
        if 0 <= target < ranges:
            route += [(source * ways + head, target * ways + head) for head in range(ways)]
    return lax.ppermute(block, "seq", route)


def on_device(queries, key_vectors, value_vectors, output_grad, rand_pick, global_ids):
    group = lax.axis_size("seq")
    rows, width = queries.shape
    ways = HEADS
    ranges = group // ways
    assert group % ways == 0 and (ranges == 1 or ranges % 4 == 0)
    alone = ranges == 1
    blocks = ways * rows // BLOCK
    scale = 1.0 / math.sqrt(width // HEADS)
    vmem = pl.BlockSpec(memory_space=pltpu.VMEM)
    half_type = jnp.bfloat16

    anywhere = pl.BlockSpec(memory_space=pl.ANY)
    packed = pl.pallas_call(
        pack_kernel,
        out_shape=[jax.ShapeDtypeStruct((2, rows, LANES), half_type)] * HEADS,
        in_specs=[anywhere] * 4,
        out_specs=[vmem] * HEADS,
        scratch_shapes=[
            pltpu.VMEM((HEADS // 2, 4, rows, LANES), half_type),
            pltpu.SemaphoreType.DMA((HEADS // 2, 4)),
        ],
        compiler_params=pltpu.CompilerParams(vmem_limit_bytes=PACK_GRANT),
        name="pack",
    )(queries, key_vectors, value_vectors, output_grad)
    sent = [part.reshape(2, 2, BLOCK, LANES) for part in exchange(packed, PARTNERS_IN)]

    kernel = functools.partial(attend_kernel, alone, scale)
    if alone:
        back = pl.pallas_call(
            kernel,
            out_shape=[jax.ShapeDtypeStruct((rows + BLOCK, LANES), half_type)] * HEADS,
            in_specs=[anywhere] + [vmem] * HEADS,
            out_specs=[vmem] * HEADS,
            scratch_shapes=[
                pltpu.VMEM((ways, 2, BLOCK, LANES), half_type),
                pltpu.VMEM((blocks, BLOCK, LANES), half_type),
                pltpu.VMEM((ways, BLOCK, LANES), half_type),
                pltpu.VMEM((blocks, BLOCK, LANES), jnp.float32),
                pltpu.VMEM((blocks, BLOCK, LANES), half_type),
                pltpu.SMEM((blocks * RAND + GLOBAL,), jnp.int32),
                pltpu.SemaphoreType.DMA,
            ],
            compiler_params=pltpu.CompilerParams(vmem_limit_bytes=24 * 2**20),
            name="attend",
        )(jnp.concatenate([rand_pick.reshape(-1), global_ids]), *[sent[m] for m in PARTNERS_IN])
    else:
        back = spread_out(kernel, sent, rand_pick, global_ids, ways, ranges, blocks)
    received = exchange(back, PARTNERS_BACK)
    return pl.pallas_call(
        unpack_kernel,
        out_shape=[jax.ShapeDtypeStruct((rows, width), half_type)] * 3,
        in_specs=[vmem] * HEADS,
        out_specs=[vmem] * 3,
        compiler_params=pltpu.CompilerParams(vmem_limit_bytes=8 * 2**20),
        name="unpack",
    )(*[received[m] for m in PARTNERS_BACK])


def spread_out(kernel, sent, rand_pick, global_ids, ways, ranges, blocks):
    vmem = pl.BlockSpec(memory_space=pltpu.VMEM)
    mine = lax.axis_index("seq") // ways
    order = lax.bitwise_xor(lax.axis_index("seq") % ways, jnp.arange(ways, dtype=jnp.int32))
    sent = jnp.take(jnp.stack(sent), order, axis=0)
    own = sent[:, 0].reshape(blocks, BLOCK, LANES)
    lags = [(slot + 1) * ranges // 4 for slot in range(RAND)]
    heads = [[r * ways + head for r in range(ranges)] for head in range(ways)]
    roots = global_ids // blocks
    offsets = global_ids % blocks
    pool = [own, moved(own[-1:], ranges, 1, ways, False), moved(own[:1], ranges, -1, ways, False)]
    chosen = jnp.where((roots == mine)[:, None, None], jnp.take(own, offsets, axis=0), 0)
    pool.append(lax.psum(chosen.astype(own.dtype), "seq", axis_index_groups=heads))
    for lag in lags:
        pool.append(moved(own[-1:], ranges, lag + 1, ways))
        pool.append(moved(own, ranges, lag, ways))
    pool = jnp.concatenate(pool, axis=0)
    picks = lax.dynamic_slice_in_dim(rand_pick, mine * blocks, blocks, 0)
    where = jnp.stack([mine, jnp.int32(ranges)]).astype(jnp.int32)
    table = jnp.concatenate([picks.reshape(-1), global_ids, where])
    grad_query, totals = pl.pallas_call(
        kernel,
        out_shape=[
            jax.ShapeDtypeStruct((ways, BLOCK, LANES), jnp.bfloat16),
            jax.ShapeDtypeStruct(pool.shape, jnp.float32),
        ],
        in_specs=[pl.BlockSpec(memory_space=pl.ANY), vmem, vmem],
        out_specs=[vmem] * 2,
        scratch_shapes=[
            pltpu.VMEM(pool.shape, pool.dtype),
            pltpu.SMEM(table.shape, jnp.int32),
            pltpu.SemaphoreType.DMA,
        ],
        compiler_params=pltpu.CompilerParams(vmem_limit_bytes=24 * 2**20),
        name="attend",
    )(table, sent[:, 1], pool)
    total = totals[:blocks]
    total = total.at[-1].add(moved(totals[blocks], ranges, -1, ways, False))
    total = total.at[0].add(moved(totals[blocks + 1], ranges, 1, ways, False))
    base = blocks + 2
    summed = lax.psum(totals[base : base + GLOBAL], "seq", axis_index_groups=heads)
    for slot in range(GLOBAL):
        owned = jnp.where(roots[slot] == mine, summed[slot], 0.0)
        total = total.at[offsets[slot]].add(owned)
    base += GLOBAL
    for lag in lags:
        total = total.at[-1].add(moved(totals[base], ranges, -lag - 1, ways))
        total = total + moved(totals[base + 1 : base + 1 + blocks], ranges, -lag, ways)
        base += blocks + 1
    grads = total.astype(jnp.bfloat16).reshape(ways, 2 * BLOCK, LANES)
    back = jnp.take(jnp.concatenate([grads, grad_query], axis=1), order, axis=0)
    return [back[m] for m in range(ways)]


def solution(mesh):
    whole = P(("doc", "seq"), None)
    return jax.shard_map(
        on_device,
        mesh=mesh,
        in_specs=(whole, whole, whole, whole, P("doc", None), P("doc")),
        out_specs=(whole, whole, whole),
        check_vma=False,
    )
```

```python
import functools
import math

import jax
import jax.numpy as jnp
from jax import lax
from jax.experimental import pallas as pl
from jax.experimental.pallas import tpu as pltpu
from jax.sharding import PartitionSpec as P

HEADS = 8
BLOCK = 64
RAND = 3
GLOBAL = 2
HEAD = 64
LANES = 2 * HEAD
PARTNERS_IN = (0, 4, 6, 3, 7, 5, 2, 1)
PARTNERS_BACK = (0, 6, 5, 7, 3, 4, 2, 1)
NEAR = (2, 3, 1, 0)
PACK_GRANT = 427 * 2**17
MASKED = -1e30


def low_lanes(shape):
    return lax.broadcasted_iota(jnp.int32, shape, len(shape) - 1) < HEAD


def swap_halves(block):
    return pltpu.roll(block, HEAD, 1)


def pack_kernel(*refs):
    in_refs, out_refs = refs[:4], refs[4 : 4 + HEADS]
    held_ref, in_sems = refs[4 + HEADS :]
    rows = held_ref.shape[2]
    low = low_lanes((rows, LANES))
    place = lax.rem(lax.axis_index("seq"), HEADS)
    odd_place = lax.rem(place, 2) == 1
    arriving = {}
    for near in NEAR:
        pair = lax.bitwise_xor(place // 2, near)
        lanes = pl.ds(pl.multiple_of(pair * LANES, LANES), LANES)
        for kind, ref in enumerate(in_refs):
            arriving[near, kind] = pltpu.make_async_copy(
                ref.at[:, lanes], held_ref.at[near, kind], in_sems.at[near, kind]
            )
            arriving[near, kind].start()
    for near in NEAR:
        for kind in range(4):
            arriving[near, kind].wait()
        q, k, v, g = [held_ref[near, kind].astype(jnp.float32) for kind in range(4)]
        for kind, (first, second) in enumerate(((k, v), (q, g))):
            even = jnp.where(low, first, swap_halves(second))
            odd = jnp.where(low, swap_halves(first), second)
            same = jnp.where(odd_place, odd, even).astype(jnp.bfloat16)
            other = jnp.where(odd_place, even, odd).astype(jnp.bfloat16)
            out_refs[2 * near][kind] = same
            out_refs[2 * near + 1][kind] = other


def unpack_kernel(*refs):
    in_refs = dict(zip(PARTNERS_BACK, refs[:HEADS]))
    gq_ref, gk_ref, gv_ref = refs[HEADS:]
    rows = gq_ref.shape[0]
    low = low_lanes((rows, LANES))
    low_block = low_lanes((BLOCK, LANES))
    place = lax.rem(lax.axis_index("seq"), HEADS)
    odd_place = lax.rem(place, 2) == 1
    for near in range(HEADS // 2):
        pair = lax.bitwise_xor(place // 2, near)
        lanes = pl.ds(pl.multiple_of(pair * LANES, LANES), LANES)
        same = in_refs[2 * near][...].astype(jnp.float32)
        other = in_refs[2 * near + 1][...].astype(jnp.float32)
        even = jnp.where(odd_place, other, same)
        odd = jnp.where(odd_place, same, other)
        gk = jnp.where(low, even[:rows], swap_halves(odd[:rows]))
        gv = jnp.where(low, swap_halves(even[:rows]), odd[:rows])
        gk_ref[:, lanes] = gk.astype(jnp.bfloat16)
        gv_ref[:, lanes] = gv.astype(jnp.bfloat16)
        first = jnp.where(low_block, even[rows:], swap_halves(odd[rows:]))
        second = jnp.where(low_block, swap_halves(even[rows:]), odd[rows:])
        gq_ref[:BLOCK, lanes] = first.astype(jnp.bfloat16)
        gq_ref[BLOCK:, lanes] = second.astype(jnp.bfloat16)


def attend_kernel(alone, scale, ints_ref, *rest):
    if alone:
        in_refs = dict(zip(PARTNERS_IN, rest[:HEADS]))
        out_refs = rest[HEADS : 2 * HEADS]
        sent_ref, gq_ref, acc_ref, table_ref, sem = rest[2 * HEADS :]
    else:
        sent_ref, pool_ref, gq_ref, acc_ref, table_ref, sem = rest
    fetch = pltpu.make_async_copy(ints_ref, table_ref, sem)
    fetch.start()
    if alone:
        place = lax.rem(lax.axis_index("seq"), HEADS)
        for m in range(HEADS):
            sent_ref[lax.bitwise_xor(place, m)] = in_refs[m][...]
    tiles = sent_ref.shape[0]
    blocks = 2 * tiles
    queries = 2 * BLOCK
    low = low_lanes((BLOCK, queries))
    zero = jnp.zeros((BLOCK, LANES), jnp.bfloat16)
    fixed = blocks * RAND
    acc_ref[...] = jnp.zeros_like(acc_ref)
    fetch.wait()

    def pooled(entry):
        if alone:
            return sent_ref[entry // 2, 0, entry % 2]
        return pool_ref[entry]

    def chosen(tile):
        first = 2 * tile
        pairs = [(first, first), (first + 1, first + 1)]
        for slot in range(GLOBAL):
            entry = table_ref[fixed + slot] if alone else blocks + 2 + slot
            pairs.append((entry, entry))
        before, after = first - 1, first + 2
        if alone:
            before, after = max(before, 0), min(after, blocks - 1)
        else:
            before = before if tile > 0 else blocks
            after = after if tile < tiles - 1 else blocks + 1
        pairs.append((before, after))
        for slot in range(RAND):
            picked = []
            for block in (first, first + 1):
                pick = table_ref[block * RAND + slot]
                if alone:
                    behind = block + blocks - (slot + 1) * blocks // 4 - pick
                    picked.append(lax.rem(behind, blocks))
                else:
                    base = blocks + 2 + GLOBAL + slot * (blocks + 1)
                    picked.append(base + block + 1 - pick)
            pairs.append(tuple(picked))
        return pairs

    def multiply(tile):
        pairs = chosen(tile)
        keys = jnp.concatenate(
            [jnp.concatenate([pooled(a), pooled(b)], axis=1) for a, b in pairs], axis=0
        )
        first, second = sent_ref[tile, 1, 0], sent_ref[tile, 1, 1]
        rows = [
            [jnp.where(low, first * scale, zero), zero],
            [zero, jnp.where(low, second * scale, zero)],
            [jnp.where(low, zero, first), zero],
            [zero, jnp.where(low, zero, second)],
        ]
        sides = jnp.concatenate([jnp.concatenate(row, axis=1) for row in rows], axis=0)
        products = lax.dot_general(
            keys, sides, (((1,), (1,)), ((), ())), preferred_element_type=jnp.float32
        )
        return pairs, keys, sides, products

    def weigh(tile, products):
        scores, grad_probs = products[:, :queries], products[:, queries:]
        edge = (2 + GLOBAL) * BLOCK
        if tile == 0 or tile == tiles - 1:
            if tile == 0:
                keep = jnp.logical_not(low)
                if not alone:
                    keep = jnp.logical_or(keep, table_ref[fixed + GLOBAL] > 0)
            else:
                keep = low
                if not alone:
                    last = table_ref[fixed + GLOBAL + 1] - 1
                    keep = jnp.logical_or(keep, table_ref[fixed + GLOBAL] < last)
            masked = jnp.where(keep, scores[edge : edge + BLOCK], MASKED)
            scores = jnp.concatenate([scores[:edge], masked, scores[edge + BLOCK :]], axis=0)
        row_max = jnp.max(scores, axis=0, keepdims=True)
        expo = jnp.exp(scores - row_max)
        row_total = jnp.sum(expo, axis=0, keepdims=True)
        inverse = 1.0 / row_total
        probs_half = (expo * inverse).astype(jnp.bfloat16)
        row_dot = jnp.sum(probs_half.astype(jnp.float32) * grad_probs, axis=0, keepdims=True)
        grad_half = (expo * ((grad_probs - row_dot) * inverse)).astype(jnp.bfloat16)
        return grad_half, probs_half

    def gather(tile, pairs, keys, sides, grad_half, probs_half):
        both = jnp.concatenate([grad_half, probs_half], axis=1)
        key_grads = jnp.dot(both, sides, preferred_element_type=jnp.float32)
        grad_query = lax.dot_general(
            grad_half, keys, (((0,), (0,)), ((), ())), preferred_element_type=jnp.float32
        )
        grad_query = grad_query * scale
        folded = jnp.where(
            low, grad_query[:BLOCK, :LANES], swap_halves(grad_query[BLOCK:, LANES:])
        ).astype(jnp.bfloat16)
        gq_ref[tile] = folded
        for place, (a, b) in enumerate(pairs):
            part = key_grads[place * BLOCK : (place + 1) * BLOCK]
            if place < 2 + GLOBAL:
                acc_ref[a] += part[:, :LANES] + part[:, LANES:]
            else:
                acc_ref[a] += part[:, :LANES]
                acc_ref[b] += part[:, LANES:]

    ahead, weighed = {}, {}
    for step in range(tiles + 2):
        if step < tiles:
            ahead[step] = multiply(step)
        if 0 <= step - 1 < tiles:
            weighed[step - 1] = weigh(step - 1, ahead[step - 1][-1])
        if step >= 2:
            pairs, keys, sides, _ = ahead.pop(step - 2)
            gather(step - 2, pairs, keys, sides, *weighed.pop(step - 2))
    if alone:
        for m in range(HEADS):
            tile = lax.bitwise_xor(place, m)
            for half in range(2):
                grads = acc_ref[2 * tile + half].astype(jnp.bfloat16)
                out_refs[m][half * BLOCK : (half + 1) * BLOCK] = grads
            out_refs[m][queries:] = gq_ref[tile]


def exchange(parts, partners):
    group = lax.axis_size("seq")
    arrived = list(parts)
    for m in partners[1:]:
        route = [(i, i ^ m) for i in range(group)]
        arrived[m] = lax.ppermute(parts[m], "seq", route)
    return arrived


def moved(block, ranges, distance, ways, wrap=True):
    route = []
    for source in range(ranges):
        target = source + distance
        if wrap:
            target %= ranges
        if 0 <= target < ranges:
            route += [(source * ways + head, target * ways + head) for head in range(ways)]
    return lax.ppermute(block, "seq", route)


def on_device(queries, key_vectors, value_vectors, output_grad, rand_pick, global_ids):
    group = lax.axis_size("seq")
    rows, width = queries.shape
    ways = HEADS
    ranges = group // ways
    assert group % ways == 0 and (ranges == 1 or ranges % 4 == 0)
    alone = ranges == 1
    blocks = ways * rows // BLOCK
    scale = 1.0 / math.sqrt(width // HEADS)
    vmem = pl.BlockSpec(memory_space=pltpu.VMEM)
    half_type = jnp.bfloat16

    anywhere = pl.BlockSpec(memory_space=pl.ANY)
    packed = pl.pallas_call(
        pack_kernel,
        out_shape=[jax.ShapeDtypeStruct((2, rows, LANES), half_type)] * HEADS,
        in_specs=[anywhere] * 4,
        out_specs=[vmem] * HEADS,
        scratch_shapes=[
            pltpu.VMEM((HEADS // 2, 4, rows, LANES), half_type),
            pltpu.SemaphoreType.DMA((HEADS // 2, 4)),
        ],
        compiler_params=pltpu.CompilerParams(vmem_limit_bytes=PACK_GRANT),
        name="pack",
    )(queries, key_vectors, value_vectors, output_grad)
    sent = [part.reshape(2, 2, BLOCK, LANES) for part in exchange(packed, PARTNERS_IN)]

    kernel = functools.partial(attend_kernel, alone, scale)
    if alone:
        back = pl.pallas_call(
            kernel,
            out_shape=[jax.ShapeDtypeStruct((rows + BLOCK, LANES), half_type)] * HEADS,
            in_specs=[anywhere] + [vmem] * HEADS,
            out_specs=[vmem] * HEADS,
            scratch_shapes=[
                pltpu.VMEM((ways, 2, 2, BLOCK, LANES), half_type),
                pltpu.VMEM((ways, BLOCK, LANES), half_type),
                pltpu.VMEM((blocks, BLOCK, LANES), jnp.float32),
                pltpu.SMEM((blocks * RAND + GLOBAL,), jnp.int32),
                pltpu.SemaphoreType.DMA,
            ],
            compiler_params=pltpu.CompilerParams(vmem_limit_bytes=24 * 2**20),
            name="attend",
        )(jnp.concatenate([rand_pick.reshape(-1), global_ids]), *[sent[m] for m in PARTNERS_IN])
    else:
        back = spread_out(kernel, sent, rand_pick, global_ids, ways, ranges, blocks)
    received = exchange(back, PARTNERS_BACK)
    return pl.pallas_call(
        unpack_kernel,
        out_shape=[jax.ShapeDtypeStruct((rows, width), half_type)] * 3,
        in_specs=[vmem] * HEADS,
        out_specs=[vmem] * 3,
        compiler_params=pltpu.CompilerParams(vmem_limit_bytes=8 * 2**20),
        name="unpack",
    )(*[received[m] for m in PARTNERS_BACK])


def spread_out(kernel, sent, rand_pick, global_ids, ways, ranges, blocks):
    vmem = pl.BlockSpec(memory_space=pltpu.VMEM)
    mine = lax.axis_index("seq") // ways
    order = lax.bitwise_xor(lax.axis_index("seq") % ways, jnp.arange(ways, dtype=jnp.int32))
    sent = jnp.take(jnp.stack(sent), order, axis=0)
    own = sent[:, 0].reshape(blocks, BLOCK, LANES)
    lags = [(slot + 1) * ranges // 4 for slot in range(RAND)]
    heads = [[r * ways + head for r in range(ranges)] for head in range(ways)]
    roots = global_ids // blocks
    offsets = global_ids % blocks
    pool = [own, moved(own[-1:], ranges, 1, ways, False), moved(own[:1], ranges, -1, ways, False)]
    chosen = jnp.where((roots == mine)[:, None, None], jnp.take(own, offsets, axis=0), 0)
    pool.append(lax.psum(chosen.astype(own.dtype), "seq", axis_index_groups=heads))
    for lag in lags:
        pool.append(moved(own[-1:], ranges, lag + 1, ways))
        pool.append(moved(own, ranges, lag, ways))
    pool = jnp.concatenate(pool, axis=0)
    picks = lax.dynamic_slice_in_dim(rand_pick, mine * blocks, blocks, 0)
    where = jnp.stack([mine, jnp.int32(ranges)]).astype(jnp.int32)
    table = jnp.concatenate([picks.reshape(-1), global_ids, where])
    grad_query, totals = pl.pallas_call(
        kernel,
        out_shape=[
            jax.ShapeDtypeStruct((ways, BLOCK, LANES), jnp.bfloat16),
            jax.ShapeDtypeStruct(pool.shape, jnp.float32),
        ],
        in_specs=[pl.BlockSpec(memory_space=pl.ANY), vmem, vmem],
        out_specs=[vmem] * 2,
        scratch_shapes=[pltpu.SMEM(table.shape, jnp.int32), pltpu.SemaphoreType.DMA],
        compiler_params=pltpu.CompilerParams(vmem_limit_bytes=24 * 2**20),
        name="attend",
    )(table, sent, pool)
    total = totals[:blocks]
    total = total.at[-1].add(moved(totals[blocks], ranges, -1, ways, False))
    total = total.at[0].add(moved(totals[blocks + 1], ranges, 1, ways, False))
    base = blocks + 2
    summed = lax.psum(totals[base : base + GLOBAL], "seq", axis_index_groups=heads)
    for slot in range(GLOBAL):
        owned = jnp.where(roots[slot] == mine, summed[slot], 0.0)
        total = total.at[offsets[slot]].add(owned)
    base += GLOBAL
    for lag in lags:
        total = total.at[-1].add(moved(totals[base], ranges, -lag - 1, ways))
        total = total + moved(totals[base + 1 : base + 1 + blocks], ranges, -lag, ways)
        base += blocks + 1
    grads = total.astype(jnp.bfloat16).reshape(ways, 2 * BLOCK, LANES)
    back = jnp.take(jnp.concatenate([grads, grad_query], axis=1), order, axis=0)
    return [back[m] for m in range(ways)]


def solution(mesh):
    whole = P(("doc", "seq"), None)
    return jax.shard_map(
        on_device,
        mesh=mesh,
        in_specs=(whole, whole, whole, whole, P("doc", None), P("doc")),
        out_specs=(whole, whole, whole),
        check_vma=False,
    )
```

```python
import functools
import math

import jax
import jax.numpy as jnp
from jax import lax
from jax.experimental import pallas as pl
from jax.experimental.pallas import tpu as pltpu
from jax.sharding import PartitionSpec as P

HEADS = 8
BLOCK = 64
RAND = 3
GLOBAL = 2
HEAD = 64
LANES = 2 * HEAD
PARTNERS_IN = (0, 4, 6, 3, 7, 5, 2, 1)
PARTNERS_BACK = (0, 6, 5, 7, 3, 4, 2, 1)
NEAR = (2, 3, 1, 0)
PACK_GRANT = 427 * 2**17
MASKED = -1e30


def low_lanes(shape):
    return lax.broadcasted_iota(jnp.int32, shape, len(shape) - 1) < HEAD


def swap_halves(block):
    return pltpu.roll(block, HEAD, 1)


def pack_kernel(*refs):
    in_refs, out_refs = refs[:4], refs[4 : 4 + HEADS]
    held_ref, in_sems = refs[4 + HEADS :]
    rows = held_ref.shape[2]
    low = low_lanes((rows, LANES))
    place = lax.rem(lax.axis_index("seq"), HEADS)
    odd_place = lax.rem(place, 2) == 1
    arriving = {}
    for near in NEAR:
        pair = lax.bitwise_xor(place // 2, near)
        lanes = pl.ds(pl.multiple_of(pair * LANES, LANES), LANES)
        for kind, ref in enumerate(in_refs):
            arriving[near, kind] = pltpu.make_async_copy(
                ref.at[:, lanes], held_ref.at[near, kind], in_sems.at[near, kind]
            )
            arriving[near, kind].start()
    for near in NEAR:
        for kind in range(4):
            arriving[near, kind].wait()
        q, k, v, g = [held_ref[near, kind].astype(jnp.float32) for kind in range(4)]
        for kind, (first, second) in enumerate(((k, v), (q, g))):
            even = jnp.where(low, first, swap_halves(second))
            odd = jnp.where(low, swap_halves(first), second)
            same = jnp.where(odd_place, odd, even).astype(jnp.bfloat16)
            other = jnp.where(odd_place, even, odd).astype(jnp.bfloat16)
            out_refs[2 * near][kind] = same
            out_refs[2 * near + 1][kind] = other


def unpack_kernel(*refs):
    in_refs = dict(zip(PARTNERS_BACK, refs[:HEADS]))
    gq_ref, gk_ref, gv_ref = refs[HEADS:]
    rows = gq_ref.shape[0]
    low = low_lanes((rows, LANES))
    place = lax.rem(lax.axis_index("seq"), HEADS)
    odd_place = lax.rem(place, 2) == 1
    for near in range(HEADS // 2):
        pair = lax.bitwise_xor(place // 2, near)
        lanes = pl.ds(pl.multiple_of(pair * LANES, LANES), LANES)
        same = in_refs[2 * near][...].astype(jnp.float32)
        other = in_refs[2 * near + 1][...].astype(jnp.float32)
        even = jnp.where(odd_place, other, same)
        odd = jnp.where(odd_place, same, other)
        gk = jnp.where(low, even[:rows], swap_halves(odd[:rows]))
        gv = jnp.where(low, swap_halves(even[:rows]), odd[:rows])
        gk_ref[:, lanes] = gk.astype(jnp.bfloat16)
        gv_ref[:, lanes] = gv.astype(jnp.bfloat16)
        gq = jnp.concatenate([even[rows:], odd[rows:]], axis=0).T
        gq_ref[:, lanes] = gq.astype(jnp.bfloat16)


def attend_kernel(alone, scale, ints_ref, *rest):
    if alone:
        in_refs = dict(zip(PARTNERS_IN, rest[:HEADS]))
        out_refs = rest[HEADS : 2 * HEADS]
        sent_ref, gq_ref, acc_ref, turned_ref, table_ref, sem = rest[2 * HEADS :]
    else:
        sent_ref, pool_ref, gq_ref, acc_ref, turned_ref, table_ref, sem = rest
    fetch = pltpu.make_async_copy(ints_ref, table_ref, sem)
    fetch.start()
    if alone:
        place = lax.rem(lax.axis_index("seq"), HEADS)
        for m in range(HEADS):
            sent_ref[lax.bitwise_xor(place, m)] = in_refs[m][...]
    tiles = sent_ref.shape[0]
    blocks = 2 * tiles
    queries = 2 * BLOCK
    low = low_lanes((BLOCK, queries))
    zero = jnp.zeros((BLOCK, LANES), jnp.bfloat16)
    fixed = blocks * RAND
    acc_ref[...] = jnp.zeros_like(acc_ref)

    def pooled(entry):
        if alone:
            return sent_ref[entry // 2, 0, entry % 2]
        return pool_ref[entry]

    entries = acc_ref.shape[0]
    for entry in range(0, entries, 2):
        after = min(entry + 1, entries - 1)
        two = jnp.concatenate([pooled(entry), pooled(after)], axis=0).astype(jnp.float32)
        keys = two.T[:HEAD]
        swapped = swap_halves(keys)
        turned_ref[entry] = jnp.where(low, keys, swapped).astype(jnp.bfloat16)
        turned_ref[after] = jnp.where(low, swapped, keys).astype(jnp.bfloat16)
    fetch.wait()

    def chosen(tile):
        first = 2 * tile
        pairs = [(first, first), (first + 1, first + 1)]
        for slot in range(GLOBAL):
            entry = table_ref[fixed + slot] if alone else blocks + 2 + slot
            pairs.append((entry, entry))
        before, after = first - 1, first + 2
        if alone:
            before, after = max(before, 0), min(after, blocks - 1)
        else:
            before = before if tile > 0 else blocks
            after = after if tile < tiles - 1 else blocks + 1
        pairs.append((before, after))
        for slot in range(RAND):
            picked = []
            for block in (first, first + 1):
                pick = table_ref[block * RAND + slot]
                if alone:
                    behind = block + blocks - (slot + 1) * blocks // 4 - pick
                    picked.append(lax.rem(behind, blocks))
                else:
                    base = blocks + 2 + GLOBAL + slot * (blocks + 1)
                    picked.append(base + block + 1 - pick)
            pairs.append(tuple(picked))
        return pairs

    def multiply(tile):
        pairs = chosen(tile)
        keys = jnp.concatenate(
            [jnp.concatenate([pooled(a), pooled(b)], axis=1) for a, b in pairs], axis=0
        )
        first, second = sent_ref[tile, 1, 0], sent_ref[tile, 1, 1]
        rows = [
            [jnp.where(low, first * scale, zero), zero],
            [zero, jnp.where(low, second * scale, zero)],
            [jnp.where(low, zero, first), zero],
            [zero, jnp.where(low, zero, second)],
        ]
        sides = jnp.concatenate([jnp.concatenate(row, axis=1) for row in rows], axis=0)
        turned = jnp.concatenate([first, second], axis=0).astype(jnp.float32).T
        turned = turned.astype(jnp.bfloat16)
        above, below = turned[:HEAD] * scale, turned[HEAD:]
        rows = [
            [jnp.where(low, above, zero), zero],
            [zero, jnp.where(low, below, zero)],
            [jnp.where(low, zero, above), zero],
            [zero, jnp.where(low, zero, below)],
        ]
        turned = jnp.concatenate([jnp.concatenate(row, axis=1) for row in rows], axis=0)
        products = jnp.dot(keys, turned, preferred_element_type=jnp.float32)
        return pairs, sides, products

    def weigh(tile, products):
        scores, grad_probs = products[:, :queries], products[:, queries:]
        edge = (2 + GLOBAL) * BLOCK
        if tile == 0 or tile == tiles - 1:
            if tile == 0:
                keep = jnp.logical_not(low)
                if not alone:
                    keep = jnp.logical_or(keep, table_ref[fixed + GLOBAL] > 0)
            else:
                keep = low
                if not alone:
                    last = table_ref[fixed + GLOBAL + 1] - 1
                    keep = jnp.logical_or(keep, table_ref[fixed + GLOBAL] < last)
            masked = jnp.where(keep, scores[edge : edge + BLOCK], MASKED)
            scores = jnp.concatenate([scores[:edge], masked, scores[edge + BLOCK :]], axis=0)
        row_max = jnp.max(scores, axis=0, keepdims=True)
        expo = jnp.exp(scores - row_max)
        row_total = jnp.sum(expo, axis=0, keepdims=True)
        inverse = 1.0 / row_total
        probs_half = (expo * inverse).astype(jnp.bfloat16)
        row_dot = jnp.sum(probs_half.astype(jnp.float32) * grad_probs, axis=0, keepdims=True)
        grad_half = (expo * ((grad_probs - row_dot) * inverse)).astype(jnp.bfloat16)
        return grad_half, probs_half

    def gather(tile, pairs, sides, grad_half, probs_half):
        both = jnp.concatenate([grad_half, probs_half], axis=1)
        key_grads = jnp.dot(both, sides, preferred_element_type=jnp.float32)
        turned = []
        for side in range(2):
            halves = [turned_ref[pair[side]] for pair in pairs]
            whole = [jnp.where(low, halves[i], halves[i + 1]) for i in range(0, len(pairs), 2)]
            turned.append(jnp.concatenate(whole, axis=1))
        grad_query = jnp.dot(
            jnp.concatenate(turned, axis=0), grad_half, preferred_element_type=jnp.float32
        )
        grad_query = jnp.where(low, grad_query[:HEAD], grad_query[HEAD:]) * scale
        gq_ref[tile] = grad_query.astype(jnp.bfloat16)
        for place, (a, b) in enumerate(pairs):
            part = key_grads[place * BLOCK : (place + 1) * BLOCK]
            if place < 2 + GLOBAL:
                acc_ref[a] += part[:, :LANES] + part[:, LANES:]
            else:
                acc_ref[a] += part[:, :LANES]
                acc_ref[b] += part[:, LANES:]

    ahead, weighed = {}, {}
    for step in range(tiles + 2):
        if step < tiles:
            ahead[step] = multiply(step)
        if 0 <= step - 1 < tiles:
            weighed[step - 1] = weigh(step - 1, ahead[step - 1][-1])
        if step >= 2:
            pairs, sides, _ = ahead.pop(step - 2)
            gather(step - 2, pairs, sides, *weighed.pop(step - 2))
    if alone:
        for m in range(HEADS):
            tile = lax.bitwise_xor(place, m)
            for half in range(2):
                grads = acc_ref[2 * tile + half].astype(jnp.bfloat16)
                out_refs[m][half * BLOCK : (half + 1) * BLOCK] = grads
            out_refs[m][queries:] = gq_ref[tile]


def exchange(parts, partners):
    group = lax.axis_size("seq")
    arrived = list(parts)
    for m in partners[1:]:
        route = [(i, i ^ m) for i in range(group)]
        arrived[m] = lax.ppermute(parts[m], "seq", route)
    return arrived


def moved(block, ranges, distance, ways, wrap=True):
    route = []
    for source in range(ranges):
        target = source + distance
        if wrap:
            target %= ranges
        if 0 <= target < ranges:
            route += [(source * ways + head, target * ways + head) for head in range(ways)]
    return lax.ppermute(block, "seq", route)


def on_device(queries, key_vectors, value_vectors, output_grad, rand_pick, global_ids):
    group = lax.axis_size("seq")
    rows, width = queries.shape
    ways = HEADS
    ranges = group // ways
    assert group % ways == 0 and (ranges == 1 or ranges % 4 == 0)
    alone = ranges == 1
    blocks = ways * rows // BLOCK
    scale = 1.0 / math.sqrt(width // HEADS)
    vmem = pl.BlockSpec(memory_space=pltpu.VMEM)
    half_type = jnp.bfloat16

    anywhere = pl.BlockSpec(memory_space=pl.ANY)
    packed = pl.pallas_call(
        pack_kernel,
        out_shape=[jax.ShapeDtypeStruct((2, rows, LANES), half_type)] * HEADS,
        in_specs=[anywhere] * 4,
        out_specs=[vmem] * HEADS,
        scratch_shapes=[
            pltpu.VMEM((HEADS // 2, 4, rows, LANES), half_type),
            pltpu.SemaphoreType.DMA((HEADS // 2, 4)),
        ],
        compiler_params=pltpu.CompilerParams(vmem_limit_bytes=PACK_GRANT),
        name="pack",
    )(queries, key_vectors, value_vectors, output_grad)
    sent = [part.reshape(2, 2, BLOCK, LANES) for part in exchange(packed, PARTNERS_IN)]

    kernel = functools.partial(attend_kernel, alone, scale)
    if alone:
        back = pl.pallas_call(
            kernel,
            out_shape=[jax.ShapeDtypeStruct((rows + BLOCK, LANES), half_type)] * HEADS,
            in_specs=[anywhere] + [vmem] * HEADS,
            out_specs=[vmem] * HEADS,
            scratch_shapes=[
                pltpu.VMEM((ways, 2, 2, BLOCK, LANES), half_type),
                pltpu.VMEM((ways, BLOCK, LANES), half_type),
                pltpu.VMEM((blocks, BLOCK, LANES), jnp.float32),
                pltpu.VMEM((blocks, HEAD, LANES), half_type),
                pltpu.SMEM((blocks * RAND + GLOBAL,), jnp.int32),
                pltpu.SemaphoreType.DMA,
            ],
            compiler_params=pltpu.CompilerParams(vmem_limit_bytes=24 * 2**20),
            name="attend",
        )(jnp.concatenate([rand_pick.reshape(-1), global_ids]), *[sent[m] for m in PARTNERS_IN])
    else:
        back = spread_out(kernel, sent, rand_pick, global_ids, ways, ranges, blocks)
    received = exchange(back, PARTNERS_BACK)
    return pl.pallas_call(
        unpack_kernel,
        out_shape=[jax.ShapeDtypeStruct((rows, width), half_type)] * 3,
        in_specs=[vmem] * HEADS,
        out_specs=[vmem] * 3,
        compiler_params=pltpu.CompilerParams(vmem_limit_bytes=8 * 2**20),
        name="unpack",
    )(*[received[m] for m in PARTNERS_BACK])


def spread_out(kernel, sent, rand_pick, global_ids, ways, ranges, blocks):
    vmem = pl.BlockSpec(memory_space=pltpu.VMEM)
    mine = lax.axis_index("seq") // ways
    order = lax.bitwise_xor(lax.axis_index("seq") % ways, jnp.arange(ways, dtype=jnp.int32))
    sent = jnp.take(jnp.stack(sent), order, axis=0)
    own = sent[:, 0].reshape(blocks, BLOCK, LANES)
    lags = [(slot + 1) * ranges // 4 for slot in range(RAND)]
    heads = [[r * ways + head for r in range(ranges)] for head in range(ways)]
    roots = global_ids // blocks
    offsets = global_ids % blocks
    pool = [own, moved(own[-1:], ranges, 1, ways, False), moved(own[:1], ranges, -1, ways, False)]
    chosen = jnp.where((roots == mine)[:, None, None], jnp.take(own, offsets, axis=0), 0)
    pool.append(lax.psum(chosen.astype(own.dtype), "seq", axis_index_groups=heads))
    for lag in lags:
        pool.append(moved(own[-1:], ranges, lag + 1, ways))
        pool.append(moved(own, ranges, lag, ways))
    pool = jnp.concatenate(pool, axis=0)
    picks = lax.dynamic_slice_in_dim(rand_pick, mine * blocks, blocks, 0)
    where = jnp.stack([mine, jnp.int32(ranges)]).astype(jnp.int32)
    table = jnp.concatenate([picks.reshape(-1), global_ids, where])
    grad_query, totals = pl.pallas_call(
        kernel,
        out_shape=[
            jax.ShapeDtypeStruct((ways, BLOCK, LANES), jnp.bfloat16),
            jax.ShapeDtypeStruct(pool.shape, jnp.float32),
        ],
        in_specs=[pl.BlockSpec(memory_space=pl.ANY), vmem, vmem],
        out_specs=[vmem] * 2,
        scratch_shapes=[
            pltpu.VMEM((pool.shape[0], HEAD, LANES), pool.dtype),
            pltpu.SMEM(table.shape, jnp.int32),
            pltpu.SemaphoreType.DMA,
        ],
        compiler_params=pltpu.CompilerParams(vmem_limit_bytes=24 * 2**20),
        name="attend",
    )(table, sent, pool)
    total = totals[:blocks]
    total = total.at[-1].add(moved(totals[blocks], ranges, -1, ways, False))
    total = total.at[0].add(moved(totals[blocks + 1], ranges, 1, ways, False))
    base = blocks + 2
    summed = lax.psum(totals[base : base + GLOBAL], "seq", axis_index_groups=heads)
    for slot in range(GLOBAL):
        owned = jnp.where(roots[slot] == mine, summed[slot], 0.0)
        total = total.at[offsets[slot]].add(owned)
    base += GLOBAL
    for lag in lags:
        total = total.at[-1].add(moved(totals[base], ranges, -lag - 1, ways))
        total = total + moved(totals[base + 1 : base + 1 + blocks], ranges, -lag, ways)
        base += blocks + 1
    grads = total.astype(jnp.bfloat16).reshape(ways, 2 * BLOCK, LANES)
    back = jnp.take(jnp.concatenate([grads, grad_query], axis=1), order, axis=0)
    return [back[m] for m in range(ways)]


def solution(mesh):
    whole = P(("doc", "seq"), None)
    return jax.shard_map(
        on_device,
        mesh=mesh,
        in_specs=(whole, whole, whole, whole, P("doc", None), P("doc")),
        out_specs=(whole, whole, whole),
        check_vma=False,
    )
```

```python
import functools
import math

import jax
import jax.numpy as jnp
from jax import lax
from jax.experimental import pallas as pl
from jax.experimental.pallas import tpu as pltpu
from jax.sharding import PartitionSpec as P

HEADS = 8
BLOCK = 64
RAND = 3
GLOBAL = 2
HEAD = 64
LANES = 2 * HEAD
PARTNERS_IN = (0, 4, 6, 3, 7, 5, 2, 1)
PARTNERS_BACK = (0, 6, 5, 7, 3, 4, 2, 1)
PACK_GRANT = 427 * 2**17
MASKED = -1e30


def low_lanes(shape):
    return lax.broadcasted_iota(jnp.int32, shape, len(shape) - 1) < HEAD


def swap_halves(block):
    return pltpu.roll(block, HEAD, 1)


def pack_kernel(*refs):
    in_refs, out_refs = refs[:4], refs[4 : 4 + HEADS]
    held_ref, in_sems = refs[4 + HEADS :]
    copies = [pltpu.make_async_copy(in_refs[i], held_ref.at[i], in_sems.at[i]) for i in range(4)]
    for copy in copies:
        copy.start()
    rows = held_ref.shape[1]
    low = low_lanes((rows, LANES))
    place = lax.rem(lax.axis_index("seq"), HEADS)
    odd_place = lax.rem(place, 2) == 1
    for copy in copies:
        copy.wait()
    for near in range(HEADS // 2):
        pair = lax.bitwise_xor(place // 2, near)
        lanes = pl.ds(pl.multiple_of(pair * LANES, LANES), LANES)
        q, k, v, g = [held_ref[i, :, lanes].astype(jnp.float32) for i in range(4)]
        for kind, (first, second) in enumerate(((k, v), (q, g))):
            even = jnp.where(low, first, swap_halves(second))
            odd = jnp.where(low, swap_halves(first), second)
            same = jnp.where(odd_place, odd, even).astype(jnp.bfloat16)
            other = jnp.where(odd_place, even, odd).astype(jnp.bfloat16)
            out_refs[2 * near][kind] = same
            out_refs[2 * near + 1][kind] = other


def unpack_kernel(*refs):
    in_refs = dict(zip(PARTNERS_BACK, refs[:HEADS]))
    out_refs, held_ref, sems = refs[HEADS : HEADS + 3], refs[-2], refs[-1]
    rows = held_ref.shape[1]
    low = low_lanes((rows, LANES))
    low_block = low_lanes((BLOCK, LANES))
    place = lax.rem(lax.axis_index("seq"), HEADS)
    odd_place = lax.rem(place, 2) == 1
    copies = [pltpu.make_async_copy(held_ref.at[i], out_refs[i], sems.at[i]) for i in range(3)]
    for kind in (1, 2, 0):
        for near in range(HEADS // 2):
            pair = lax.bitwise_xor(place // 2, near)
            lanes = pl.ds(pl.multiple_of(pair * LANES, LANES), LANES)
            part = slice(rows, rows + BLOCK) if kind == 0 else slice(0, rows)
            same = in_refs[2 * near][part].astype(jnp.float32)
            other = in_refs[2 * near + 1][part].astype(jnp.float32)
            even = jnp.where(odd_place, other, same)
            odd = jnp.where(odd_place, same, other)
            if kind == 1:
                whole = jnp.where(low, even, swap_halves(odd))
            elif kind == 2:
                whole = jnp.where(low, swap_halves(even), odd)
            else:
                first = jnp.where(low_block, even, swap_halves(odd))
                second = jnp.where(low_block, swap_halves(even), odd)
                whole = jnp.concatenate([first, second], axis=0)
            held_ref[kind, :, lanes] = whole.astype(jnp.bfloat16)
        copies[kind].start()
    for copy in copies:
        copy.wait()


def attend_kernel(alone, scale, ints_ref, *rest):
    if alone:
        in_refs = dict(zip(PARTNERS_IN, rest[:HEADS]))
        out_refs = rest[HEADS : 2 * HEADS]
        sent_ref, gq_ref, acc_ref, *rest = rest[2 * HEADS :]
    else:
        sent_ref, pool_ref, gq_ref, acc_ref, *rest = rest
    global_ref, global_acc_ref, table_ref, sem = rest
    fetch = pltpu.make_async_copy(ints_ref, table_ref, sem)
    fetch.start()
    if alone:
        place = lax.rem(lax.axis_index("seq"), HEADS)
        for m in range(HEADS):
            sent_ref[lax.bitwise_xor(place, m)] = in_refs[m][...]
    tiles = sent_ref.shape[0]
    blocks = 2 * tiles
    queries = 2 * BLOCK
    low = low_lanes((BLOCK, queries))
    zero = jnp.zeros((BLOCK, LANES), jnp.bfloat16)
    fixed = blocks * RAND
    acc_ref[...] = jnp.zeros_like(acc_ref)
    fetch.wait()

    def pooled(entry):
        if alone:
            return sent_ref[entry // 2, 0, entry % 2]
        return pool_ref[entry]

    for slot in range(GLOBAL):
        entry = table_ref[fixed + slot] if alone else blocks + 2 + slot
        global_ref[slot] = pooled(entry)
        global_acc_ref[slot] = jnp.zeros((BLOCK, LANES), jnp.float32)

    def window(tile):
        first = 2 * tile
        before, after = first - 1, first + 2
        if alone:
            return first, first + 1, max(before, 0), min(after, blocks - 1)
        before = before if tile > 0 else blocks
        after = after if tile < tiles - 1 else blocks + 1
        return first, first + 1, before, after

    def random(block, slot):
        if alone:
            here = (block - (slot + 1) * blocks // 4) % blocks
            back = (here - 1) % blocks
        else:
            back = blocks + 2 + GLOBAL + slot * (blocks + 1) + block
            here = back + 1
        return here, back, table_ref[block * RAND + slot] == 1

    def drawn(block, slot):
        here, back, picked = random(block, slot)
        return jnp.where(picked, pooled(back), pooled(here))

    def multiply(tile):
        one, two, before, after = window(tile)
        pairs = [(pooled(one), pooled(one)), (pooled(two), pooled(two))]
        pairs += [(global_ref[slot], global_ref[slot]) for slot in range(GLOBAL)]
        pairs.append((pooled(before), pooled(after)))
        pairs += [(drawn(one, slot), drawn(two, slot)) for slot in range(RAND)]
        keys = jnp.concatenate([jnp.concatenate(pair, axis=1) for pair in pairs], axis=0)
        first, second = sent_ref[tile, 1, 0], sent_ref[tile, 1, 1]
        rows = [
            [jnp.where(low, first * scale, zero), zero],
            [zero, jnp.where(low, second * scale, zero)],
            [jnp.where(low, zero, first), zero],
            [zero, jnp.where(low, zero, second)],
        ]
        sides = jnp.concatenate([jnp.concatenate(row, axis=1) for row in rows], axis=0)
        products = lax.dot_general(
            keys, sides, (((1,), (1,)), ((), ())), preferred_element_type=jnp.float32
        )
        return keys, sides, products

    def weigh(tile, products):
        scores, grad_probs = products[:, :queries], products[:, queries:]
        edge = (2 + GLOBAL) * BLOCK
        if tile == 0 or tile == tiles - 1:
            if tile == 0:
                keep = jnp.logical_not(low)
                if not alone:
                    keep = jnp.logical_or(keep, table_ref[fixed + GLOBAL] > 0)
            else:
                keep = low
                if not alone:
                    last = table_ref[fixed + GLOBAL + 1] - 1
                    keep = jnp.logical_or(keep, table_ref[fixed + GLOBAL] < last)
            masked = jnp.where(keep, scores[edge : edge + BLOCK], MASKED)
            scores = jnp.concatenate([scores[:edge], masked, scores[edge + BLOCK :]], axis=0)
        row_max = jnp.max(scores, axis=0, keepdims=True)
        expo = jnp.exp(scores - row_max)
        row_total = jnp.sum(expo, axis=0, keepdims=True)
        inverse = 1.0 / row_total
        probs_half = (expo * inverse).astype(jnp.bfloat16)
        row_dot = jnp.sum(probs_half.astype(jnp.float32) * grad_probs, axis=0, keepdims=True)
        grad_half = (expo * ((grad_probs - row_dot) * inverse)).astype(jnp.bfloat16)
        return grad_half, probs_half

    def gather(tile, keys, sides, grad_half, probs_half):
        both = jnp.concatenate([grad_half, probs_half], axis=1)
        key_grads = jnp.dot(both, sides, preferred_element_type=jnp.float32)
        grad_query = lax.dot_general(
            grad_half, keys, (((0,), (0,)), ((), ())), preferred_element_type=jnp.float32
        )
        grad_query = grad_query * scale
        folded = jnp.where(
            low, grad_query[:BLOCK, :LANES], swap_halves(grad_query[BLOCK:, LANES:])
        ).astype(jnp.bfloat16)
        gq_ref[tile] = folded
        parts = [key_grads[i * BLOCK : (i + 1) * BLOCK] for i in range(3 + GLOBAL + RAND)]
        one, two, before, after = window(tile)
        acc_ref[one] += parts[0][:, :LANES] + parts[0][:, LANES:]
        acc_ref[two] += parts[1][:, :LANES] + parts[1][:, LANES:]
        for slot in range(GLOBAL):
            part = parts[2 + slot]
            global_acc_ref[slot] += part[:, :LANES] + part[:, LANES:]
        acc_ref[before] += parts[2 + GLOBAL][:, :LANES]
        acc_ref[after] += parts[2 + GLOBAL][:, LANES:]
        for slot in range(RAND):
            part = parts[3 + GLOBAL + slot]
            for side, block in enumerate((one, two)):
                here, back, picked = random(block, slot)
                mine = part[:, side * LANES : (side + 1) * LANES]
                acc_ref[back] += jnp.where(picked, mine, 0.0)
                acc_ref[here] += jnp.where(picked, 0.0, mine)

    ahead, weighed = {}, {}
    for step in range(tiles + 2):
        if step < tiles:
            ahead[step] = multiply(step)
        if 0 <= step - 1 < tiles:
            weighed[step - 1] = weigh(step - 1, ahead[step - 1][-1])
        if step >= 2:
            keys, sides, _ = ahead.pop(step - 2)
            gather(step - 2, keys, sides, *weighed.pop(step - 2))
    for slot in range(GLOBAL):
        entry = table_ref[fixed + slot] if alone else blocks + 2 + slot
        acc_ref[entry] += global_acc_ref[slot]
    if alone:
        for m in range(HEADS):
            tile = lax.bitwise_xor(place, m)
            for half in range(2):
                grads = acc_ref[2 * tile + half].astype(jnp.bfloat16)
                out_refs[m][half * BLOCK : (half + 1) * BLOCK] = grads
            out_refs[m][queries:] = gq_ref[tile]


def exchange(parts, partners):
    group = lax.axis_size("seq")
    arrived = list(parts)
    for m in partners[1:]:
        route = [(i, i ^ m) for i in range(group)]
        arrived[m] = lax.ppermute(parts[m], "seq", route)
    return arrived


def moved(block, ranges, distance, ways, wrap=True):
    route = []
    for source in range(ranges):
        target = source + distance
        if wrap:
            target %= ranges
        if 0 <= target < ranges:
            route += [(source * ways + head, target * ways + head) for head in range(ways)]
    return lax.ppermute(block, "seq", route)


def on_device(queries, key_vectors, value_vectors, output_grad, rand_pick, global_ids):
    group = lax.axis_size("seq")
    rows, width = queries.shape
    ways = HEADS
    ranges = group // ways
    assert group % ways == 0 and (ranges == 1 or ranges % 4 == 0)
    alone = ranges == 1
    blocks = ways * rows // BLOCK
    scale = 1.0 / math.sqrt(width // HEADS)
    vmem = pl.BlockSpec(memory_space=pltpu.VMEM)
    half_type = jnp.bfloat16

    anywhere = pl.BlockSpec(memory_space=pl.ANY)
    packed = pl.pallas_call(
        pack_kernel,
        out_shape=[jax.ShapeDtypeStruct((2, rows, LANES), half_type)] * HEADS,
        in_specs=[anywhere] * 4,
        out_specs=[vmem] * HEADS,
        scratch_shapes=[
            pltpu.VMEM((4, rows, width), half_type),
            pltpu.SemaphoreType.DMA((4,)),
        ],
        compiler_params=pltpu.CompilerParams(vmem_limit_bytes=PACK_GRANT),
        name="pack",
    )(queries, key_vectors, value_vectors, output_grad)
    sent = [part.reshape(2, 2, BLOCK, LANES) for part in exchange(packed, PARTNERS_IN)]

    kernel = functools.partial(attend_kernel, alone, scale)
    if alone:
        back = pl.pallas_call(
            kernel,
            out_shape=[jax.ShapeDtypeStruct((rows + BLOCK, LANES), half_type)] * HEADS,
            in_specs=[anywhere] + [vmem] * HEADS,
            out_specs=[vmem] * HEADS,
            scratch_shapes=[
                pltpu.VMEM((ways, 2, 2, BLOCK, LANES), half_type),
                pltpu.VMEM((ways, BLOCK, LANES), half_type),
                pltpu.VMEM((blocks, BLOCK, LANES), jnp.float32),
                pltpu.VMEM((GLOBAL, BLOCK, LANES), half_type),
                pltpu.VMEM((GLOBAL, BLOCK, LANES), jnp.float32),
                pltpu.SMEM((blocks * RAND + GLOBAL,), jnp.int32),
                pltpu.SemaphoreType.DMA,
            ],
            compiler_params=pltpu.CompilerParams(vmem_limit_bytes=24 * 2**20),
            name="attend",
        )(jnp.concatenate([rand_pick.reshape(-1), global_ids]), *[sent[m] for m in PARTNERS_IN])
    else:
        back = spread_out(kernel, sent, rand_pick, global_ids, ways, ranges, blocks)
    received = exchange(back, PARTNERS_BACK)
    return pl.pallas_call(
        unpack_kernel,
        out_shape=[jax.ShapeDtypeStruct((rows, width), half_type)] * 3,
        in_specs=[vmem] * HEADS,
        out_specs=[anywhere] * 3,
        scratch_shapes=[
            pltpu.VMEM((3, rows, width), half_type),
            pltpu.SemaphoreType.DMA((3,)),
        ],
        compiler_params=pltpu.CompilerParams(vmem_limit_bytes=8 * 2**20),
        name="unpack",
    )(*[received[m] for m in PARTNERS_BACK])


def spread_out(kernel, sent, rand_pick, global_ids, ways, ranges, blocks):
    vmem = pl.BlockSpec(memory_space=pltpu.VMEM)
    mine = lax.axis_index("seq") // ways
    order = lax.bitwise_xor(lax.axis_index("seq") % ways, jnp.arange(ways, dtype=jnp.int32))
    sent = jnp.take(jnp.stack(sent), order, axis=0)
    own = sent[:, 0].reshape(blocks, BLOCK, LANES)
    lags = [(slot + 1) * ranges // 4 for slot in range(RAND)]
    heads = [[r * ways + head for r in range(ranges)] for head in range(ways)]
    roots = global_ids // blocks
    offsets = global_ids % blocks
    pool = [own, moved(own[-1:], ranges, 1, ways, False), moved(own[:1], ranges, -1, ways, False)]
    chosen = jnp.where((roots == mine)[:, None, None], jnp.take(own, offsets, axis=0), 0)
    pool.append(lax.psum(chosen.astype(own.dtype), "seq", axis_index_groups=heads))
    for lag in lags:
        pool.append(moved(own[-1:], ranges, lag + 1, ways))
        pool.append(moved(own, ranges, lag, ways))
    pool = jnp.concatenate(pool, axis=0)
    picks = lax.dynamic_slice_in_dim(rand_pick, mine * blocks, blocks, 0)
    where = jnp.stack([mine, jnp.int32(ranges)]).astype(jnp.int32)
    table = jnp.concatenate([picks.reshape(-1), global_ids, where])
    grad_query, totals = pl.pallas_call(
        kernel,
        out_shape=[
            jax.ShapeDtypeStruct((ways, BLOCK, LANES), jnp.bfloat16),
            jax.ShapeDtypeStruct(pool.shape, jnp.float32),
        ],
        in_specs=[pl.BlockSpec(memory_space=pl.ANY), vmem, vmem],
        out_specs=[vmem] * 2,
        scratch_shapes=[
            pltpu.VMEM((GLOBAL, BLOCK, LANES), pool.dtype),
            pltpu.VMEM((GLOBAL, BLOCK, LANES), jnp.float32),
            pltpu.SMEM(table.shape, jnp.int32),
            pltpu.SemaphoreType.DMA,
        ],
        compiler_params=pltpu.CompilerParams(vmem_limit_bytes=24 * 2**20),
        name="attend",
    )(table, sent, pool)
    total = totals[:blocks]
    total = total.at[-1].add(moved(totals[blocks], ranges, -1, ways, False))
    total = total.at[0].add(moved(totals[blocks + 1], ranges, 1, ways, False))
    base = blocks + 2
    summed = lax.psum(totals[base : base + GLOBAL], "seq", axis_index_groups=heads)
    for slot in range(GLOBAL):
        owned = jnp.where(roots[slot] == mine, summed[slot], 0.0)
        total = total.at[offsets[slot]].add(owned)
    base += GLOBAL
    for lag in lags:
        total = total.at[-1].add(moved(totals[base], ranges, -lag - 1, ways))
        total = total + moved(totals[base + 1 : base + 1 + blocks], ranges, -lag, ways)
        base += blocks + 1
    grads = total.astype(jnp.bfloat16).reshape(ways, 2 * BLOCK, LANES)
    back = jnp.take(jnp.concatenate([grads, grad_query], axis=1), order, axis=0)
    return [back[m] for m in range(ways)]


def solution(mesh):
    whole = P(("doc", "seq"), None)
    return jax.shard_map(
        on_device,
        mesh=mesh,
        in_specs=(whole, whole, whole, whole, P("doc", None), P("doc")),
        out_specs=(whole, whole, whole),
        check_vma=False,
    )
```

```python
import functools
import math

import jax
import jax.numpy as jnp
from jax import lax
from jax.experimental import pallas as pl
from jax.experimental.pallas import tpu as pltpu
from jax.sharding import PartitionSpec as P

HEADS = 8
BLOCK = 64
RAND = 3
GLOBAL = 2
HEAD = 64
LANES = 2 * HEAD
PARTNERS_IN = (0, 4, 6, 3, 7, 5, 2, 1)
PARTNERS_BACK = (0, 6, 5, 7, 3, 4, 2, 1)
PACK_GRANT = 427 * 2**17
MASKED = -1e30


def low_lanes(shape):
    return lax.broadcasted_iota(jnp.int32, shape, len(shape) - 1) < HEAD


def swap_halves(block):
    return pltpu.roll(block, HEAD, 1)


def folded(reduce, rows):
    return reduce(reduce(rows.reshape(-1, BLOCK, rows.shape[1]), axis=0), axis=0, keepdims=True)


def pack_kernel(*refs):
    in_refs, out_refs = refs[:4], refs[4 : 4 + HEADS]
    held_ref, in_sems = refs[4 + HEADS :]
    copies = [pltpu.make_async_copy(in_refs[i], held_ref.at[i], in_sems.at[i]) for i in range(4)]
    for copy in copies:
        copy.start()
    rows = held_ref.shape[1]
    low = low_lanes((rows, LANES))
    place = lax.rem(lax.axis_index("seq"), HEADS)
    odd_place = lax.rem(place, 2) == 1
    for copy in copies:
        copy.wait()
    for near in range(HEADS // 2):
        pair = lax.bitwise_xor(place // 2, near)
        lanes = pl.ds(pl.multiple_of(pair * LANES, LANES), LANES)
        q, k, v, g = [held_ref[i, :, lanes].astype(jnp.float32) for i in range(4)]
        for kind, (first, second) in enumerate(((k, v), (q, g))):
            even = jnp.where(low, first, swap_halves(second))
            odd = jnp.where(low, swap_halves(first), second)
            same = jnp.where(odd_place, odd, even).astype(jnp.bfloat16)
            other = jnp.where(odd_place, even, odd).astype(jnp.bfloat16)
            out_refs[2 * near][kind] = same
            out_refs[2 * near + 1][kind] = other


def unpack_kernel(*refs):
    in_refs = dict(zip(PARTNERS_BACK, refs[:HEADS]))
    out_refs, held_ref, sems = refs[HEADS : HEADS + 3], refs[-2], refs[-1]
    rows = held_ref.shape[1]
    low = low_lanes((rows, LANES))
    low_block = low_lanes((BLOCK, LANES))
    place = lax.rem(lax.axis_index("seq"), HEADS)
    odd_place = lax.rem(place, 2) == 1
    copies = [pltpu.make_async_copy(held_ref.at[i], out_refs[i], sems.at[i]) for i in range(3)]
    for kind in (1, 2, 0):
        for near in range(HEADS // 2):
            pair = lax.bitwise_xor(place // 2, near)
            lanes = pl.ds(pl.multiple_of(pair * LANES, LANES), LANES)
            part = slice(rows, rows + BLOCK) if kind == 0 else slice(0, rows)
            same = in_refs[2 * near][part].astype(jnp.float32)
            other = in_refs[2 * near + 1][part].astype(jnp.float32)
            even = jnp.where(odd_place, other, same)
            odd = jnp.where(odd_place, same, other)
            if kind == 1:
                whole = jnp.where(low, even, swap_halves(odd))
            elif kind == 2:
                whole = jnp.where(low, swap_halves(even), odd)
            else:
                first = jnp.where(low_block, even, swap_halves(odd))
                second = jnp.where(low_block, swap_halves(even), odd)
                whole = jnp.concatenate([first, second], axis=0)
            held_ref[kind, :, lanes] = whole.astype(jnp.bfloat16)
        copies[kind].start()
    for copy in copies:
        copy.wait()


def attend_kernel(alone, scale, ints_ref, *rest):
    if alone:
        in_refs = dict(zip(PARTNERS_IN, rest[:HEADS]))
        out_refs = rest[HEADS : 2 * HEADS]
        sent_ref, gq_ref, acc_ref, table_ref, sem = rest[2 * HEADS :]
    else:
        sent_ref, pool_ref, gq_ref, acc_ref, table_ref, sem = rest
    fetch = pltpu.make_async_copy(ints_ref, table_ref, sem)
    fetch.start()
    if alone:
        place = lax.rem(lax.axis_index("seq"), HEADS)
        for m in range(HEADS):
            sent_ref[lax.bitwise_xor(place, m)] = in_refs[m][...]
    tiles = sent_ref.shape[0]
    blocks = 2 * tiles
    queries = 2 * BLOCK
    low = low_lanes((BLOCK, queries))
    zero = jnp.zeros((BLOCK, LANES), jnp.bfloat16)
    fixed = blocks * RAND
    acc_ref[...] = jnp.zeros_like(acc_ref)
    fetch.wait()

    def pooled(entry):
        if alone:
            return sent_ref[entry // 2, 0, entry % 2]
        return pool_ref[entry]

    def chosen(tile):
        first = 2 * tile
        pairs = [(first, first), (first + 1, first + 1)]
        for slot in range(GLOBAL):
            entry = table_ref[fixed + slot] if alone else blocks + 2 + slot
            pairs.append((entry, entry))
        before, after = first - 1, first + 2
        if alone:
            before, after = max(before, 0), min(after, blocks - 1)
        else:
            before = before if tile > 0 else blocks
            after = after if tile < tiles - 1 else blocks + 1
        pairs.append((before, after))
        for slot in range(RAND):
            picked = []
            for block in (first, first + 1):
                pick = table_ref[block * RAND + slot]
                if alone:
                    behind = block + blocks - (slot + 1) * blocks // 4 - pick
                    picked.append(lax.rem(behind, blocks))
                else:
                    base = blocks + 2 + GLOBAL + slot * (blocks + 1)
                    picked.append(base + block + 1 - pick)
            pairs.append(tuple(picked))
        return pairs

    def multiply(tile):
        pairs = chosen(tile)
        keys = jnp.concatenate(
            [jnp.concatenate([pooled(a), pooled(b)], axis=1) for a, b in pairs], axis=0
        )
        first, second = sent_ref[tile, 1, 0], sent_ref[tile, 1, 1]
        rows = [
            [jnp.where(low, first * scale, zero), zero],
            [zero, jnp.where(low, second * scale, zero)],
            [jnp.where(low, zero, first), zero],
            [zero, jnp.where(low, zero, second)],
        ]
        sides = jnp.concatenate([jnp.concatenate(row, axis=1) for row in rows], axis=0)
        products = lax.dot_general(
            keys, sides, (((1,), (1,)), ((), ())), preferred_element_type=jnp.float32
        )
        return pairs, keys, sides, products

    def weigh(tile, products):
        scores, grad_probs = products[:, :queries], products[:, queries:]
        edge = (2 + GLOBAL) * BLOCK
        if tile == 0 or tile == tiles - 1:
            if tile == 0:
                keep = jnp.logical_not(low)
                if not alone:
                    keep = jnp.logical_or(keep, table_ref[fixed + GLOBAL] > 0)
            else:
                keep = low
                if not alone:
                    last = table_ref[fixed + GLOBAL + 1] - 1
                    keep = jnp.logical_or(keep, table_ref[fixed + GLOBAL] < last)
            masked = jnp.where(keep, scores[edge : edge + BLOCK], MASKED)
            scores = jnp.concatenate([scores[:edge], masked, scores[edge + BLOCK :]], axis=0)
        row_max = folded(jnp.max, scores)
        expo = jnp.exp(scores - row_max)
        row_total = folded(jnp.sum, expo)
        inverse = 1.0 / row_total
        probs_half = (expo * inverse).astype(jnp.bfloat16)
        row_dot = folded(jnp.sum, probs_half.astype(jnp.float32) * grad_probs)
        grad_half = (expo * ((grad_probs - row_dot) * inverse)).astype(jnp.bfloat16)
        return grad_half, probs_half

    def gather(tile, pairs, keys, sides, grad_half, probs_half):
        both = jnp.concatenate([grad_half, probs_half], axis=1)
        key_grads = jnp.dot(both, sides, preferred_element_type=jnp.float32)
        grad_query = lax.dot_general(
            grad_half, keys, (((0,), (0,)), ((), ())), preferred_element_type=jnp.float32
        )
        grad_query = grad_query * scale
        grad_query = jnp.where(
            low, grad_query[:BLOCK, :LANES], swap_halves(grad_query[BLOCK:, LANES:])
        )
        gq_ref[tile] = grad_query.astype(jnp.bfloat16)
        for place, (a, b) in enumerate(pairs):
            part = key_grads[place * BLOCK : (place + 1) * BLOCK]
            if place < 2 + GLOBAL:
                acc_ref[a] += part[:, :LANES] + part[:, LANES:]
            else:
                acc_ref[a] += part[:, :LANES]
                acc_ref[b] += part[:, LANES:]

    ahead, weighed = {}, {}
    for step in range(tiles + 2):
        if step < tiles:
            ahead[step] = multiply(step)
        if 0 <= step - 1 < tiles:
            weighed[step - 1] = weigh(step - 1, ahead[step - 1][-1])
        if step >= 2:
            pairs, keys, sides, _ = ahead.pop(step - 2)
            gather(step - 2, pairs, keys, sides, *weighed.pop(step - 2))
    if alone:
        for m in range(HEADS):
            tile = lax.bitwise_xor(place, m)
            for half in range(2):
                grads = acc_ref[2 * tile + half].astype(jnp.bfloat16)
                out_refs[m][half * BLOCK : (half + 1) * BLOCK] = grads
            out_refs[m][queries:] = gq_ref[tile]


def exchange(parts, partners):
    group = lax.axis_size("seq")
    arrived = list(parts)
    for m in partners[1:]:
        route = [(i, i ^ m) for i in range(group)]
        arrived[m] = lax.ppermute(parts[m], "seq", route)
    return arrived


def moved(block, ranges, distance, ways, wrap=True):
    route = []
    for source in range(ranges):
        target = source + distance
        if wrap:
            target %= ranges
        if 0 <= target < ranges:
            route += [(source * ways + head, target * ways + head) for head in range(ways)]
    return lax.ppermute(block, "seq", route)


def on_device(queries, key_vectors, value_vectors, output_grad, rand_pick, global_ids):
    group = lax.axis_size("seq")
    rows, width = queries.shape
    ways = HEADS
    ranges = group // ways
    assert group % ways == 0 and (ranges == 1 or ranges % 4 == 0)
    alone = ranges == 1
    blocks = ways * rows // BLOCK
    scale = 1.0 / math.sqrt(width // HEADS)
    vmem = pl.BlockSpec(memory_space=pltpu.VMEM)
    half_type = jnp.bfloat16

    anywhere = pl.BlockSpec(memory_space=pl.ANY)
    packed = pl.pallas_call(
        pack_kernel,
        out_shape=[jax.ShapeDtypeStruct((2, rows, LANES), half_type)] * HEADS,
        in_specs=[anywhere] * 4,
        out_specs=[vmem] * HEADS,
        scratch_shapes=[
            pltpu.VMEM((4, rows, width), half_type),
            pltpu.SemaphoreType.DMA((4,)),
        ],
        compiler_params=pltpu.CompilerParams(vmem_limit_bytes=PACK_GRANT),
        name="pack",
    )(queries, key_vectors, value_vectors, output_grad)
    sent = [part.reshape(2, 2, BLOCK, LANES) for part in exchange(packed, PARTNERS_IN)]

    kernel = functools.partial(attend_kernel, alone, scale)
    if alone:
        back = pl.pallas_call(
            kernel,
            out_shape=[jax.ShapeDtypeStruct((rows + BLOCK, LANES), half_type)] * HEADS,
            in_specs=[anywhere] + [vmem] * HEADS,
            out_specs=[vmem] * HEADS,
            scratch_shapes=[
                pltpu.VMEM((ways, 2, 2, BLOCK, LANES), half_type),
                pltpu.VMEM((ways, BLOCK, LANES), half_type),
                pltpu.VMEM((blocks, BLOCK, LANES), jnp.float32),
                pltpu.SMEM((blocks * RAND + GLOBAL,), jnp.int32),
                pltpu.SemaphoreType.DMA,
            ],
            compiler_params=pltpu.CompilerParams(vmem_limit_bytes=24 * 2**20),
            name="attend",
        )(jnp.concatenate([rand_pick.reshape(-1), global_ids]), *[sent[m] for m in PARTNERS_IN])
    else:
        back = spread_out(kernel, sent, rand_pick, global_ids, ways, ranges, blocks)
    received = exchange(back, PARTNERS_BACK)
    return pl.pallas_call(
        unpack_kernel,
        out_shape=[jax.ShapeDtypeStruct((rows, width), half_type)] * 3,
        in_specs=[vmem] * HEADS,
        out_specs=[anywhere] * 3,
        scratch_shapes=[
            pltpu.VMEM((3, rows, width), half_type),
            pltpu.SemaphoreType.DMA((3,)),
        ],
        compiler_params=pltpu.CompilerParams(vmem_limit_bytes=8 * 2**20),
        name="unpack",
    )(*[received[m] for m in PARTNERS_BACK])


def spread_out(kernel, sent, rand_pick, global_ids, ways, ranges, blocks):
    vmem = pl.BlockSpec(memory_space=pltpu.VMEM)
    mine = lax.axis_index("seq") // ways
    order = lax.bitwise_xor(lax.axis_index("seq") % ways, jnp.arange(ways, dtype=jnp.int32))
    sent = jnp.take(jnp.stack(sent), order, axis=0)
    own = sent[:, 0].reshape(blocks, BLOCK, LANES)
    lags = [(slot + 1) * ranges // 4 for slot in range(RAND)]
    heads = [[r * ways + head for r in range(ranges)] for head in range(ways)]
    roots = global_ids // blocks
    offsets = global_ids % blocks
    pool = [own, moved(own[-1:], ranges, 1, ways, False), moved(own[:1], ranges, -1, ways, False)]
    chosen = jnp.where((roots == mine)[:, None, None], jnp.take(own, offsets, axis=0), 0)
    pool.append(lax.psum(chosen.astype(own.dtype), "seq", axis_index_groups=heads))
    for lag in lags:
        pool.append(moved(own[-1:], ranges, lag + 1, ways))
        pool.append(moved(own, ranges, lag, ways))
    pool = jnp.concatenate(pool, axis=0)
    picks = lax.dynamic_slice_in_dim(rand_pick, mine * blocks, blocks, 0)
    where = jnp.stack([mine, jnp.int32(ranges)]).astype(jnp.int32)
    table = jnp.concatenate([picks.reshape(-1), global_ids, where])
    grad_query, totals = pl.pallas_call(
        kernel,
        out_shape=[
            jax.ShapeDtypeStruct((ways, BLOCK, LANES), jnp.bfloat16),
            jax.ShapeDtypeStruct(pool.shape, jnp.float32),
        ],
        in_specs=[pl.BlockSpec(memory_space=pl.ANY), vmem, vmem],
        out_specs=[vmem] * 2,
        scratch_shapes=[
            pltpu.SMEM(table.shape, jnp.int32),
            pltpu.SemaphoreType.DMA,
        ],
        compiler_params=pltpu.CompilerParams(vmem_limit_bytes=24 * 2**20),
        name="attend",
    )(table, sent, pool)
    total = totals[:blocks]
    total = total.at[-1].add(moved(totals[blocks], ranges, -1, ways, False))
    total = total.at[0].add(moved(totals[blocks + 1], ranges, 1, ways, False))
    base = blocks + 2
    summed = lax.psum(totals[base : base + GLOBAL], "seq", axis_index_groups=heads)
    for slot in range(GLOBAL):
        owned = jnp.where(roots[slot] == mine, summed[slot], 0.0)
        total = total.at[offsets[slot]].add(owned)
    base += GLOBAL
    for lag in lags:
        total = total.at[-1].add(moved(totals[base], ranges, -lag - 1, ways))
        total = total + moved(totals[base + 1 : base + 1 + blocks], ranges, -lag, ways)
        base += blocks + 1
    grads = total.astype(jnp.bfloat16).reshape(ways, 2 * BLOCK, LANES)
    back = jnp.take(jnp.concatenate([grads, grad_query], axis=1), order, axis=0)
    return [back[m] for m in range(ways)]


def solution(mesh):
    whole = P(("doc", "seq"), None)
    return jax.shard_map(
        on_device,
        mesh=mesh,
        in_specs=(whole, whole, whole, whole, P("doc", None), P("doc")),
        out_specs=(whole, whole, whole),
        check_vma=False,
    )
```

```python
import functools
import math

import jax
import jax.numpy as jnp
from jax import lax
from jax.experimental import pallas as pl
from jax.experimental.pallas import tpu as pltpu
from jax.sharding import PartitionSpec as P

HEADS = 8
BLOCK = 64
RAND = 3
GLOBAL = 2
HEAD = 64
LANES = 2 * HEAD
PARTNERS_IN = (0, 4, 5, 2, 3, 7, 6, 1)
PARTNERS_BACK = (0, 2, 6, 4, 7, 5, 1, 3)
PACK_GRANT = 427 * 2**17
MASKED = -1e30


def low_lanes(shape):
    return lax.broadcasted_iota(jnp.int32, shape, len(shape) - 1) < HEAD


def swap_halves(block):
    return pltpu.roll(block, HEAD, 1)


def folded(reduce, rows):
    return reduce(reduce(rows.reshape(-1, BLOCK, rows.shape[1]), axis=0), axis=0, keepdims=True)


def pack_kernel(*refs):
    in_refs, out_refs = refs[:4], refs[4 : 4 + HEADS]
    held_ref, in_sems = refs[4 + HEADS :]
    copies = [pltpu.make_async_copy(in_refs[i], held_ref.at[i], in_sems.at[i]) for i in range(4)]
    for copy in copies:
        copy.start()
    rows = held_ref.shape[1]
    low = low_lanes((rows, LANES))
    place = lax.rem(lax.axis_index("seq"), HEADS)
    odd_place = lax.rem(place, 2) == 1
    for copy in copies:
        copy.wait()
    for near in range(HEADS // 2):
        pair = lax.bitwise_xor(place // 2, near)
        lanes = pl.ds(pl.multiple_of(pair * LANES, LANES), LANES)
        q, k, v, g = [held_ref[i, :, lanes].astype(jnp.float32) for i in range(4)]
        for kind, (first, second) in enumerate(((k, v), (q, g))):
            even = jnp.where(low, first, swap_halves(second))
            odd = jnp.where(low, swap_halves(first), second)
            same = jnp.where(odd_place, odd, even).astype(jnp.bfloat16)
            other = jnp.where(odd_place, even, odd).astype(jnp.bfloat16)
            out_refs[2 * near][kind] = same
            out_refs[2 * near + 1][kind] = other


def unpack_kernel(*refs):
    in_refs = dict(zip(PARTNERS_BACK, refs[:HEADS]))
    out_refs, held_ref, sems = refs[HEADS : HEADS + 3], refs[-2], refs[-1]
    rows = held_ref.shape[1]
    low = low_lanes((rows, LANES))
    low_block = low_lanes((BLOCK, LANES))
    place = lax.rem(lax.axis_index("seq"), HEADS)
    odd_place = lax.rem(place, 2) == 1
    copies = [pltpu.make_async_copy(held_ref.at[i], out_refs[i], sems.at[i]) for i in range(3)]
    for kind in (1, 2, 0):
        for near in range(HEADS // 2):
            pair = lax.bitwise_xor(place // 2, near)
            lanes = pl.ds(pl.multiple_of(pair * LANES, LANES), LANES)
            part = slice(rows, rows + BLOCK) if kind == 0 else slice(0, rows)
            same = in_refs[2 * near][part].astype(jnp.float32)
            other = in_refs[2 * near + 1][part].astype(jnp.float32)
            even = jnp.where(odd_place, other, same)
            odd = jnp.where(odd_place, same, other)
            if kind == 1:
                whole = jnp.where(low, even, swap_halves(odd))
            elif kind == 2:
                whole = jnp.where(low, swap_halves(even), odd)
            else:
                first = jnp.where(low_block, even, swap_halves(odd))
                second = jnp.where(low_block, swap_halves(even), odd)
                whole = jnp.concatenate([first, second], axis=0)
            held_ref[kind, :, lanes] = whole.astype(jnp.bfloat16)
        copies[kind].start()
    for copy in copies:
        copy.wait()


def attend_kernel(alone, scale, ints_ref, *rest):
    if alone:
        in_refs = dict(zip(PARTNERS_IN, rest[:HEADS]))
        out_refs = rest[HEADS : 2 * HEADS]
        sent_ref, gq_ref, acc_ref, table_ref, sem = rest[2 * HEADS :]
    else:
        sent_ref, pool_ref, gq_ref, acc_ref, table_ref, sem = rest
    fetch = pltpu.make_async_copy(ints_ref, table_ref, sem)
    fetch.start()
    if alone:
        place = lax.rem(lax.axis_index("seq"), HEADS)
        for m in range(HEADS):
            sent_ref[lax.bitwise_xor(place, m)] = in_refs[m][...]
    tiles = sent_ref.shape[0]
    blocks = 2 * tiles
    queries = 2 * BLOCK
    low = low_lanes((BLOCK, queries))
    zero = jnp.zeros((BLOCK, LANES), jnp.bfloat16)
    fixed = blocks * RAND
    acc_ref[...] = jnp.zeros_like(acc_ref)
    fetch.wait()

    def pooled(entry):
        if alone:
            return sent_ref[entry // 2, 0, entry % 2]
        return pool_ref[entry]

    def chosen(tile):
        first = 2 * tile
        pairs = [(first, first), (first + 1, first + 1)]
        for slot in range(GLOBAL):
            entry = table_ref[fixed + slot] if alone else blocks + 2 + slot
            pairs.append((entry, entry))
        before, after = first - 1, first + 2
        if alone:
            before, after = max(before, 0), min(after, blocks - 1)
        else:
            before = before if tile > 0 else blocks
            after = after if tile < tiles - 1 else blocks + 1
        pairs.append((before, after))
        for slot in range(RAND):
            picked = []
            for block in (first, first + 1):
                pick = table_ref[block * RAND + slot]
                if alone:
                    behind = block + blocks - (slot + 1) * blocks // 4 - pick
                    picked.append(lax.rem(behind, blocks))
                else:
                    base = blocks + 2 + GLOBAL + slot * (blocks + 1)
                    picked.append(base + block + 1 - pick)
            pairs.append(tuple(picked))
        return pairs

    def multiply(tile):
        pairs = chosen(tile)
        keys = jnp.concatenate(
            [jnp.concatenate([pooled(a), pooled(b)], axis=1) for a, b in pairs], axis=0
        )
        first, second = sent_ref[tile, 1, 0], sent_ref[tile, 1, 1]
        rows = [
            [jnp.where(low, first * scale, zero), zero],
            [zero, jnp.where(low, second * scale, zero)],
            [jnp.where(low, zero, first), zero],
            [zero, jnp.where(low, zero, second)],
        ]
        sides = jnp.concatenate([jnp.concatenate(row, axis=1) for row in rows], axis=0)
        products = lax.dot_general(
            keys, sides, (((1,), (1,)), ((), ())), preferred_element_type=jnp.float32
        )
        return pairs, keys, sides, products

    def weigh(tile, products):
        scores, grad_probs = products[:, :queries], products[:, queries:]
        edge = (2 + GLOBAL) * BLOCK
        if tile == 0 or tile == tiles - 1:
            if tile == 0:
                keep = jnp.logical_not(low)
                if not alone:
                    keep = jnp.logical_or(keep, table_ref[fixed + GLOBAL] > 0)
            else:
                keep = low
                if not alone:
                    last = table_ref[fixed + GLOBAL + 1] - 1
                    keep = jnp.logical_or(keep, table_ref[fixed + GLOBAL] < last)
            masked = jnp.where(keep, scores[edge : edge + BLOCK], MASKED)
            scores = jnp.concatenate([scores[:edge], masked, scores[edge + BLOCK :]], axis=0)
        row_max = folded(jnp.max, scores)
        expo = jnp.exp(scores - row_max)
        row_total = folded(jnp.sum, expo)
        inverse = 1.0 / row_total
        probs_half = (expo * inverse).astype(jnp.bfloat16)
        row_dot = folded(jnp.sum, probs_half.astype(jnp.float32) * grad_probs)
        grad_half = (expo * ((grad_probs - row_dot) * inverse)).astype(jnp.bfloat16)
        return grad_half, probs_half

    def gather(tile, pairs, keys, sides, grad_half, probs_half):
        both = jnp.concatenate([grad_half, probs_half], axis=1)
        key_grads = jnp.dot(both, sides, preferred_element_type=jnp.float32)
        grad_query = lax.dot_general(
            grad_half, keys, (((0,), (0,)), ((), ())), preferred_element_type=jnp.float32
        )
        grad_query = grad_query * scale
        grad_query = jnp.where(
            low, grad_query[:BLOCK, :LANES], swap_halves(grad_query[BLOCK:, LANES:])
        )
        gq_ref[tile] = grad_query.astype(jnp.bfloat16)
        for place, (a, b) in enumerate(pairs):
            part = key_grads[place * BLOCK : (place + 1) * BLOCK]
            if place < 2 + GLOBAL:
                acc_ref[a] += part[:, :LANES] + part[:, LANES:]
            else:
                acc_ref[a] += part[:, :LANES]
                acc_ref[b] += part[:, LANES:]

    ahead, weighed = {}, {}
    for step in range(tiles + 2):
        if step < tiles:
            ahead[step] = multiply(step)
        if 0 <= step - 1 < tiles:
            weighed[step - 1] = weigh(step - 1, ahead[step - 1][-1])
        if step >= 2:
            pairs, keys, sides, _ = ahead.pop(step - 2)
            gather(step - 2, pairs, keys, sides, *weighed.pop(step - 2))
    if alone:
        for m in range(HEADS):
            tile = lax.bitwise_xor(place, m)
            for half in range(2):
                grads = acc_ref[2 * tile + half].astype(jnp.bfloat16)
                out_refs[m][half * BLOCK : (half + 1) * BLOCK] = grads
            out_refs[m][queries:] = gq_ref[tile]


def exchange(parts, partners):
    group = lax.axis_size("seq")
    arrived = list(parts)
    for m in partners[1:]:
        route = [(i, i ^ m) for i in range(group)]
        arrived[m] = lax.ppermute(parts[m], "seq", route)
    return arrived


def moved(block, ranges, distance, ways, wrap=True):
    route = []
    for source in range(ranges):
        target = source + distance
        if wrap:
            target %= ranges
        if 0 <= target < ranges:
            route += [(source * ways + head, target * ways + head) for head in range(ways)]
    return lax.ppermute(block, "seq", route)


def on_device(queries, key_vectors, value_vectors, output_grad, rand_pick, global_ids):
    group = lax.axis_size("seq")
    rows, width = queries.shape
    ways = HEADS
    ranges = group // ways
    assert group % ways == 0 and (ranges == 1 or ranges % 4 == 0)
    alone = ranges == 1
    blocks = ways * rows // BLOCK
    scale = 1.0 / math.sqrt(width // HEADS)
    vmem = pl.BlockSpec(memory_space=pltpu.VMEM)
    half_type = jnp.bfloat16

    anywhere = pl.BlockSpec(memory_space=pl.ANY)
    packed = pl.pallas_call(
        pack_kernel,
        out_shape=[jax.ShapeDtypeStruct((2, rows, LANES), half_type)] * HEADS,
        in_specs=[anywhere] * 4,
        out_specs=[vmem] * HEADS,
        scratch_shapes=[
            pltpu.VMEM((4, rows, width), half_type),
            pltpu.SemaphoreType.DMA((4,)),
        ],
        compiler_params=pltpu.CompilerParams(vmem_limit_bytes=PACK_GRANT),
        name="pack",
    )(queries, key_vectors, value_vectors, output_grad)
    sent = [part.reshape(2, 2, BLOCK, LANES) for part in exchange(packed, PARTNERS_IN)]

    kernel = functools.partial(attend_kernel, alone, scale)
    if alone:
        back = pl.pallas_call(
            kernel,
            out_shape=[jax.ShapeDtypeStruct((rows + BLOCK, LANES), half_type)] * HEADS,
            in_specs=[anywhere] + [vmem] * HEADS,
            out_specs=[vmem] * HEADS,
            scratch_shapes=[
                pltpu.VMEM((ways, 2, 2, BLOCK, LANES), half_type),
                pltpu.VMEM((ways, BLOCK, LANES), half_type),
                pltpu.VMEM((blocks, BLOCK, LANES), jnp.float32),
                pltpu.SMEM((blocks * RAND + GLOBAL,), jnp.int32),
                pltpu.SemaphoreType.DMA,
            ],
            compiler_params=pltpu.CompilerParams(vmem_limit_bytes=24 * 2**20),
            name="attend",
        )(jnp.concatenate([rand_pick.reshape(-1), global_ids]), *[sent[m] for m in PARTNERS_IN])
    else:
        back = spread_out(kernel, sent, rand_pick, global_ids, ways, ranges, blocks)
    received = exchange(back, PARTNERS_BACK)
    return pl.pallas_call(
        unpack_kernel,
        out_shape=[jax.ShapeDtypeStruct((rows, width), half_type)] * 3,
        in_specs=[vmem] * HEADS,
        out_specs=[anywhere] * 3,
        scratch_shapes=[
            pltpu.VMEM((3, rows, width), half_type),
            pltpu.SemaphoreType.DMA((3,)),
        ],
        compiler_params=pltpu.CompilerParams(vmem_limit_bytes=8 * 2**20),
        name="unpack",
    )(*[received[m] for m in PARTNERS_BACK])


def spread_out(kernel, sent, rand_pick, global_ids, ways, ranges, blocks):
    vmem = pl.BlockSpec(memory_space=pltpu.VMEM)
    mine = lax.axis_index("seq") // ways
    order = lax.bitwise_xor(lax.axis_index("seq") % ways, jnp.arange(ways, dtype=jnp.int32))
    sent = jnp.take(jnp.stack(sent), order, axis=0)
    own = sent[:, 0].reshape(blocks, BLOCK, LANES)
    lags = [(slot + 1) * ranges // 4 for slot in range(RAND)]
    heads = [[r * ways + head for r in range(ranges)] for head in range(ways)]
    roots = global_ids // blocks
    offsets = global_ids % blocks
    pool = [own, moved(own[-1:], ranges, 1, ways, False), moved(own[:1], ranges, -1, ways, False)]
    chosen = jnp.where((roots == mine)[:, None, None], jnp.take(own, offsets, axis=0), 0)
    pool.append(lax.psum(chosen.astype(own.dtype), "seq", axis_index_groups=heads))
    for lag in lags:
        pool.append(moved(own[-1:], ranges, lag + 1, ways))
        pool.append(moved(own, ranges, lag, ways))
    pool = jnp.concatenate(pool, axis=0)
    picks = lax.dynamic_slice_in_dim(rand_pick, mine * blocks, blocks, 0)
    where = jnp.stack([mine, jnp.int32(ranges)]).astype(jnp.int32)
    table = jnp.concatenate([picks.reshape(-1), global_ids, where])
    grad_query, totals = pl.pallas_call(
        kernel,
        out_shape=[
            jax.ShapeDtypeStruct((ways, BLOCK, LANES), jnp.bfloat16),
            jax.ShapeDtypeStruct(pool.shape, jnp.float32),
        ],
        in_specs=[pl.BlockSpec(memory_space=pl.ANY), vmem, vmem],
        out_specs=[vmem] * 2,
        scratch_shapes=[
            pltpu.SMEM(table.shape, jnp.int32),
            pltpu.SemaphoreType.DMA,
        ],
        compiler_params=pltpu.CompilerParams(vmem_limit_bytes=24 * 2**20),
        name="attend",
    )(table, sent, pool)
    total = totals[:blocks]
    total = total.at[-1].add(moved(totals[blocks], ranges, -1, ways, False))
    total = total.at[0].add(moved(totals[blocks + 1], ranges, 1, ways, False))
    base = blocks + 2
    summed = lax.psum(totals[base : base + GLOBAL], "seq", axis_index_groups=heads)
    for slot in range(GLOBAL):
        owned = jnp.where(roots[slot] == mine, summed[slot], 0.0)
        total = total.at[offsets[slot]].add(owned)
    base += GLOBAL
    for lag in lags:
        total = total.at[-1].add(moved(totals[base], ranges, -lag - 1, ways))
        total = total + moved(totals[base + 1 : base + 1 + blocks], ranges, -lag, ways)
        base += blocks + 1
    grads = total.astype(jnp.bfloat16).reshape(ways, 2 * BLOCK, LANES)
    back = jnp.take(jnp.concatenate([grads, grad_query], axis=1), order, axis=0)
    return [back[m] for m in range(ways)]


def solution(mesh):
    whole = P(("doc", "seq"), None)
    return jax.shard_map(
        on_device,
        mesh=mesh,
        in_specs=(whole, whole, whole, whole, P("doc", None), P("doc")),
        out_specs=(whole, whole, whole),
        check_vma=False,
    )
```

```python
import functools
import math

import jax
import jax.numpy as jnp
from jax import lax
from jax.experimental import pallas as pl
from jax.experimental.pallas import tpu as pltpu
from jax.sharding import PartitionSpec as P

HEADS = 8
BLOCK = 64
RAND = 3
GLOBAL = 2
HEAD = 64
LANES = 2 * HEAD
PARTNERS_IN = (0, 4, 5, 2, 7, 3, 6, 1)
PARTNERS_BACK = (0, 4, 6, 5, 7, 3, 1, 2)
PACK_GRANT = 427 * 2**17
MASKED = -1e30


def low_lanes(shape):
    return lax.broadcasted_iota(jnp.int32, shape, len(shape) - 1) < HEAD


def swap_halves(block):
    return pltpu.roll(block, HEAD, 1)


def folded(reduce, rows):
    return reduce(reduce(rows.reshape(-1, BLOCK, rows.shape[1]), axis=0), axis=0, keepdims=True)


def pack_kernel(*refs):
    in_refs, out_refs = refs[:4], refs[4 : 4 + HEADS]
    held_ref, in_sems = refs[4 + HEADS :]
    copies = [pltpu.make_async_copy(in_refs[i], held_ref.at[i], in_sems.at[i]) for i in range(4)]
    for copy in copies:
        copy.start()
    rows = held_ref.shape[1]
    low = low_lanes((rows, LANES))
    place = lax.rem(lax.axis_index("seq"), HEADS)
    odd_place = lax.rem(place, 2) == 1
    for copy in copies:
        copy.wait()
    for near in range(HEADS // 2):
        pair = lax.bitwise_xor(place // 2, near)
        lanes = pl.ds(pl.multiple_of(pair * LANES, LANES), LANES)
        q, k, v, g = [held_ref[i, :, lanes].astype(jnp.float32) for i in range(4)]
        for kind, (first, second) in enumerate(((k, v), (q, g))):
            even = jnp.where(low, first, swap_halves(second))
            odd = jnp.where(low, swap_halves(first), second)
            same = jnp.where(odd_place, odd, even).astype(jnp.bfloat16)
            other = jnp.where(odd_place, even, odd).astype(jnp.bfloat16)
            out_refs[2 * near][kind] = same
            out_refs[2 * near + 1][kind] = other


def unpack_kernel(*refs):
    in_refs = dict(zip(PARTNERS_BACK, refs[:HEADS]))
    out_refs, held_ref, sems = refs[HEADS : HEADS + 3], refs[-2], refs[-1]
    rows = held_ref.shape[1]
    low = low_lanes((rows, LANES))
    low_block = low_lanes((BLOCK, LANES))
    place = lax.rem(lax.axis_index("seq"), HEADS)
    odd_place = lax.rem(place, 2) == 1
    copies = [pltpu.make_async_copy(held_ref.at[i], out_refs[i], sems.at[i]) for i in range(3)]
    for kind in (1, 2, 0):
        for near in range(HEADS // 2):
            pair = lax.bitwise_xor(place // 2, near)
            lanes = pl.ds(pl.multiple_of(pair * LANES, LANES), LANES)
            part = slice(rows, rows + BLOCK) if kind == 0 else slice(0, rows)
            same = in_refs[2 * near][part].astype(jnp.float32)
            other = in_refs[2 * near + 1][part].astype(jnp.float32)
            even = jnp.where(odd_place, other, same)
            odd = jnp.where(odd_place, same, other)
            if kind == 1:
                whole = jnp.where(low, even, swap_halves(odd))
            elif kind == 2:
                whole = jnp.where(low, swap_halves(even), odd)
            else:
                first = jnp.where(low_block, even, swap_halves(odd))
                second = jnp.where(low_block, swap_halves(even), odd)
                whole = jnp.concatenate([first, second], axis=0)
            held_ref[kind, :, lanes] = whole.astype(jnp.bfloat16)
        copies[kind].start()
    for copy in copies:
        copy.wait()


def attend_kernel(alone, scale, ints_ref, *rest):
    if alone:
        in_refs = dict(zip(PARTNERS_IN, rest[:HEADS]))
        out_refs = rest[HEADS : 2 * HEADS]
        sent_ref, gq_ref, acc_ref, table_ref, sem = rest[2 * HEADS :]
    else:
        sent_ref, pool_ref, gq_ref, acc_ref, table_ref, sem = rest
    fetch = pltpu.make_async_copy(ints_ref, table_ref, sem)
    fetch.start()
    if alone:
        place = lax.rem(lax.axis_index("seq"), HEADS)
        for m in range(HEADS):
            sent_ref[lax.bitwise_xor(place, m)] = in_refs[m][...]
    tiles = sent_ref.shape[0]
    blocks = 2 * tiles
    queries = 2 * BLOCK
    low = low_lanes((BLOCK, queries))
    zero = jnp.zeros((BLOCK, LANES), jnp.bfloat16)
    fixed = blocks * RAND
    acc_ref[...] = jnp.zeros_like(acc_ref)
    fetch.wait()

    def pooled(entry):
        if alone:
            return sent_ref[entry // 2, 0, entry % 2]
        return pool_ref[entry]

    def chosen(tile):
        first = 2 * tile
        pairs = [(first, first), (first + 1, first + 1)]
        for slot in range(GLOBAL):
            entry = table_ref[fixed + slot] if alone else blocks + 2 + slot
            pairs.append((entry, entry))
        before, after = first - 1, first + 2
        if alone:
            before, after = max(before, 0), min(after, blocks - 1)
        else:
            before = before if tile > 0 else blocks
            after = after if tile < tiles - 1 else blocks + 1
        pairs.append((before, after))
        for slot in range(RAND):
            picked = []
            for block in (first, first + 1):
                pick = table_ref[block * RAND + slot]
                if alone:
                    behind = block + blocks - (slot + 1) * blocks // 4 - pick
                    picked.append(lax.rem(behind, blocks))
                else:
                    base = blocks + 2 + GLOBAL + slot * (blocks + 1)
                    picked.append(base + block + 1 - pick)
            pairs.append(tuple(picked))
        return pairs

    def multiply(tile):
        pairs = chosen(tile)
        keys = jnp.concatenate(
            [jnp.concatenate([pooled(a), pooled(b)], axis=1) for a, b in pairs], axis=0
        )
        first, second = sent_ref[tile, 1, 0], sent_ref[tile, 1, 1]
        rows = [
            [jnp.where(low, first * scale, zero), zero],
            [zero, jnp.where(low, second * scale, zero)],
            [jnp.where(low, zero, first), zero],
            [zero, jnp.where(low, zero, second)],
        ]
        sides = jnp.concatenate([jnp.concatenate(row, axis=1) for row in rows], axis=0)
        products = lax.dot_general(
            keys, sides, (((1,), (1,)), ((), ())), preferred_element_type=jnp.float32
        )
        return pairs, keys, sides, products

    def weigh(tile, products):
        scores, grad_probs = products[:, :queries], products[:, queries:]
        edge = (2 + GLOBAL) * BLOCK
        if tile == 0 or tile == tiles - 1:
            if tile == 0:
                keep = jnp.logical_not(low)
                if not alone:
                    keep = jnp.logical_or(keep, table_ref[fixed + GLOBAL] > 0)
            else:
                keep = low
                if not alone:
                    last = table_ref[fixed + GLOBAL + 1] - 1
                    keep = jnp.logical_or(keep, table_ref[fixed + GLOBAL] < last)
            masked = jnp.where(keep, scores[edge : edge + BLOCK], MASKED)
            scores = jnp.concatenate([scores[:edge], masked, scores[edge + BLOCK :]], axis=0)
        row_max = folded(jnp.max, scores)
        expo = jnp.exp(scores - row_max)
        row_total = folded(jnp.sum, expo)
        inverse = 1.0 / row_total
        probs_half = (expo * inverse).astype(jnp.bfloat16)
        row_dot = folded(jnp.sum, probs_half.astype(jnp.float32) * grad_probs)
        grad_half = (expo * ((grad_probs - row_dot) * inverse)).astype(jnp.bfloat16)
        return grad_half, probs_half

    def gather(tile, pairs, keys, sides, grad_half, probs_half):
        both = jnp.concatenate([grad_half, probs_half], axis=1)
        key_grads = jnp.dot(both, sides, preferred_element_type=jnp.float32)
        grad_query = lax.dot_general(
            grad_half, keys, (((0,), (0,)), ((), ())), preferred_element_type=jnp.float32
        )
        grad_query = grad_query * scale
        grad_query = jnp.where(
            low, grad_query[:BLOCK, :LANES], swap_halves(grad_query[BLOCK:, LANES:])
        )
        gq_ref[tile] = grad_query.astype(jnp.bfloat16)
        for place, (a, b) in enumerate(pairs):
            part = key_grads[place * BLOCK : (place + 1) * BLOCK]
            if place < 2 + GLOBAL:
                acc_ref[a] += part[:, :LANES] + part[:, LANES:]
            else:
                acc_ref[a] += part[:, :LANES]
                acc_ref[b] += part[:, LANES:]

    ahead, weighed = {}, {}
    for step in range(tiles + 2):
        if step < tiles:
            ahead[step] = multiply(step)
        if 0 <= step - 1 < tiles:
            weighed[step - 1] = weigh(step - 1, ahead[step - 1][-1])
        if step >= 2:
            pairs, keys, sides, _ = ahead.pop(step - 2)
            gather(step - 2, pairs, keys, sides, *weighed.pop(step - 2))
    if alone:
        for m in range(HEADS):
            tile = lax.bitwise_xor(place, m)
            for half in range(2):
                grads = acc_ref[2 * tile + half].astype(jnp.bfloat16)
                out_refs[m][half * BLOCK : (half + 1) * BLOCK] = grads
            out_refs[m][queries:] = gq_ref[tile]


def exchange(parts, partners):
    group = lax.axis_size("seq")
    arrived = list(parts)
    for m in partners[1:]:
        route = [(i, i ^ m) for i in range(group)]
        arrived[m] = lax.ppermute(parts[m], "seq", route)
    return arrived


def moved(block, ranges, distance, ways, wrap=True):
    route = []
    for source in range(ranges):
        target = source + distance
        if wrap:
            target %= ranges
        if 0 <= target < ranges:
            route += [(source * ways + head, target * ways + head) for head in range(ways)]
    return lax.ppermute(block, "seq", route)


def on_device(queries, key_vectors, value_vectors, output_grad, rand_pick, global_ids):
    group = lax.axis_size("seq")
    rows, width = queries.shape
    ways = HEADS
    ranges = group // ways
    assert group % ways == 0 and (ranges == 1 or ranges % 4 == 0)
    alone = ranges == 1
    blocks = ways * rows // BLOCK
    scale = 1.0 / math.sqrt(width // HEADS)
    vmem = pl.BlockSpec(memory_space=pltpu.VMEM)
    half_type = jnp.bfloat16

    anywhere = pl.BlockSpec(memory_space=pl.ANY)
    packed = pl.pallas_call(
        pack_kernel,
        out_shape=[jax.ShapeDtypeStruct((2, rows, LANES), half_type)] * HEADS,
        in_specs=[anywhere] * 4,
        out_specs=[vmem] * HEADS,
        scratch_shapes=[
            pltpu.VMEM((4, rows, width), half_type),
            pltpu.SemaphoreType.DMA((4,)),
        ],
        compiler_params=pltpu.CompilerParams(vmem_limit_bytes=PACK_GRANT),
        name="pack",
    )(queries, key_vectors, value_vectors, output_grad)
    sent = [part.reshape(2, 2, BLOCK, LANES) for part in exchange(packed, PARTNERS_IN)]

    kernel = functools.partial(attend_kernel, alone, scale)
    if alone:
        back = pl.pallas_call(
            kernel,
            out_shape=[jax.ShapeDtypeStruct((rows + BLOCK, LANES), half_type)] * HEADS,
            in_specs=[anywhere] + [vmem] * HEADS,
            out_specs=[vmem] * HEADS,
            scratch_shapes=[
                pltpu.VMEM((ways, 2, 2, BLOCK, LANES), half_type),
                pltpu.VMEM((ways, BLOCK, LANES), half_type),
                pltpu.VMEM((blocks, BLOCK, LANES), jnp.float32),
                pltpu.SMEM((blocks * RAND + GLOBAL,), jnp.int32),
                pltpu.SemaphoreType.DMA,
            ],
            compiler_params=pltpu.CompilerParams(vmem_limit_bytes=24 * 2**20),
            name="attend",
        )(jnp.concatenate([rand_pick.reshape(-1), global_ids]), *[sent[m] for m in PARTNERS_IN])
    else:
        back = spread_out(kernel, sent, rand_pick, global_ids, ways, ranges, blocks)
    received = exchange(back, PARTNERS_BACK)
    return pl.pallas_call(
        unpack_kernel,
        out_shape=[jax.ShapeDtypeStruct((rows, width), half_type)] * 3,
        in_specs=[vmem] * HEADS,
        out_specs=[anywhere] * 3,
        scratch_shapes=[
            pltpu.VMEM((3, rows, width), half_type),
            pltpu.SemaphoreType.DMA((3,)),
        ],
        compiler_params=pltpu.CompilerParams(vmem_limit_bytes=8 * 2**20),
        name="unpack",
    )(*[received[m] for m in PARTNERS_BACK])


def spread_out(kernel, sent, rand_pick, global_ids, ways, ranges, blocks):
    vmem = pl.BlockSpec(memory_space=pltpu.VMEM)
    mine = lax.axis_index("seq") // ways
    order = lax.bitwise_xor(lax.axis_index("seq") % ways, jnp.arange(ways, dtype=jnp.int32))
    sent = jnp.take(jnp.stack(sent), order, axis=0)
    own = sent[:, 0].reshape(blocks, BLOCK, LANES)
    lags = [(slot + 1) * ranges // 4 for slot in range(RAND)]
    heads = [[r * ways + head for r in range(ranges)] for head in range(ways)]
    roots = global_ids // blocks
    offsets = global_ids % blocks
    pool = [own, moved(own[-1:], ranges, 1, ways, False), moved(own[:1], ranges, -1, ways, False)]
    chosen = jnp.where((roots == mine)[:, None, None], jnp.take(own, offsets, axis=0), 0)
    pool.append(lax.psum(chosen.astype(own.dtype), "seq", axis_index_groups=heads))
    for lag in lags:
        pool.append(moved(own[-1:], ranges, lag + 1, ways))
        pool.append(moved(own, ranges, lag, ways))
    pool = jnp.concatenate(pool, axis=0)
    picks = lax.dynamic_slice_in_dim(rand_pick, mine * blocks, blocks, 0)
    where = jnp.stack([mine, jnp.int32(ranges)]).astype(jnp.int32)
    table = jnp.concatenate([picks.reshape(-1), global_ids, where])
    grad_query, totals = pl.pallas_call(
        kernel,
        out_shape=[
            jax.ShapeDtypeStruct((ways, BLOCK, LANES), jnp.bfloat16),
            jax.ShapeDtypeStruct(pool.shape, jnp.float32),
        ],
        in_specs=[pl.BlockSpec(memory_space=pl.ANY), vmem, vmem],
        out_specs=[vmem] * 2,
        scratch_shapes=[
            pltpu.SMEM(table.shape, jnp.int32),
            pltpu.SemaphoreType.DMA,
        ],
        compiler_params=pltpu.CompilerParams(vmem_limit_bytes=24 * 2**20),
        name="attend",
    )(table, sent, pool)
    total = totals[:blocks]
    total = total.at[-1].add(moved(totals[blocks], ranges, -1, ways, False))
    total = total.at[0].add(moved(totals[blocks + 1], ranges, 1, ways, False))
    base = blocks + 2
    summed = lax.psum(totals[base : base + GLOBAL], "seq", axis_index_groups=heads)
    for slot in range(GLOBAL):
        owned = jnp.where(roots[slot] == mine, summed[slot], 0.0)
        total = total.at[offsets[slot]].add(owned)
    base += GLOBAL
    for lag in lags:
        total = total.at[-1].add(moved(totals[base], ranges, -lag - 1, ways))
        total = total + moved(totals[base + 1 : base + 1 + blocks], ranges, -lag, ways)
        base += blocks + 1
    grads = total.astype(jnp.bfloat16).reshape(ways, 2 * BLOCK, LANES)
    back = jnp.take(jnp.concatenate([grads, grad_query], axis=1), order, axis=0)
    return [back[m] for m in range(ways)]


def solution(mesh):
    whole = P(("doc", "seq"), None)
    return jax.shard_map(
        on_device,
        mesh=mesh,
        in_specs=(whole, whole, whole, whole, P("doc", None), P("doc")),
        out_specs=(whole, whole, whole),
        check_vma=False,
    )
```

```python
import functools
import math

import jax
import jax.numpy as jnp
from jax import lax
from jax.experimental import pallas as pl
from jax.experimental.pallas import tpu as pltpu
from jax.sharding import PartitionSpec as P

HEADS = 8
BLOCK = 64
RAND = 3
GLOBAL = 2
HEAD = 64
LANES = 2 * HEAD
PARTNERS_IN = (0, 4, 5, 2, 7, 3, 6, 1)
PARTNERS_BACK = (0, 4, 7, 5, 6, 3, 1, 2)
PACK_GRANT = 427 * 2**17
MASKED = -1e30


def low_lanes(shape):
    return lax.broadcasted_iota(jnp.int32, shape, len(shape) - 1) < HEAD


def swap_halves(block):
    return pltpu.roll(block, HEAD, 1)


def folded(reduce, rows):
    return reduce(reduce(rows.reshape(-1, BLOCK, rows.shape[1]), axis=0), axis=0, keepdims=True)


def pack_kernel(*refs):
    in_refs, out_refs = refs[:4], refs[4 : 4 + HEADS]
    held_ref, in_sems = refs[4 + HEADS :]
    copies = [pltpu.make_async_copy(in_refs[i], held_ref.at[i], in_sems.at[i]) for i in range(4)]
    for copy in copies:
        copy.start()
    rows = held_ref.shape[1]
    low = low_lanes((rows, LANES))
    place = lax.rem(lax.axis_index("seq"), HEADS)
    odd_place = lax.rem(place, 2) == 1
    for copy in copies:
        copy.wait()
    for near in range(HEADS // 2):
        pair = lax.bitwise_xor(place // 2, near)
        lanes = pl.ds(pl.multiple_of(pair * LANES, LANES), LANES)
        q, k, v, g = [held_ref[i, :, lanes].astype(jnp.float32) for i in range(4)]
        for kind, (first, second) in enumerate(((k, v), (q, g))):
            even = jnp.where(low, first, swap_halves(second))
            odd = jnp.where(low, swap_halves(first), second)
            same = jnp.where(odd_place, odd, even).astype(jnp.bfloat16)
            other = jnp.where(odd_place, even, odd).astype(jnp.bfloat16)
            out_refs[2 * near][kind] = same
            out_refs[2 * near + 1][kind] = other


def unpack_kernel(*refs):
    in_refs = dict(zip(PARTNERS_BACK, refs[:HEADS]))
    out_refs, held_ref, sems = refs[HEADS : HEADS + 3], refs[-2], refs[-1]
    rows = held_ref.shape[1]
    low = low_lanes((rows, LANES))
    low_block = low_lanes((BLOCK, LANES))
    place = lax.rem(lax.axis_index("seq"), HEADS)
    odd_place = lax.rem(place, 2) == 1
    copies = [pltpu.make_async_copy(held_ref.at[i], out_refs[i], sems.at[i]) for i in range(3)]
    for kind in (1, 2, 0):
        for near in range(HEADS // 2):
            pair = lax.bitwise_xor(place // 2, near)
            lanes = pl.ds(pl.multiple_of(pair * LANES, LANES), LANES)
            part = slice(rows, rows + BLOCK) if kind == 0 else slice(0, rows)
            same = in_refs[2 * near][part].astype(jnp.float32)
            other = in_refs[2 * near + 1][part].astype(jnp.float32)
            even = jnp.where(odd_place, other, same)
            odd = jnp.where(odd_place, same, other)
            if kind == 1:
                whole = jnp.where(low, even, swap_halves(odd))
            elif kind == 2:
                whole = jnp.where(low, swap_halves(even), odd)
            else:
                first = jnp.where(low_block, even, swap_halves(odd))
                second = jnp.where(low_block, swap_halves(even), odd)
                whole = jnp.concatenate([first, second], axis=0)
            held_ref[kind, :, lanes] = whole.astype(jnp.bfloat16)
        copies[kind].start()
    for copy in copies:
        copy.wait()


def attend_kernel(alone, scale, ints_ref, *rest):
    if alone:
        in_refs = dict(zip(PARTNERS_IN, rest[:HEADS]))
        out_refs = rest[HEADS : 2 * HEADS]
        sent_ref, gq_ref, acc_ref, table_ref, sem = rest[2 * HEADS :]
    else:
        sent_ref, pool_ref, gq_ref, acc_ref, table_ref, sem = rest
    fetch = pltpu.make_async_copy(ints_ref, table_ref, sem)
    fetch.start()
    if alone:
        place = lax.rem(lax.axis_index("seq"), HEADS)
        for m in range(HEADS):
            sent_ref[lax.bitwise_xor(place, m)] = in_refs[m][...]
    tiles = sent_ref.shape[0]
    blocks = 2 * tiles
    queries = 2 * BLOCK
    low = low_lanes((BLOCK, queries))
    zero = jnp.zeros((BLOCK, LANES), jnp.bfloat16)
    fixed = blocks * RAND
    acc_ref[...] = jnp.zeros_like(acc_ref)
    fetch.wait()

    def pooled(entry):
        if alone:
            return sent_ref[entry // 2, 0, entry % 2]
        return pool_ref[entry]

    def chosen(tile):
        first = 2 * tile
        pairs = [(first, first), (first + 1, first + 1)]
        for slot in range(GLOBAL):
            entry = table_ref[fixed + slot] if alone else blocks + 2 + slot
            pairs.append((entry, entry))
        before, after = first - 1, first + 2
        if alone:
            before, after = max(before, 0), min(after, blocks - 1)
        else:
            before = before if tile > 0 else blocks
            after = after if tile < tiles - 1 else blocks + 1
        pairs.append((before, after))
        for slot in range(RAND):
            picked = []
            for block in (first, first + 1):
                pick = table_ref[block * RAND + slot]
                if alone:
                    behind = block + blocks - (slot + 1) * blocks // 4 - pick
                    picked.append(lax.rem(behind, blocks))
                else:
                    base = blocks + 2 + GLOBAL + slot * (blocks + 1)
                    picked.append(base + block + 1 - pick)
            pairs.append(tuple(picked))
        return pairs

    def multiply(tile):
        pairs = chosen(tile)
        keys = jnp.concatenate(
            [jnp.concatenate([pooled(a), pooled(b)], axis=1) for a, b in pairs], axis=0
        )
        first, second = sent_ref[tile, 1, 0], sent_ref[tile, 1, 1]
        rows = [
            [jnp.where(low, first * scale, zero), zero],
            [zero, jnp.where(low, second * scale, zero)],
            [jnp.where(low, zero, first), zero],
            [zero, jnp.where(low, zero, second)],
        ]
        sides = jnp.concatenate([jnp.concatenate(row, axis=1) for row in rows], axis=0)
        products = lax.dot_general(
            keys, sides, (((1,), (1,)), ((), ())), preferred_element_type=jnp.float32
        )
        return pairs, keys, sides, products

    def weigh(tile, products):
        scores, grad_probs = products[:, :queries], products[:, queries:]
        edge = (2 + GLOBAL) * BLOCK
        if tile == 0 or tile == tiles - 1:
            if tile == 0:
                keep = jnp.logical_not(low)
                if not alone:
                    keep = jnp.logical_or(keep, table_ref[fixed + GLOBAL] > 0)
            else:
                keep = low
                if not alone:
                    last = table_ref[fixed + GLOBAL + 1] - 1
                    keep = jnp.logical_or(keep, table_ref[fixed + GLOBAL] < last)
            masked = jnp.where(keep, scores[edge : edge + BLOCK], MASKED)
            scores = jnp.concatenate([scores[:edge], masked, scores[edge + BLOCK :]], axis=0)
        row_max = folded(jnp.max, scores)
        expo = jnp.exp(scores - row_max)
        row_total = folded(jnp.sum, expo)
        inverse = 1.0 / row_total
        probs_half = (expo * inverse).astype(jnp.bfloat16)
        row_dot = folded(jnp.sum, probs_half.astype(jnp.float32) * grad_probs)
        grad_half = (expo * ((grad_probs - row_dot) * inverse)).astype(jnp.bfloat16)
        return grad_half, probs_half

    def gather(tile, pairs, keys, sides, grad_half, probs_half):
        both = jnp.concatenate([grad_half, probs_half], axis=1)
        key_grads = jnp.dot(both, sides, preferred_element_type=jnp.float32)
        grad_query = lax.dot_general(
            grad_half, keys, (((0,), (0,)), ((), ())), preferred_element_type=jnp.float32
        )
        grad_query = grad_query * scale
        grad_query = jnp.where(
            low, grad_query[:BLOCK, :LANES], swap_halves(grad_query[BLOCK:, LANES:])
        )
        gq_ref[tile] = grad_query.astype(jnp.bfloat16)
        for place, (a, b) in enumerate(pairs):
            part = key_grads[place * BLOCK : (place + 1) * BLOCK]
            if place < 2 + GLOBAL:
                acc_ref[a] += part[:, :LANES] + part[:, LANES:]
            else:
                acc_ref[a] += part[:, :LANES]
                acc_ref[b] += part[:, LANES:]

    ahead, weighed = {}, {}
    for step in range(tiles + 2):
        if step < tiles:
            ahead[step] = multiply(step)
        if 0 <= step - 1 < tiles:
            weighed[step - 1] = weigh(step - 1, ahead[step - 1][-1])
        if step >= 2:
            pairs, keys, sides, _ = ahead.pop(step - 2)
            gather(step - 2, pairs, keys, sides, *weighed.pop(step - 2))
    if alone:
        for m in range(HEADS):
            tile = lax.bitwise_xor(place, m)
            for half in range(2):
                grads = acc_ref[2 * tile + half].astype(jnp.bfloat16)
                out_refs[m][half * BLOCK : (half + 1) * BLOCK] = grads
            out_refs[m][queries:] = gq_ref[tile]


def exchange(parts, partners):
    group = lax.axis_size("seq")
    arrived = list(parts)
    for m in partners[1:]:
        route = [(i, i ^ m) for i in range(group)]
        arrived[m] = lax.ppermute(parts[m], "seq", route)
    return arrived


def moved(block, ranges, distance, ways, wrap=True):
    route = []
    for source in range(ranges):
        target = source + distance
        if wrap:
            target %= ranges
        if 0 <= target < ranges:
            route += [(source * ways + head, target * ways + head) for head in range(ways)]
    return lax.ppermute(block, "seq", route)


def on_device(queries, key_vectors, value_vectors, output_grad, rand_pick, global_ids):
    group = lax.axis_size("seq")
    rows, width = queries.shape
    ways = HEADS
    ranges = group // ways
    assert group % ways == 0 and (ranges == 1 or ranges % 4 == 0)
    alone = ranges == 1
    blocks = ways * rows // BLOCK
    scale = 1.0 / math.sqrt(width // HEADS)
    vmem = pl.BlockSpec(memory_space=pltpu.VMEM)
    half_type = jnp.bfloat16

    anywhere = pl.BlockSpec(memory_space=pl.ANY)
    packed = pl.pallas_call(
        pack_kernel,
        out_shape=[jax.ShapeDtypeStruct((2, rows, LANES), half_type)] * HEADS,
        in_specs=[anywhere] * 4,
        out_specs=[vmem] * HEADS,
        scratch_shapes=[
            pltpu.VMEM((4, rows, width), half_type),
            pltpu.SemaphoreType.DMA((4,)),
        ],
        compiler_params=pltpu.CompilerParams(vmem_limit_bytes=PACK_GRANT),
        name="pack",
    )(queries, key_vectors, value_vectors, output_grad)
    sent = [part.reshape(2, 2, BLOCK, LANES) for part in exchange(packed, PARTNERS_IN)]

    kernel = functools.partial(attend_kernel, alone, scale)
    if alone:
        back = pl.pallas_call(
            kernel,
            out_shape=[jax.ShapeDtypeStruct((rows + BLOCK, LANES), half_type)] * HEADS,
            in_specs=[anywhere] + [vmem] * HEADS,
            out_specs=[vmem] * HEADS,
            scratch_shapes=[
                pltpu.VMEM((ways, 2, 2, BLOCK, LANES), half_type),
                pltpu.VMEM((ways, BLOCK, LANES), half_type),
                pltpu.VMEM((blocks, BLOCK, LANES), jnp.float32),
                pltpu.SMEM((blocks * RAND + GLOBAL,), jnp.int32),
                pltpu.SemaphoreType.DMA,
            ],
            compiler_params=pltpu.CompilerParams(vmem_limit_bytes=24 * 2**20),
            name="attend",
        )(jnp.concatenate([rand_pick.reshape(-1), global_ids]), *[sent[m] for m in PARTNERS_IN])
    else:
        back = spread_out(kernel, sent, rand_pick, global_ids, ways, ranges, blocks)
    received = exchange(back, PARTNERS_BACK)
    return pl.pallas_call(
        unpack_kernel,
        out_shape=[jax.ShapeDtypeStruct((rows, width), half_type)] * 3,
        in_specs=[vmem] * HEADS,
        out_specs=[anywhere] * 3,
        scratch_shapes=[
            pltpu.VMEM((3, rows, width), half_type),
            pltpu.SemaphoreType.DMA((3,)),
        ],
        compiler_params=pltpu.CompilerParams(vmem_limit_bytes=8 * 2**20),
        name="unpack",
    )(*[received[m] for m in PARTNERS_BACK])


def spread_out(kernel, sent, rand_pick, global_ids, ways, ranges, blocks):
    vmem = pl.BlockSpec(memory_space=pltpu.VMEM)
    mine = lax.axis_index("seq") // ways
    order = lax.bitwise_xor(lax.axis_index("seq") % ways, jnp.arange(ways, dtype=jnp.int32))
    sent = jnp.take(jnp.stack(sent), order, axis=0)
    own = sent[:, 0].reshape(blocks, BLOCK, LANES)
    lags = [(slot + 1) * ranges // 4 for slot in range(RAND)]
    heads = [[r * ways + head for r in range(ranges)] for head in range(ways)]
    roots = global_ids // blocks
    offsets = global_ids % blocks
    pool = [own, moved(own[-1:], ranges, 1, ways, False), moved(own[:1], ranges, -1, ways, False)]
    chosen = jnp.where((roots == mine)[:, None, None], jnp.take(own, offsets, axis=0), 0)
    pool.append(lax.psum(chosen.astype(own.dtype), "seq", axis_index_groups=heads))
    for lag in lags:
        pool.append(moved(own[-1:], ranges, lag + 1, ways))
        pool.append(moved(own, ranges, lag, ways))
    pool = jnp.concatenate(pool, axis=0)
    picks = lax.dynamic_slice_in_dim(rand_pick, mine * blocks, blocks, 0)
    where = jnp.stack([mine, jnp.int32(ranges)]).astype(jnp.int32)
    table = jnp.concatenate([picks.reshape(-1), global_ids, where])
    grad_query, totals = pl.pallas_call(
        kernel,
        out_shape=[
            jax.ShapeDtypeStruct((ways, BLOCK, LANES), jnp.bfloat16),
            jax.ShapeDtypeStruct(pool.shape, jnp.float32),
        ],
        in_specs=[pl.BlockSpec(memory_space=pl.ANY), vmem, vmem],
        out_specs=[vmem] * 2,
        scratch_shapes=[
            pltpu.SMEM(table.shape, jnp.int32),
            pltpu.SemaphoreType.DMA,
        ],
        compiler_params=pltpu.CompilerParams(vmem_limit_bytes=24 * 2**20),
        name="attend",
    )(table, sent, pool)
    total = totals[:blocks]
    total = total.at[-1].add(moved(totals[blocks], ranges, -1, ways, False))
    total = total.at[0].add(moved(totals[blocks + 1], ranges, 1, ways, False))
    base = blocks + 2
    summed = lax.psum(totals[base : base + GLOBAL], "seq", axis_index_groups=heads)
    for slot in range(GLOBAL):
        owned = jnp.where(roots[slot] == mine, summed[slot], 0.0)
        total = total.at[offsets[slot]].add(owned)
    base += GLOBAL
    for lag in lags:
        total = total.at[-1].add(moved(totals[base], ranges, -lag - 1, ways))
        total = total + moved(totals[base + 1 : base + 1 + blocks], ranges, -lag, ways)
        base += blocks + 1
    grads = total.astype(jnp.bfloat16).reshape(ways, 2 * BLOCK, LANES)
    back = jnp.take(jnp.concatenate([grads, grad_query], axis=1), order, axis=0)
    return [back[m] for m in range(ways)]


def solution(mesh):
    whole = P(("doc", "seq"), None)
    return jax.shard_map(
        on_device,
        mesh=mesh,
        in_specs=(whole, whole, whole, whole, P("doc", None), P("doc")),
        out_specs=(whole, whole, whole),
        check_vma=False,
    )
```

```python
import functools
import math

import jax
import jax.numpy as jnp
from jax import lax
from jax.experimental import pallas as pl
from jax.experimental.pallas import tpu as pltpu
from jax.sharding import PartitionSpec as P

HEADS = 8
BLOCK = 64
RAND = 3
GLOBAL = 2
HEAD = 64
LANES = 2 * HEAD
PARTNERS_IN = (0, 4, 7, 3, 5, 2, 6, 1)
PARTNERS_BACK = (0, 4, 7, 5, 6, 3, 1, 2)
PACK_GRANT = 427 * 2**17
MASKED = -1e30


def low_lanes(shape):
    return lax.broadcasted_iota(jnp.int32, shape, len(shape) - 1) < HEAD


def swap_halves(block):
    return pltpu.roll(block, HEAD, 1)


def folded(reduce, rows):
    return reduce(reduce(rows.reshape(-1, BLOCK, rows.shape[1]), axis=0), axis=0, keepdims=True)


def pack_kernel(*refs):
    in_refs, out_refs = refs[:4], refs[4 : 4 + HEADS]
    held_ref, in_sems = refs[4 + HEADS :]
    copies = [pltpu.make_async_copy(in_refs[i], held_ref.at[i], in_sems.at[i]) for i in range(4)]
    for copy in copies:
        copy.start()
    rows = held_ref.shape[1]
    low = low_lanes((rows, LANES))
    place = lax.rem(lax.axis_index("seq"), HEADS)
    odd_place = lax.rem(place, 2) == 1
    for copy in copies:
        copy.wait()
    for near in range(HEADS // 2):
        pair = lax.bitwise_xor(place // 2, near)
        lanes = pl.ds(pl.multiple_of(pair * LANES, LANES), LANES)
        q, k, v, g = [held_ref[i, :, lanes].astype(jnp.float32) for i in range(4)]
        for kind, (first, second) in enumerate(((k, v), (q, g))):
            even = jnp.where(low, first, swap_halves(second))
            odd = jnp.where(low, swap_halves(first), second)
            same = jnp.where(odd_place, odd, even).astype(jnp.bfloat16)
            other = jnp.where(odd_place, even, odd).astype(jnp.bfloat16)
            out_refs[2 * near][kind] = same
            out_refs[2 * near + 1][kind] = other


def unpack_kernel(*refs):
    in_refs = dict(zip(PARTNERS_BACK, refs[:HEADS]))
    out_refs, held_ref, sems = refs[HEADS : HEADS + 3], refs[-2], refs[-1]
    rows = held_ref.shape[1]
    low = low_lanes((rows, LANES))
    low_block = low_lanes((BLOCK, LANES))
    place = lax.rem(lax.axis_index("seq"), HEADS)
    odd_place = lax.rem(place, 2) == 1
    copies = [pltpu.make_async_copy(held_ref.at[i], out_refs[i], sems.at[i]) for i in range(3)]
    for kind in (1, 2, 0):
        for near in range(HEADS // 2):
            pair = lax.bitwise_xor(place // 2, near)
            lanes = pl.ds(pl.multiple_of(pair * LANES, LANES), LANES)
            part = slice(rows, rows + BLOCK) if kind == 0 else slice(0, rows)
            same = in_refs[2 * near][part].astype(jnp.float32)
            other = in_refs[2 * near + 1][part].astype(jnp.float32)
            even = jnp.where(odd_place, other, same)
            odd = jnp.where(odd_place, same, other)
            if kind == 1:
                whole = jnp.where(low, even, swap_halves(odd))
            elif kind == 2:
                whole = jnp.where(low, swap_halves(even), odd)
            else:
                first = jnp.where(low_block, even, swap_halves(odd))
                second = jnp.where(low_block, swap_halves(even), odd)
                whole = jnp.concatenate([first, second], axis=0)
            held_ref[kind, :, lanes] = whole.astype(jnp.bfloat16)
        copies[kind].start()
    for copy in copies:
        copy.wait()


def attend_kernel(alone, scale, ints_ref, *rest):
    if alone:
        in_refs = dict(zip(PARTNERS_IN, rest[:HEADS]))
        out_refs = rest[HEADS : 2 * HEADS]
        sent_ref, gq_ref, acc_ref, table_ref, sem = rest[2 * HEADS :]
    else:
        sent_ref, pool_ref, gq_ref, acc_ref, table_ref, sem = rest
    fetch = pltpu.make_async_copy(ints_ref, table_ref, sem)
    fetch.start()
    if alone:
        place = lax.rem(lax.axis_index("seq"), HEADS)
        for m in range(HEADS):
            sent_ref[lax.bitwise_xor(place, m)] = in_refs[m][...]
    tiles = sent_ref.shape[0]
    blocks = 2 * tiles
    queries = 2 * BLOCK
    low = low_lanes((BLOCK, queries))
    zero = jnp.zeros((BLOCK, LANES), jnp.bfloat16)
    fixed = blocks * RAND
    acc_ref[...] = jnp.zeros_like(acc_ref)
    fetch.wait()

    def pooled(entry):
        if alone:
            return sent_ref[entry // 2, 0, entry % 2]
        return pool_ref[entry]

    def chosen(tile):
        first = 2 * tile
        pairs = [(first, first), (first + 1, first + 1)]
        for slot in range(GLOBAL):
            entry = table_ref[fixed + slot] if alone else blocks + 2 + slot
            pairs.append((entry, entry))
        before, after = first - 1, first + 2
        if alone:
            before, after = max(before, 0), min(after, blocks - 1)
        else:
            before = before if tile > 0 else blocks
            after = after if tile < tiles - 1 else blocks + 1
        pairs.append((before, after))
        for slot in range(RAND):
            picked = []
            for block in (first, first + 1):
                pick = table_ref[block * RAND + slot]
                if alone:
                    behind = block + blocks - (slot + 1) * blocks // 4 - pick
                    picked.append(lax.rem(behind, blocks))
                else:
                    base = blocks + 2 + GLOBAL + slot * (blocks + 1)
                    picked.append(base + block + 1 - pick)
            pairs.append(tuple(picked))
        return pairs

    def multiply(tile):
        pairs = chosen(tile)
        keys = jnp.concatenate(
            [jnp.concatenate([pooled(a), pooled(b)], axis=1) for a, b in pairs], axis=0
        )
        first, second = sent_ref[tile, 1, 0], sent_ref[tile, 1, 1]
        rows = [
            [jnp.where(low, first * scale, zero), zero],
            [zero, jnp.where(low, second * scale, zero)],
            [jnp.where(low, zero, first), zero],
            [zero, jnp.where(low, zero, second)],
        ]
        sides = jnp.concatenate([jnp.concatenate(row, axis=1) for row in rows], axis=0)
        products = lax.dot_general(
            keys, sides, (((1,), (1,)), ((), ())), preferred_element_type=jnp.float32
        )
        return pairs, keys, sides, products

    def weigh(tile, products):
        scores, grad_probs = products[:, :queries], products[:, queries:]
        edge = (2 + GLOBAL) * BLOCK
        if tile == 0 or tile == tiles - 1:
            if tile == 0:
                keep = jnp.logical_not(low)
                if not alone:
                    keep = jnp.logical_or(keep, table_ref[fixed + GLOBAL] > 0)
            else:
                keep = low
                if not alone:
                    last = table_ref[fixed + GLOBAL + 1] - 1
                    keep = jnp.logical_or(keep, table_ref[fixed + GLOBAL] < last)
            masked = jnp.where(keep, scores[edge : edge + BLOCK], MASKED)
            scores = jnp.concatenate([scores[:edge], masked, scores[edge + BLOCK :]], axis=0)
        row_max = folded(jnp.max, scores)
        expo = jnp.exp(scores - row_max)
        row_total = folded(jnp.sum, expo)
        inverse = 1.0 / row_total
        probs_half = (expo * inverse).astype(jnp.bfloat16)
        row_dot = folded(jnp.sum, probs_half.astype(jnp.float32) * grad_probs)
        grad_half = (expo * ((grad_probs - row_dot) * inverse)).astype(jnp.bfloat16)
        return grad_half, probs_half

    def gather(tile, pairs, keys, sides, grad_half, probs_half):
        both = jnp.concatenate([grad_half, probs_half], axis=1)
        key_grads = jnp.dot(both, sides, preferred_element_type=jnp.float32)
        grad_query = lax.dot_general(
            grad_half, keys, (((0,), (0,)), ((), ())), preferred_element_type=jnp.float32
        )
        grad_query = grad_query * scale
        grad_query = jnp.where(
            low, grad_query[:BLOCK, :LANES], swap_halves(grad_query[BLOCK:, LANES:])
        )
        gq_ref[tile] = grad_query.astype(jnp.bfloat16)
        for place, (a, b) in enumerate(pairs):
            part = key_grads[place * BLOCK : (place + 1) * BLOCK]
            if place < 2 + GLOBAL:
                acc_ref[a] += part[:, :LANES] + part[:, LANES:]
            else:
                acc_ref[a] += part[:, :LANES]
                acc_ref[b] += part[:, LANES:]

    ahead, weighed = {}, {}
    for step in range(tiles + 2):
        if step < tiles:
            ahead[step] = multiply(step)
        if 0 <= step - 1 < tiles:
            weighed[step - 1] = weigh(step - 1, ahead[step - 1][-1])
        if step >= 2:
            pairs, keys, sides, _ = ahead.pop(step - 2)
            gather(step - 2, pairs, keys, sides, *weighed.pop(step - 2))
    if alone:
        for m in range(HEADS):
            tile = lax.bitwise_xor(place, m)
            for half in range(2):
                grads = acc_ref[2 * tile + half].astype(jnp.bfloat16)
                out_refs[m][half * BLOCK : (half + 1) * BLOCK] = grads
            out_refs[m][queries:] = gq_ref[tile]


def exchange(parts, partners):
    group = lax.axis_size("seq")
    arrived = list(parts)
    for m in partners[1:]:
        route = [(i, i ^ m) for i in range(group)]
        arrived[m] = lax.ppermute(parts[m], "seq", route)
    return arrived


def moved(block, ranges, distance, ways, wrap=True):
    route = []
    for source in range(ranges):
        target = source + distance
        if wrap:
            target %= ranges
        if 0 <= target < ranges:
            route += [(source * ways + head, target * ways + head) for head in range(ways)]
    return lax.ppermute(block, "seq", route)


def on_device(queries, key_vectors, value_vectors, output_grad, rand_pick, global_ids):
    group = lax.axis_size("seq")
    rows, width = queries.shape
    ways = HEADS
    ranges = group // ways
    assert group % ways == 0 and (ranges == 1 or ranges % 4 == 0)
    alone = ranges == 1
    blocks = ways * rows // BLOCK
    scale = 1.0 / math.sqrt(width // HEADS)
    vmem = pl.BlockSpec(memory_space=pltpu.VMEM)
    half_type = jnp.bfloat16

    anywhere = pl.BlockSpec(memory_space=pl.ANY)
    packed = pl.pallas_call(
        pack_kernel,
        out_shape=[jax.ShapeDtypeStruct((2, rows, LANES), half_type)] * HEADS,
        in_specs=[anywhere] * 4,
        out_specs=[vmem] * HEADS,
        scratch_shapes=[
            pltpu.VMEM((4, rows, width), half_type),
            pltpu.SemaphoreType.DMA((4,)),
        ],
        compiler_params=pltpu.CompilerParams(vmem_limit_bytes=PACK_GRANT),
        name="pack",
    )(queries, key_vectors, value_vectors, output_grad)
    sent = [part.reshape(2, 2, BLOCK, LANES) for part in exchange(packed, PARTNERS_IN)]

    kernel = functools.partial(attend_kernel, alone, scale)
    if alone:
        back = pl.pallas_call(
            kernel,
            out_shape=[jax.ShapeDtypeStruct((rows + BLOCK, LANES), half_type)] * HEADS,
            in_specs=[anywhere] + [vmem] * HEADS,
            out_specs=[vmem] * HEADS,
            scratch_shapes=[
                pltpu.VMEM((ways, 2, 2, BLOCK, LANES), half_type),
                pltpu.VMEM((ways, BLOCK, LANES), half_type),
                pltpu.VMEM((blocks, BLOCK, LANES), jnp.float32),
                pltpu.SMEM((blocks * RAND + GLOBAL,), jnp.int32),
                pltpu.SemaphoreType.DMA,
            ],
            compiler_params=pltpu.CompilerParams(vmem_limit_bytes=24 * 2**20),
            name="attend",
        )(jnp.concatenate([rand_pick.reshape(-1), global_ids]), *[sent[m] for m in PARTNERS_IN])
    else:
        back = spread_out(kernel, sent, rand_pick, global_ids, ways, ranges, blocks)
    received = exchange(back, PARTNERS_BACK)
    return pl.pallas_call(
        unpack_kernel,
        out_shape=[jax.ShapeDtypeStruct((rows, width), half_type)] * 3,
        in_specs=[vmem] * HEADS,
        out_specs=[anywhere] * 3,
        scratch_shapes=[
            pltpu.VMEM((3, rows, width), half_type),
            pltpu.SemaphoreType.DMA((3,)),
        ],
        compiler_params=pltpu.CompilerParams(vmem_limit_bytes=8 * 2**20),
        name="unpack",
    )(*[received[m] for m in PARTNERS_BACK])


def spread_out(kernel, sent, rand_pick, global_ids, ways, ranges, blocks):
    vmem = pl.BlockSpec(memory_space=pltpu.VMEM)
    mine = lax.axis_index("seq") // ways
    order = lax.bitwise_xor(lax.axis_index("seq") % ways, jnp.arange(ways, dtype=jnp.int32))
    sent = jnp.take(jnp.stack(sent), order, axis=0)
    own = sent[:, 0].reshape(blocks, BLOCK, LANES)
    lags = [(slot + 1) * ranges // 4 for slot in range(RAND)]
    heads = [[r * ways + head for r in range(ranges)] for head in range(ways)]
    roots = global_ids // blocks
    offsets = global_ids % blocks
    pool = [own, moved(own[-1:], ranges, 1, ways, False), moved(own[:1], ranges, -1, ways, False)]
    chosen = jnp.where((roots == mine)[:, None, None], jnp.take(own, offsets, axis=0), 0)
    pool.append(lax.psum(chosen.astype(own.dtype), "seq", axis_index_groups=heads))
    for lag in lags:
        pool.append(moved(own[-1:], ranges, lag + 1, ways))
        pool.append(moved(own, ranges, lag, ways))
    pool = jnp.concatenate(pool, axis=0)
    picks = lax.dynamic_slice_in_dim(rand_pick, mine * blocks, blocks, 0)
    where = jnp.stack([mine, jnp.int32(ranges)]).astype(jnp.int32)
    table = jnp.concatenate([picks.reshape(-1), global_ids, where])
    grad_query, totals = pl.pallas_call(
        kernel,
        out_shape=[
            jax.ShapeDtypeStruct((ways, BLOCK, LANES), jnp.bfloat16),
            jax.ShapeDtypeStruct(pool.shape, jnp.float32),
        ],
        in_specs=[pl.BlockSpec(memory_space=pl.ANY), vmem, vmem],
        out_specs=[vmem] * 2,
        scratch_shapes=[
            pltpu.SMEM(table.shape, jnp.int32),
            pltpu.SemaphoreType.DMA,
        ],
        compiler_params=pltpu.CompilerParams(vmem_limit_bytes=24 * 2**20),
        name="attend",
    )(table, sent, pool)
    total = totals[:blocks]
    total = total.at[-1].add(moved(totals[blocks], ranges, -1, ways, False))
    total = total.at[0].add(moved(totals[blocks + 1], ranges, 1, ways, False))
    base = blocks + 2
    summed = lax.psum(totals[base : base + GLOBAL], "seq", axis_index_groups=heads)
    for slot in range(GLOBAL):
        owned = jnp.where(roots[slot] == mine, summed[slot], 0.0)
        total = total.at[offsets[slot]].add(owned)
    base += GLOBAL
    for lag in lags:
        total = total.at[-1].add(moved(totals[base], ranges, -lag - 1, ways))
        total = total + moved(totals[base + 1 : base + 1 + blocks], ranges, -lag, ways)
        base += blocks + 1
    grads = total.astype(jnp.bfloat16).reshape(ways, 2 * BLOCK, LANES)
    back = jnp.take(jnp.concatenate([grads, grad_query], axis=1), order, axis=0)
    return [back[m] for m in range(ways)]


def solution(mesh):
    whole = P(("doc", "seq"), None)
    return jax.shard_map(
        on_device,
        mesh=mesh,
        in_specs=(whole, whole, whole, whole, P("doc", None), P("doc")),
        out_specs=(whole, whole, whole),
        check_vma=False,
    )
```
